32 devices in a mesh: section: 2 (over core), expert: 4 (over z), shard: 4 (over y, x).
Axes of the slice: x: 2, y: 2, z: 4, core: 2. Of those that a mesh axis runs over, the one named last changes fastest.
Arguments:
- inputs: bfloat16 [2, 4, 1024, 1536], P(None, 'expert', 'shard'), may hold values from -6 to 6
- cotangent: bfloat16 [2, 4, 1024, 1536], P(None, 'expert', 'shard'), may hold values from -6 to 6
- segments: int32 [2, 4, 1024], P(None, 'expert', 'shard'), may hold values from 0 to 2, as said below
- routes: int32 [2, 2, 4, 1024, 8], P('section', None, 'expert', 'shard'), may hold values from 0 to 19, all different within a row; in each aligned block of 256 rows (0 to 255, 256 to 511, ..., all dimensions but the last counted through in order) at most 153 rows name the same one
- attn_gain: bfloat16 [2, 1536], P('section', ('expert', 'shard')), may hold values from 0.5 to 1.5
- w_query: bfloat16 [2, 1536, 1536], P('section', ('expert', 'shard')), may hold values from -0.15625 to 0.15625
- w_key: bfloat16 [2, 1536, 512], P('section', ('expert', 'shard')), may hold values from -0.15625 to 0.15625
- w_value: bfloat16 [2, 1536, 512], P('section', ('expert', 'shard')), may hold values from -0.15625 to 0.15625
- w_output: bfloat16 [2, 1536, 1536], P('section', ('expert', 'shard')), may hold values from -0.625 to 0.625
- ffn_gain: bfloat16 [2, 1536], P('section', ('expert', 'shard')), may hold values from 0.5 to 1.5
- router: bfloat16 [2, 1536, 20], P('section', ('expert', 'shard')), may hold values from -0.078125 to 0.078125
- w_gate: bfloat16 [2, 20, 1536, 512], P('section', 'expert', 'shard'), may hold values from -0.15625 to 0.15625
- w_up: bfloat16 [2, 20, 1536, 512], P('section', 'expert', 'shard'), may hold values from -0.15625 to 0.15625
- w_down: bfloat16 [2, 20, 512, 1536], P('section', 'expert', None, 'shard'), may hold values from -1 to 1
Outputs:
- layer_out: bfloat16 [2, 2, 4, 1024, 1536], P('section', None, 'expert', 'shard')
- input_grad: bfloat16 [2, 2, 4, 1024, 1536], P('section', None, 'expert', 'shard')
- grad_attn_gain: float32 [2, 1536], P('section', ('expert', 'shard'))
- grad_query: float32 [2, 1536, 1536], P('section', ('expert', 'shard'))
- grad_key: float32 [2, 1536, 512], P('section', ('expert', 'shard'))
- grad_value: float32 [2, 1536, 512], P('section', ('expert', 'shard'))
- grad_output: float32 [2, 1536, 1536], P('section', ('expert', 'shard'))
- grad_ffn_gain: float32 [2, 1536], P('section', ('expert', 'shard'))
- grad_router: float32 [2, 1536, 20], P('section', ('expert', 'shard'))
- grad_gate: float32 [2, 20, 1536, 512], P('section', 'expert', 'shard')
- grad_up: float32 [2, 20, 1536, 512], P('section', 'expert', 'shard')
- grad_down: float32 [2, 20, 512, 1536], P('section', 'expert', None, 'shard')
The draws below stay inside these ranges and needn't reach their ends.
Inputs may be any that keep to these rules, and one draw needn't show every extreme that they name: `segments`: in each sequence the segment numbers never fall: 0 on the first 1 to 128 positions, 2 on the last 1 to 128, 1 on all between. `routes`: each row names 8 different experts. Within one layer and micro-batch, in the 256 rows of one device no expert is named by more than 153 rows.
All inputs are finite; a program needn't handle non-finite values.
Results may differ from the reference program's by a relative error of at most 0.028.
Values may be sent and summed in bfloat16 or wider, within the bound.
No kernel may reach another device: no remote copies, remote signals or barrier semaphores. Data moves between devices by JAX's collectives and lax.ppermute only.
A program may use at most 448 MiB of HBM per device.

```python
import math
import jax
import jax.numpy as jnp
import numpy as np
from jax import lax

D = 1536
HEADS = 24
KV_HEADS = 8
HEAD = 64
FF = 512
TOPK = 8
SEQ = 1024
MICRO = 2
EXPERTS = 20
SPAN = 256
SEQS = 4
CAP = 153
N_SECTION = 2


def draw_segments(key, part):
    key = jax.random.fold_in(key, 7)
    first_key, second_key = jax.random.split(key)
    first_cut = jax.random.randint(first_key, (MICRO, SEQS, 1), 1, SPAN // 2 + 1)
    second_cut = jax.random.randint(second_key, (MICRO, SEQS, 1), SEQ - SPAN // 2, SEQ)
    places = jnp.arange(SEQ, dtype=jnp.int32)[None, None, :]
    return (places >= first_cut).astype(jnp.int32) + (places >= second_cut).astype(jnp.int32)


def level_of(stream_key, shape, shards, smallest, largest):
    level, own = 1.0, jax.random.fold_in(stream_key, 6)
    for dim, shards_of in shards:
        steps = jnp.exp(jax.random.uniform(jax.random.fold_in(own, dim), (shards_of,), jnp.float32, smallest / len(shards), largest / len(shards)))
        level = level * jnp.repeat(steps, shape[dim] // shards_of).reshape([-1 if axis == dim else 1 for axis in range(len(shape))])
    return level


def shared_out(stream_key, own, number, rows, number_of, top, limit, skew):
    ranking = jax.random.permutation(stream_key, number_of)
    crowded, common = portions_of(number_of, rows * top, limit, skew, True), portions_of(number_of, rows * top, limit, skew, False)
    places = jnp.arange(number_of)

    def named(sizes, offset_by):
        used = int((sizes > 0).sum())
        fixed = max(1, used // 4)
        shifted = fixed + (places - fixed + offset_by * (used - fixed)) % max(1, number_of - fixed)
        return jnp.zeros((number_of,), jnp.int32).at[ranking[jnp.where(places < fixed, places, shifted)]].set(jnp.asarray(sizes, jnp.int32))

    sizes = jnp.where(number % 4 == 0, named(crowded, number // 4), named(common, number - number // 4 - 1))
    mixed = jax.random.permutation(jax.random.fold_in(own, 3), number_of)
    giver, taker = mixed[0:number_of // 2 * 2:2], mixed[1:number_of // 2 * 2:2]
    margin = jnp.minimum(sizes[giver] - 1, limit - sizes[taker]) // 2
    margin = jnp.where((giver == ranking[0]) | (taker == ranking[0]) | (sizes[taker] == 0), 0, jnp.maximum(margin, 0))
    shifted = jax.random.randint(jax.random.fold_in(own, 4), (number_of // 2,), 0, 1 << 20) % (margin + 1)
    sizes = sizes.at[giver].add(-shifted).at[taker].add(shifted)
    labels = jnp.searchsorted(jnp.cumsum(sizes), jnp.arange(rows * top), side="right").astype(jnp.int32)
    grid = labels.reshape(top, rows).T
    grid = grid[jax.random.permutation(jax.random.fold_in(own, 1), rows)]
    offset_by = jax.random.randint(jax.random.fold_in(own, 2), (rows, 1), 0, top)
    return jnp.take_along_axis(grid, (jnp.arange(top)[None, :] + offset_by) % top, axis=1)


def portions_of(count, total, limit, skew, full):
    weights = [(1 << 20) // math.isqrt(grade ** skew) + 1 for grade in range(1, count + 1)]
    largest = limit if full else min(limit, max(-(-total // count), total * weights[0] // sum(weights)))
    least = 1 if total - largest >= count - 1 else 0
    holding, surplus = [largest] + [least] * (count - 1), total - largest - least * (count - 1)
    while surplus > 0:
        candidates = [i for i in range(1, count) if holding[i] < largest] or [i for i in range(1, count) if holding[i] < limit]
        pool, budget = sum([weights[i] for i in candidates]), surplus
        for i in candidates:
            more = min(limit - holding[i], max(1, budget * weights[i] // pool), surplus)
            holding[i] = holding[i] + more
            surplus = surplus - more
    return np.array(holding)


def bell_draw(rng, extent, scale, most, cuts=(), held_as=jnp.bfloat16):
    gain = level_of(rng, extent, cuts, -0.22, 0.18) if cuts else 1.0
    array = jax.random.normal(rng, extent, jnp.float32) * scale * gain
    return jnp.minimum(jnp.maximum(array, -most), most).astype(held_as)


def setup_inputs(seed: int = 0) -> dict:
    seeds = jax.random.split(jax.random.key(seed), 15)
    inputs = bell_draw(seeds[0], (MICRO, SEQS, SEQ, D), 1.0, 6.0, ((1, 4), (2, 4)))
    cotangent = bell_draw(seeds[1], (MICRO, SEQS, SEQ, D), 1.0, 6.0, ((1, 4), (2, 4)))
    segments = draw_segments(jax.random.fold_in(seeds[14], 71), 0)
    routes_keys = jax.random.split(jax.random.fold_in(seeds[3], 1), N_SECTION * MICRO * SEQS * SEQ // SPAN)
    routes_turns = jax.random.permutation(jax.random.fold_in(seeds[3], 3), N_SECTION * MICRO * SEQS * SEQ // SPAN)
    routes = jax.vmap(lambda own, number: shared_out(jax.random.fold_in(seeds[3], 2), own, number, SPAN, EXPERTS, TOPK, CAP, 2))(routes_keys, routes_turns).reshape((N_SECTION, MICRO, SEQS, SEQ, TOPK))
    attn_gain = jnp.clip(1.0 + 0.1 * jax.random.normal(seeds[4], (N_SECTION, D), jnp.float32), 0.5, 1.5).astype(jnp.bfloat16)
    w_query = bell_draw(seeds[5], (N_SECTION, D, HEADS * HEAD), D ** -0.5, 0.15625, ((0, 2), (1, 16)))
    w_key = bell_draw(seeds[6], (N_SECTION, D, KV_HEADS * HEAD), D ** -0.5, 0.15625, ((0, 2), (1, 16)))
    w_value = bell_draw(seeds[7], (N_SECTION, D, KV_HEADS * HEAD), D ** -0.5, 0.15625, ((0, 2), (1, 16)))
    w_output = bell_draw(seeds[8], (N_SECTION, HEADS * HEAD, D), (HEADS * HEAD // 16) ** -0.5, 0.625, ((0, 2), (1, 16)))
    ffn_gain = jnp.clip(1.0 + 0.1 * jax.random.normal(seeds[9], (N_SECTION, D), jnp.float32), 0.5, 1.5).astype(jnp.bfloat16)
    router = bell_draw(seeds[10], (N_SECTION, D, EXPERTS), (4 * D) ** -0.5, 0.078125, ((0, 2), (1, 16)))
    w_gate = bell_draw(seeds[11], (N_SECTION, EXPERTS, D, FF), D ** -0.5, 0.15625, ((0, 2), (1, 4), (2, 4)))
    w_up = bell_draw(seeds[12], (N_SECTION, EXPERTS, D, FF), D ** -0.5, 0.15625, ((0, 2), (1, 4), (2, 4)))
    w_down = bell_draw(seeds[13], (N_SECTION, EXPERTS, FF, D), (FF // 16) ** -0.5, 1.0, ((0, 2), (1, 4), (3, 4)))
    return {"inputs": inputs, "cotangent": cotangent, "segments": segments, "routes": routes, "attn_gain": attn_gain, "w_query": w_query, "w_key": w_key, "w_value": w_value, "w_output": w_output, "ffn_gain": ffn_gain, "router": router, "w_gate": w_gate, "w_up": w_up, "w_down": w_down}


EPSILON = 1e-06
ROPE_BASE = 10000.0
NEGATIVE = -1e+30
HIGHEST = lax.Precision.HIGHEST

@jax.custom_vjp
def low(v):
    return lax.optimization_barrier(v.astype(jnp.bfloat16)).astype(jnp.float32)

@jax.custom_vjp
def low_back(v):
    return v

def low_keep(v):
    return (low(v), None)

def low_pass(kept, grad):
    return (grad,)

def back_keep(v):
    return (v, None)

def back_low(kept, grad):
    return (low(grad),)
low.defvjp(low_keep, low_pass)
low_back.defvjp(back_keep, back_low)

def rotary(positions):
    frequency = 1.0 / ROPE_BASE ** (jnp.arange(0, HEAD, 2, dtype=jnp.float32) / HEAD)
    angles = positions.astype(jnp.float32)[:, None] * frequency[None, :]
    return (jnp.cos(angles)[:, None, :], jnp.sin(angles)[:, None, :])

def rotate(values, cosine_table, sine_table):
    half_size = values.shape[-1] // 2
    first_half = values[..., :half_size]
    second_half = values[..., half_size:]
    return jnp.concatenate([first_half * cosine_table - second_half * sine_table, second_half * cosine_table + first_half * sine_table], axis=-1)

def rms_scale(values, scale_gain):
    return values * lax.rsqrt(lax.optimization_barrier(jnp.mean(values * values, axis=-1, keepdims=True)) + EPSILON) * scale_gain

def attend_one(arrays):
    queries, key_rows, value_rows, segment_ids = arrays
    places = jnp.arange(SEQ, dtype=jnp.int32)
    score_scale = 1.0 / math.sqrt(HEAD)
    scores = low_back(score_scale * jnp.einsum('qngd,knd->qngk', queries, key_rows, precision=HIGHEST))
    allowed = (places[None, :] <= places[:, None]) & (segment_ids[None, :] == segment_ids[:, None])
    attn_probs = low(jax.nn.softmax(jnp.where(allowed[:, None, None, :], scores, NEGATIVE), axis=-1))
    return jnp.einsum('qngk,knd->qngd', attn_probs, value_rows, precision=HIGHEST).reshape(SEQ, HEADS * HEAD)

def block_layer(stream, segment_ids, route_ids, params):
    gain_one, query_w, key_w, value_w, output_w, gain_two, router_w, gate_w, up_w, down_w = params
    seq_count = stream.shape[0]
    group_size = HEADS // KV_HEADS
    cosine_table, sine_table = rotary(jnp.arange(SEQ, dtype=jnp.int32))
    normed = low(rms_scale(stream, gain_one))
    queries = low_back(jnp.einsum('bsd,de->bse', normed, query_w, precision=HIGHEST))
    queries = low(rotate(queries.reshape(seq_count, SEQ, HEADS, HEAD), cosine_table, sine_table))
    key_rows = low_back(jnp.einsum('bsd,de->bse', normed, key_w, precision=HIGHEST))
    key_rows = low(rotate(key_rows.reshape(seq_count, SEQ, KV_HEADS, HEAD), cosine_table, sine_table))
    value_rows = low_back(low(jnp.einsum('bsd,de->bse', normed, value_w, precision=HIGHEST)))
    value_rows = value_rows.reshape(seq_count, SEQ, KV_HEADS, HEAD)
    queries = queries.reshape(seq_count, SEQ, KV_HEADS, group_size, HEAD)
    attended = lax.map(jax.checkpoint(attend_one), (queries, key_rows, value_rows, segment_ids))
    attended = low_back(low(attended))
    middle = stream + low_back(jnp.einsum('bse,ed->bsd', attended, output_w, precision=HIGHEST))
    hidden_in = low(rms_scale(middle, gain_two))
    logits = jnp.einsum('bsd,de->bse', hidden_in, router_w, precision=HIGHEST)
    gate_weights = jax.nn.softmax(jnp.take_along_axis(logits, route_ids, axis=-1), axis=-1)
    blocks = seq_count * SEQ // SPAN
    expert_ids = jnp.arange(EXPERTS, dtype=jnp.int32)

    def expert_block(arrays):
        block_rows, block_ids, block_gates = arrays
        flat_ids = block_ids.reshape(-1)
        one_hot = (flat_ids[:, None] == expert_ids[None, :]).astype(jnp.int32)
        slot_index = lax.optimization_barrier(jnp.sum(jnp.cumsum(one_hot, axis=0) * one_hot, axis=1)) - 1
        targets = flat_ids * CAP + slot_index
        buffer = jnp.zeros((EXPERTS * CAP, D), jnp.float32).at[targets].set(jnp.repeat(block_rows, TOPK, axis=0))
        buffer = low_back(buffer).reshape(EXPERTS, CAP, D)
        gate_raw = low_back(jnp.einsum('ecd,edf->ecf', buffer, gate_w, precision=HIGHEST))
        up_raw = low_back(jnp.einsum('ecd,edf->ecf', buffer, up_w, precision=HIGHEST))
        activated = low(jax.nn.silu(gate_raw) * up_raw)
        expert_out = low_back(low(jnp.einsum('ecf,efd->ecd', activated, down_w, precision=HIGHEST)))
        picked = expert_out.reshape(EXPERTS * CAP, D)[targets].reshape(SPAN, TOPK, D)
        return lax.optimization_barrier(jnp.sum(block_gates[:, :, None] * picked, axis=1))
    expert_mix = lax.map(jax.checkpoint(expert_block), (hidden_in.reshape(blocks, SPAN, D), route_ids.reshape(blocks, SPAN, TOPK), gate_weights.reshape(blocks, SPAN, TOPK)))
    return middle + expert_mix.reshape(seq_count, SEQ, D)

def reference(inputs, cotangent, segments, routes, attn_gain, w_query, w_key, w_value, w_output, ffn_gain, router, w_gate, w_up, w_down):
    seq_count = MICRO * SEQS
    stream = inputs.astype(jnp.float32).reshape(seq_count, SEQ, D)
    segment_ids = segments.reshape(seq_count, SEQ)
    weights = [arrays.astype(jnp.float32) for arrays in (attn_gain, w_query, w_key, w_value, w_output, ffn_gain, router, w_gate, w_up, w_down)]
    params_one = tuple((arrays[0] for arrays in weights))
    params_two = tuple((arrays[1] for arrays in weights))
    routes_one = routes[0].reshape(seq_count, SEQ, TOPK)
    routes_two = routes[1].reshape(seq_count, SEQ, TOPK)

    def first_layer(layer_in, params):
        return block_layer(layer_in, segment_ids, routes_one, params)

    def second_layer(layer_in, params):
        return block_layer(layer_in, segment_ids, routes_two, params)
    middle_out, first_back = jax.vjp(first_layer, stream, params_one)
    middle_out = low(middle_out)
    final_out, second_back = jax.vjp(second_layer, middle_out, params_two)
    grad_mid, grads_two = second_back(cotangent.astype(jnp.float32).reshape(seq_count, SEQ, D))
    grad_mid = low(grad_mid)
    grad_in, grads_one = first_back(grad_mid)
    shape_out = (N_SECTION, MICRO, SEQS, SEQ, D)
    layer_out = jnp.stack([middle_out, final_out]).reshape(shape_out).astype(jnp.bfloat16)
    input_grad = jnp.stack([grad_in, grad_mid]).reshape(shape_out).astype(jnp.bfloat16)
    stacked = [jnp.stack([first_grad, second_grad]) for first_grad, second_grad in zip(grads_one, grads_two)]
    return (layer_out, input_grad, stacked[0], stacked[1], stacked[2], stacked[3], stacked[4], stacked[5], stacked[6], stacked[7], stacked[8], stacked[9])
```

```python
import functools
import math

import jax
import jax.numpy as jnp
from jax import lax
from jax.experimental import pallas as pl
from jax.experimental.pallas import tpu as pltpu
from jax.sharding import PartitionSpec as P

HEADS = 24
KV_HEADS = 8
HEAD = 64

EPSILON = 1e-06
ROPE_BASE = 10000.0
NEGATIVE = -1e30
LANES = 128
MISC = 256
TILE = 256
VMEM_LIMIT = 60 * 1024 * 1024

F32 = jnp.float32
BF16 = jnp.bfloat16


def swap(array):
    return lax.ppermute(array, "section", [(0, 1), (1, 0)])


def shifted(array, axis, by):
    length = lax.axis_size(axis)
    return lax.ppermute(array, axis, [(i, (i + by) % length) for i in range(length)])


def flipped(array, mask):
    return lax.ppermute(array, "shard", [(i, i ^ mask) for i in range(lax.axis_size("shard"))])


def slots_of(array, axis):
    return [array] + [shifted(array, axis, k) for k in range(1, lax.axis_size(axis))]


def after(array, *others):
    return lax.optimization_barrier((array, *others))[0]


def cut(array, start, stop, axis):
    return lax.slice_in_dim(array, start, stop, axis=axis)


def ring_gather(array, axis):
    count = lax.axis_size("shard")
    me = lax.axis_index("shard")
    if count != 4:
        return [
            (slot, lax.rem(me - k + count, count), 0)
            for k, slot in enumerate(slots_of(array, "shard"))
        ]
    length = array.shape[axis]
    half = length // 2
    one = flipped(array, 1)
    two = flipped(array, 2)
    far_low = flipped(cut(one, 0, half, axis), 2)
    far_high = flipped(cut(two, half, length, axis), 1)
    return [
        (array, me, 0),
        (one, me ^ 1, 0),
        (two, me ^ 2, 0),
        (far_low, me ^ 3, 0),
        (far_high, me ^ 3, half),
    ]


def ring_scatter(pieces, axis):
    count = lax.axis_size("shard")
    if count != 4:
        total = pieces[0].astype(F32)
        for k in range(1, count):
            total = total + shifted(pieces[k], "shard", -k).astype(F32)
        return total
    own, one, two, far_low, far_high = pieces
    half = far_low.shape[axis]
    length = own.shape[axis]
    low = flipped(far_low, 2)
    high = flipped(far_high, 1)
    one_high = flipped(cut(one, half, length, axis), 1)
    two_low = flipped(cut(two, 0, half, axis), 2)
    one_low = flipped((cut(one, 0, half, axis).astype(F32) + low.astype(F32)).astype(BF16), 1)
    two_high = flipped(
        (cut(two, half, length, axis).astype(F32) + high.astype(F32)).astype(BF16), 2
    )
    return own.astype(F32) + jnp.concatenate(
        [
            one_low.astype(F32) + two_low.astype(F32),
            one_high.astype(F32) + two_high.astype(F32),
        ],
        axis=axis,
    )


def rotary(positions, head_size):
    frequency = 1.0 / ROPE_BASE ** (jnp.arange(0, head_size, 2, dtype=F32) / head_size)
    angles = positions.astype(F32)[:, None] * frequency[None, :]
    return (jnp.cos(angles)[:, None, :], jnp.sin(angles)[:, None, :])


def rotate(values, cosine_table, sine_table):
    half_size = values.shape[-1] // 2
    first_half = values[..., :half_size]
    second_half = values[..., half_size:]
    return jnp.concatenate(
        [
            first_half * cosine_table - second_half * sine_table,
            second_half * cosine_table + first_half * sine_table,
        ],
        axis=-1,
    )


def norm_back(grad_in, values, scale_rows, scale_gain):
    shaped = grad_in * scale_gain
    grad_values = scale_rows * shaped - values * scale_rows**3 * jnp.mean(
        shaped * values, axis=-1, keepdims=True
    )
    return (grad_values, jnp.sum(grad_in * values * scale_rows, axis=0))


def dot_nt(left, right):
    return lax.dot_general(left, right, (((1,), (1,)), ((), ())), preferred_element_type=F32)


def dot_nn(left, right):
    return jnp.dot(left, right, preferred_element_type=F32)


def dot_tn(left, right):
    return lax.dot_general(left, right, (((0,), (0,)), ((), ())), preferred_element_type=F32)


def fill_weights(off_ref, piece_refs, count, gate_up, down):
    for index in range(2 * count):
        half, place = divmod(index, count)
        ref = piece_refs[index]
        rows = ref.shape[1]
        width = ref.shape[2] // 3
        span = pl.ds(pl.multiple_of(off_ref[place], 16), rows)
        gate_up[span, 2 * half * width : 2 * (half + 1) * width] = ref[0, :, : 2 * width]
        down[span, half * width : (half + 1) * width] = ref[0, :, 2 * width :]


def column_of(table, index):
    lane = lax.broadcasted_iota(jnp.int32, table.shape, 1)
    return jnp.sum(jnp.where(lane == index, table, 0.0), axis=1, keepdims=True)


def split_gate_up(raw, width):
    gate = jnp.concatenate([raw[:, :width], raw[:, 2 * width : 3 * width]], axis=1)
    up = jnp.concatenate([raw[:, width : 2 * width], raw[:, 3 * width :]], axis=1)
    return gate, up


def join_gate_up(gate, up, width):
    return jnp.concatenate(
        [gate[:, :width], up[:, :width], gate[:, width:], up[:, width:]], axis=1
    )


def moe_forward(rows, gates, mine, other, offsets):
    total, model = rows.shape
    experts = mine[0].shape[0]
    width = mine[0].shape[2] // 3
    count = len(mine)
    tile = min(TILE, total)

    def body(off_ref, rows_ref, gates_ref, *rest):
        pieces = rest[: 2 * count]
        out_ref, raw_ref, gate_up, down, sums = rest[2 * count :]
        expert = pl.program_id(0)
        fill_weights(off_ref, pieces, count, gate_up, down)

        def step(index, carry):
            span = pl.ds(pl.multiple_of(index * tile, tile), tile)
            raw = dot_nn(rows_ref[span, :], gate_up[...])
            raw_ref[0, span, :] = raw.astype(BF16)
            gate, up = split_gate_up(raw, width)
            weight = column_of(gates_ref[span, :], expert)
            act = (gate * jax.nn.sigmoid(gate) * up * weight).astype(BF16)
            part = dot_nt(act, down[...])

            @pl.when(expert == 0)
            def _():
                sums[span, :] = part

            @pl.when(expert > 0)
            def _():
                sums[span, :] += part

            @pl.when(expert == experts - 1)
            def _():
                out_ref[span, :] = sums[span, :].astype(BF16)

            return carry

        lax.fori_loop(0, total // tile, step, 0)

    whole = lambda e, *_: (0, 0)
    per_expert = lambda e, *_: (e, 0, 0)
    once = pl.Buffered(1)
    return pl.pallas_call(
        body,
        grid_spec=pltpu.PrefetchScalarGridSpec(
            num_scalar_prefetch=1,
            grid=(experts,),
            in_specs=[
                pl.BlockSpec((total, model), whole, pipeline_mode=once),
                pl.BlockSpec((total, LANES), whole, pipeline_mode=once),
            ]
            + [pl.BlockSpec((1, *piece.shape[1:]), per_expert) for piece in mine + other],
            out_specs=[
                pl.BlockSpec((total, model), whole),
                pl.BlockSpec((1, total, 4 * width), per_expert),
            ],
            scratch_shapes=[
                pltpu.VMEM((model, 4 * width), BF16),
                pltpu.VMEM((model, 2 * width), BF16),
                pltpu.VMEM((total, model), F32),
            ],
        ),
        out_shape=[
            jax.ShapeDtypeStruct((total, model), BF16),
            jax.ShapeDtypeStruct((experts, total, 4 * width), BF16),
        ],
        compiler_params=pltpu.CompilerParams(vmem_limit_bytes=VMEM_LIMIT),
        cost_estimate=pl.CostEstimate(
            flops=2 * experts * total * model * 6 * width,
            bytes_accessed=experts * model * 12 * width,
            transcendentals=0,
        ),
        name="moe_forward",
    )(offsets, rows, gates, *mine, *other)


def moe_backward_rows(grads, gates, raws, mine, other, offsets):
    total, model = grads.shape
    experts = mine[0].shape[0]
    width = mine[0].shape[2] // 3
    count = len(mine)
    tile = min(TILE, total)

    def body(off_ref, grads_ref, gates_ref, raw_ref, *rest):
        pieces = rest[: 2 * count]
        out_ref, scores_ref, d_raw_ref, act_ref, gate_up, down, sums = rest[2 * count :]
        expert = pl.program_id(0)
        fill_weights(off_ref, pieces, count, gate_up, down)

        def step(index, carry):
            span = pl.ds(pl.multiple_of(index * tile, tile), tile)
            weight = column_of(gates_ref[span, :], expert)
            gate, up = split_gate_up(raw_ref[0, span, :].astype(F32), width)
            back = dot_nn(grads_ref[span, :], down[...])
            sigmoid = jax.nn.sigmoid(gate)
            swish = gate * sigmoid
            act = swish * up
            score = jnp.sum(back * act, axis=1, keepdims=True)
            act_ref[0, span, :] = (act * weight).astype(BF16)
            d_act = back * weight
            d_gate = d_act * up * sigmoid * (1.0 + gate * (1.0 - sigmoid))
            d_raw = join_gate_up(d_gate, d_act * swish, width).astype(BF16)
            d_raw_ref[0, span, :] = d_raw
            part = dot_nt(d_raw, gate_up[...])
            lane = lax.broadcasted_iota(jnp.int32, (tile, LANES), 1)

            @pl.when(expert == 0)
            def _():
                sums[span, :] = part
                scores_ref[span, :] = jnp.where(lane == 0, score, 0.0)

            @pl.when(expert > 0)
            def _():
                sums[span, :] += part
                scores_ref[span, :] = jnp.where(lane == expert, score, scores_ref[span, :])

            @pl.when(expert == experts - 1)
            def _():
                out_ref[span, :] = sums[span, :].astype(BF16)

            return carry

        lax.fori_loop(0, total // tile, step, 0)

    whole = lambda e, *_: (0, 0)
    per_expert = lambda e, *_: (e, 0, 0)
    once = pl.Buffered(1)
    return pl.pallas_call(
        body,
        grid_spec=pltpu.PrefetchScalarGridSpec(
            num_scalar_prefetch=1,
            grid=(experts,),
            in_specs=[
                pl.BlockSpec((total, model), whole, pipeline_mode=once),
                pl.BlockSpec((total, LANES), whole, pipeline_mode=once),
                pl.BlockSpec((1, total, 4 * width), per_expert),
            ]
            + [pl.BlockSpec((1, *piece.shape[1:]), per_expert) for piece in mine + other],
            out_specs=[
                pl.BlockSpec((total, model), whole),
                pl.BlockSpec((total, LANES), whole),
                pl.BlockSpec((1, total, 4 * width), per_expert),
                pl.BlockSpec((1, total, 2 * width), per_expert),
            ],
            scratch_shapes=[
                pltpu.VMEM((model, 4 * width), BF16),
                pltpu.VMEM((model, 2 * width), BF16),
                pltpu.VMEM((total, model), F32),
            ],
        ),
        out_shape=[
            jax.ShapeDtypeStruct((total, model), BF16),
            jax.ShapeDtypeStruct((total, LANES), F32),
            jax.ShapeDtypeStruct((experts, total, 4 * width), BF16),
            jax.ShapeDtypeStruct((experts, total, 2 * width), BF16),
        ],
        compiler_params=pltpu.CompilerParams(vmem_limit_bytes=VMEM_LIMIT),
        cost_estimate=pl.CostEstimate(
            flops=2 * experts * total * model * 6 * width,
            bytes_accessed=experts * model * 12 * width + experts * total * 20 * width,
            transcendentals=0,
        ),
        name="moe_backward_rows",
    )(offsets, grads, gates, raws, *mine, *other)


def moe_backward_weights(rows, grads, d_raws, acts, pieces, offsets):
    total, model = rows.shape
    experts = pieces[0].shape[0]
    width = pieces[0].shape[2] // 3
    count = len(pieces)

    def body(off_ref, rows_ref, grads_ref, d_raw_ref, act_ref, *rest):
        outs = rest[: 2 * count]
        rows_t, grads_t = rest[2 * count :]

        @pl.when(pl.program_id(0) == 0)
        def _():
            for start in range(0, model, TILE):
                rows_t[start : start + TILE, :] = rows_ref[:, start : start + TILE].T
                grads_t[start : start + TILE, :] = grads_ref[:, start : start + TILE].T

        for place in range(count):
            depth = pieces[place].shape[1]
            span = pl.ds(pl.multiple_of(off_ref[place], 16), depth)
            gate_up = dot_nn(rows_t[span, :], d_raw_ref[0]).astype(BF16)
            down = dot_nn(grads_t[span, :], act_ref[0]).astype(BF16)
            for half in range(2):
                ref = outs[half * count + place]
                ref[0, :, : 2 * width] = gate_up[:, 2 * half * width : 2 * (half + 1) * width]
                ref[0, :, 2 * width :] = down[:, half * width : (half + 1) * width]

    whole = lambda e, *_: (0, 0)
    per_expert = lambda e, *_: (e, 0, 0)
    once = pl.Buffered(1)
    return pl.pallas_call(
        body,
        grid_spec=pltpu.PrefetchScalarGridSpec(
            num_scalar_prefetch=1,
            grid=(experts,),
            in_specs=[
                pl.BlockSpec((total, model), whole, pipeline_mode=once),
                pl.BlockSpec((total, model), whole, pipeline_mode=once),
                pl.BlockSpec((1, total, 4 * width), per_expert),
                pl.BlockSpec((1, total, 2 * width), per_expert),
            ],
            out_specs=[
                pl.BlockSpec((1, *piece.shape[1:]), per_expert) for piece in pieces + pieces
            ],
            scratch_shapes=[
                pltpu.VMEM((model, total), BF16),
                pltpu.VMEM((model, total), BF16),
            ],
        ),
        out_shape=[jax.ShapeDtypeStruct(piece.shape, BF16) for piece in pieces + pieces],
        compiler_params=pltpu.CompilerParams(vmem_limit_bytes=VMEM_LIMIT),
        cost_estimate=pl.CostEstimate(
            flops=2 * experts * total * model * 6 * width,
            bytes_accessed=experts * (model * 12 + total * 12) * width,
            transcendentals=0,
        ),
        name="moe_backward_weights",
    )(offsets, rows, grads, d_raws, acts)


def on_device(
    inputs,
    cotangent,
    segments,
    routes,
    attn_gain,
    w_query,
    w_key,
    w_value,
    w_output,
    ffn_gain,
    router,
    w_gate,
    w_up,
    w_down,
):
    core = lax.axis_index("section")
    shard = lax.axis_index("shard")
    plane = lax.axis_index("expert")
    shards = lax.axis_size("shard")
    planes = lax.axis_size("expert")
    span_rows, model = inputs.shape[2:]
    seq_rows = span_rows * shards
    gathered_rows = span_rows * planes
    local_experts = w_gate.shape[1]
    all_experts = local_experts * planes
    hidden = w_gate.shape[3]
    half_hidden = hidden // 2
    part_rows = w_query.shape[1]
    query_width = HEADS * HEAD
    kv_width = KV_HEADS * HEAD
    group_size = HEADS // KV_HEADS
    score_scale = 1.0 / math.sqrt(HEAD)
    first = core == 0

    def mine_of(array):
        return lax.dynamic_index_in_dim(array, core, 0, keepdims=False)

    def by_layer(own, received):
        return [jnp.where(first, own, received), jnp.where(first, received, own)]

    def halved(own_halves):
        kept = jnp.where(first, own_halves[0], own_halves[1])
        sent = jnp.where(first, own_halves[1], own_halves[0])
        return by_layer(kept, swap(sent))

    misc = jnp.concatenate(
        [
            attn_gain[0][:, None],
            ffn_gain[0][:, None],
            router[0],
            jnp.zeros((part_rows, MISC - 2 - all_experts), BF16),
        ],
        axis=1,
    )
    qkv_pack = jnp.concatenate([w_query[0], w_key[0], w_value[0], misc], axis=1)
    qkv_half = qkv_pack.shape[1] // 2
    output_half = model // 2
    qkv_mine = halved([qkv_pack[:, :qkv_half], qkv_pack[:, qkv_half:]])
    output_mine = halved([w_output[0][:, :output_half], w_output[0][:, output_half:]])
    down_turned = jnp.swapaxes(w_down[0], 1, 2)

    def expert_half(start):
        stop = start + half_hidden
        return jnp.concatenate(
            [w_gate[0][:, :, start:stop], w_up[0][:, :, start:stop], down_turned[:, :, start:stop]],
            axis=2,
        )

    expert_mine = halved([expert_half(0), expert_half(half_hidden)])

    def dense_weights(array):
        width = array.shape[1]
        lined = jnp.zeros((planes, part_rows, width), BF16)
        for k, slot in enumerate(slots_of(array, "expert")):
            place = lax.rem(plane - k + planes, planes)
            lined = lax.dynamic_update_slice(lined, slot[None], (place, 0, 0))
        pieces = ring_gather(lined, 0)
        others = [swap(piece) for piece, _, _ in pieces]
        result = jnp.zeros((planes, shards, part_rows, 2 * width), BF16)
        for (piece, owner, start), other in zip(pieces, others):
            result = lax.dynamic_update_slice(
                result, piece[:, None], (start, owner, 0, core * width)
            )
            result = lax.dynamic_update_slice(
                result, other[:, None], (start, owner, 0, (1 - core) * width)
            )
        return result.reshape(model, 2 * width)

    def expert_weights(array):
        pieces = ring_gather(array, 1)
        mine = [piece for piece, _, _ in pieces]
        depth = array.shape[1]
        offsets = jnp.stack([owner * depth + start for _, owner, start in pieces])
        return (mine, [swap(piece) for piece in mine], offsets.astype(jnp.int32))

    qkv_full = [None, None]
    output_full = [None, None]
    experts_full = [None, None]
    qkv_full[0] = dense_weights(qkv_mine[0])
    output_full[0] = dense_weights(after(output_mine[0], qkv_full[0]))
    experts_full[0] = expert_weights(after(expert_mine[0], qkv_full[0]))
    qkv_full[1] = dense_weights(after(qkv_mine[1], experts_full[0][0][-1], experts_full[0][0][-2]))
    output_full[1] = dense_weights(
        after(output_mine[1], experts_full[0][0][-1], experts_full[0][0][-2])
    )
    experts_full[1] = expert_weights(after(expert_mine[1], qkv_full[1], output_full[1]))

    segment_local = mine_of(segments)[0]
    positions = shard * span_rows + jnp.arange(span_rows, dtype=jnp.int32)
    cosine_table, sine_table = rotary(positions, HEAD)
    all_places = jnp.concatenate(
        [
            lax.rem(shard - k + shards, shards) * span_rows
            + jnp.arange(span_rows, dtype=jnp.int32)
            for k in range(shards)
        ]
    )
    segment_all = jnp.concatenate(
        [slot[0] for slot in slots_of(segment_local[None], "shard")]
    )
    allowed = (all_places[None, :] <= positions[:, None]) & (
        segment_all[None, :] == segment_local[:, None]
    )
    own_routes = routes[0, :, 0]
    route_rows = by_layer(
        lax.dynamic_index_in_dim(own_routes, core, 0, keepdims=False),
        swap(lax.dynamic_index_in_dim(own_routes, 1 - core, 0, keepdims=False)),
    )
    expert_ids = jnp.arange(all_experts, dtype=jnp.int32)
    chosen = jnp.stack(
        [
            jnp.any(rows[:, :, None] == expert_ids[None, None, :], axis=1).astype(BF16)
            for rows in route_rows
        ]
    )
    chosen_all = jnp.concatenate(slots_of(jnp.swapaxes(chosen, 1, 2), "expert"), axis=2)
    chosen_all = jnp.swapaxes(chosen_all, 1, 2) > 0.5

    def score_block(query_rot, key_all):
        grouped = query_rot.reshape(span_rows, KV_HEADS, group_size, HEAD)
        keyed = key_all.reshape(seq_rows, KV_HEADS, HEAD)
        scores = (
            jnp.einsum("cngd,knd->cngk", grouped, keyed, preferred_element_type=F32) * score_scale
        )
        return jnp.where(allowed[:, None, None, :], scores, NEGATIVE)

    def forward(layer, stream):
        packed = qkv_full[layer]
        side = packed[:, query_width + 2 * kv_width :]
        gain_one = side[:, 0].astype(F32)
        gain_two = side[:, 1].astype(F32)
        router_full = side[:, 2 : 2 + all_experts]
        scale_one = lax.rsqrt(jnp.mean(stream * stream, axis=-1, keepdims=True) + EPSILON)
        normed = (stream * scale_one * gain_one).astype(BF16)
        raw = dot_nn(normed, packed[:, : query_width + 2 * kv_width])
        query_rot = (
            rotate(raw[:, :query_width].reshape(span_rows, HEADS, HEAD), cosine_table, sine_table)
            .astype(BF16)
            .reshape(span_rows, query_width)
        )
        key_rot = (
            rotate(
                raw[:, query_width : query_width + kv_width].reshape(span_rows, KV_HEADS, HEAD),
                cosine_table,
                sine_table,
            )
            .astype(BF16)
            .reshape(span_rows, kv_width)
        )
        value_low = raw[:, query_width + kv_width :].astype(BF16)
        pair_all = jnp.concatenate(
            slots_of(jnp.concatenate([key_rot, value_low], axis=1), "shard"), axis=0
        )
        key_all = pair_all[:, :kv_width]
        value_all = pair_all[:, kv_width:]
        scores = score_block(query_rot, key_all)
        row_max = jnp.max(scores, axis=-1, keepdims=True)
        exponent = jnp.exp(scores - row_max)
        row_sum = jnp.sum(exponent, axis=-1, keepdims=True)
        attn_probs = (exponent / row_sum).astype(BF16)
        weighted = jnp.einsum(
            "cngk,knd->cngd",
            attn_probs,
            value_all.reshape(seq_rows, KV_HEADS, HEAD),
            preferred_element_type=F32,
        )
        attended = weighted.reshape(span_rows, query_width).astype(BF16)
        middle = stream + dot_nn(attended, output_full[layer])
        scale_two = lax.rsqrt(jnp.mean(middle * middle, axis=-1, keepdims=True) + EPSILON)
        hidden_in = (middle * scale_two * gain_two).astype(BF16)
        rows = jnp.concatenate(slots_of(hidden_in, "expert"), axis=0)
        logits = jnp.where(chosen_all[layer], dot_nn(rows, router_full), NEGATIVE)
        gates = jax.nn.softmax(logits, axis=-1)
        gates = jnp.where(chosen_all[layer], gates, 0.0)
        own_gates = lax.dynamic_slice_in_dim(gates, plane * local_experts, local_experts, axis=1)
        own_gates = jnp.pad(own_gates, ((0, 0), (0, LANES - local_experts)))
        mine, other, offsets = experts_full[layer]
        partial, raws = moe_forward(rows, own_gates, mine, other, offsets)
        combined = partial[:span_rows].astype(F32)
        for k in range(1, planes):
            back = shifted(partial[k * span_rows : (k + 1) * span_rows], "expert", -k)
            combined = combined + back.astype(F32)
        kept = dict(
            stream=stream,
            scale_one=scale_one,
            normed=normed,
            query_rot=query_rot,
            key_all=key_all,
            value_all=value_all,
            row_max=row_max,
            row_sum=row_sum,
            attended=attended,
            middle=middle,
            scale_two=scale_two,
            hidden_in=hidden_in,
            rows=rows,
            gates=gates[:span_rows],
            own_gates=own_gates,
            raws=raws,
            combined=combined,
            gain_one=gain_one,
            gain_two=gain_two,
            router_full=router_full,
        )
        return ((middle + combined).astype(BF16), kept)

    def backward(layer, kept, grad_rows):
        grad_low = grad_rows[:span_rows]
        grad_out = grad_low.astype(F32)
        mine, other, offsets = experts_full[layer]
        d_rows, scores, d_raws, acts = moe_backward_rows(
            grad_rows, kept["own_gates"], kept["raws"], mine, other, offsets
        )
        scores_turned = scores.T[: max(8, local_experts)]
        d_hidden = d_rows[:span_rows].astype(F32)
        d_gates = jnp.zeros((all_experts, span_rows), F32)
        d_gates = lax.dynamic_update_slice(
            d_gates, scores_turned[:local_experts, :span_rows], (plane * local_experts, 0)
        )
        for k in range(1, planes):
            span = slice(k * span_rows, (k + 1) * span_rows)
            d_hidden = d_hidden + shifted(d_rows[span], "expert", -k).astype(F32)
            back = shifted(scores_turned[:, span], "expert", -k)
            place = lax.rem(plane + k, planes) * local_experts
            d_gates = lax.dynamic_update_slice(d_gates, back[:local_experts], (place, 0))
        weight_pieces = moe_backward_weights(kept["rows"], grad_rows, d_raws, acts, mine, offsets)
        gates = kept["gates"]
        share = jnp.sum(grad_out * kept["combined"], axis=-1, keepdims=True)
        d_logits = gates * (d_gates.T - share)
        d_logits_high = d_logits.astype(BF16)
        d_logits_low = (d_logits - d_logits_high.astype(F32)).astype(BF16)
        d_hidden = (
            d_hidden
            + dot_nt(d_logits_high, kept["router_full"])
            + dot_nt(d_logits_low, kept["router_full"])
        )
        grad_router = dot_tn(kept["hidden_in"], d_logits_high) + dot_tn(
            kept["hidden_in"], d_logits_low
        )
        d_middle, grad_gain_two = norm_back(
            d_hidden, kept["middle"], kept["scale_two"], kept["gain_two"]
        )
        d_middle = grad_out + d_middle
        d_branch = d_middle.astype(BF16)
        d_attended = dot_nt(d_branch, output_full[layer]).astype(BF16)
        grad_output = dot_tn(kept["attended"], d_branch)
        probs_wide = (
            jnp.exp(score_block(kept["query_rot"], kept["key_all"]) - kept["row_max"])
            / kept["row_sum"]
        )
        attn_probs = probs_wide.astype(BF16)
        d_weighted = d_attended.reshape(span_rows, KV_HEADS, group_size, HEAD)
        value_heads = kept["value_all"].reshape(seq_rows, KV_HEADS, HEAD)
        key_heads = kept["key_all"].reshape(seq_rows, KV_HEADS, HEAD)
        query_heads = kept["query_rot"].reshape(span_rows, KV_HEADS, group_size, HEAD)
        d_values = jnp.einsum(
            "cngk,cngd->knd", attn_probs, d_weighted, preferred_element_type=F32
        )
        d_probs = jnp.einsum(
            "cngd,knd->cngk", d_weighted, value_heads, preferred_element_type=F32
        )
        d_scores = (
            probs_wide * (d_probs - jnp.sum(probs_wide * d_probs, axis=-1, keepdims=True))
        ).astype(BF16)
        d_queries = (
            jnp.einsum("cngk,knd->cngd", d_scores, key_heads, preferred_element_type=F32)
            * score_scale
        )
        d_keys = (
            jnp.einsum("cngk,cngd->knd", d_scores, query_heads, preferred_element_type=F32)
            * score_scale
        )
        d_pairs = jnp.concatenate(
            [d_keys.reshape(seq_rows, kv_width), d_values.reshape(seq_rows, kv_width)], axis=1
        ).astype(BF16)
        d_pair = d_pairs[:span_rows].astype(F32)
        for k in range(1, shards):
            back = shifted(d_pairs[k * span_rows : (k + 1) * span_rows], "shard", -k)
            d_pair = d_pair + back.astype(F32)
        d_query_raw = (
            rotate(d_queries.reshape(span_rows, HEADS, HEAD), cosine_table, -sine_table)
            .astype(BF16)
            .reshape(span_rows, query_width)
        )
        d_key_raw = (
            rotate(
                d_pair[:, :kv_width].reshape(span_rows, KV_HEADS, HEAD), cosine_table, -sine_table
            )
            .astype(BF16)
            .reshape(span_rows, kv_width)
        )
        d_value_raw = d_pair[:, kv_width:].astype(BF16)
        d_packed = jnp.concatenate([d_query_raw, d_key_raw, d_value_raw], axis=1)
        packed = qkv_full[layer][:, : query_width + 2 * kv_width]
        d_normed = dot_nt(d_packed, packed)
        d_stream, grad_gain_one = norm_back(
            d_normed, kept["stream"], kept["scale_one"], kept["gain_one"]
        )
        d_stream = (d_middle + d_stream).astype(BF16)
        grad_packed = dot_tn(kept["normed"], d_packed).astype(BF16)
        grad_side = jnp.concatenate(
            [
                grad_gain_one[:, None],
                grad_gain_two[:, None],
                grad_router,
                jnp.zeros((model, MISC - 2 - all_experts), F32),
            ],
            axis=1,
        ).astype(BF16)
        grad_qkv = jnp.concatenate([grad_packed, grad_side], axis=1)
        return d_stream, weight_pieces, grad_output.astype(BF16), grad_qkv

    def dense_scatter(grad):
        width = grad.shape[1] // 2
        shaped = grad.reshape(planes, shards, part_rows, 2 * width)
        size = (planes, shards, part_rows, width)
        kept = lax.dynamic_slice(shaped, (0, 0, 0, core * width), size)
        sent = lax.dynamic_slice(shaped, (0, 0, 0, (1 - core) * width), size)
        summed = (kept.astype(F32) + swap(sent).astype(F32)).astype(BF16)

        def chunk(owner, start, stop):
            return lax.dynamic_slice(
                summed, (start, owner, 0, 0), (stop - start, 1, part_rows, width)
            )[:, 0]

        if shards == 4:
            middle = planes // 2
            chunks = [
                chunk(shard, 0, planes),
                chunk(shard ^ 1, 0, planes),
                chunk(shard ^ 2, 0, planes),
                chunk(shard ^ 3, 0, middle),
                chunk(shard ^ 3, middle, planes),
            ]
        else:
            chunks = [
                chunk(lax.rem(shard - k + shards, shards), 0, planes) for k in range(shards)
            ]
        lined = ring_scatter(chunks, 0)
        total = lax.dynamic_index_in_dim(lined, plane, 0, keepdims=False)
        for k in range(1, planes):
            sent = lax.dynamic_index_in_dim(
                lined, lax.rem(plane - k + planes, planes), 0, keepdims=False
            )
            total = total + shifted(sent.astype(BF16), "expert", -k).astype(F32)
        return total

    def expert_scatter(pieces):
        count = len(pieces) // 2
        summed = [
            (mine.astype(F32) + swap(other).astype(F32)).astype(BF16)
            for mine, other in zip(pieces[:count], pieces[count:])
        ]
        return ring_scatter(summed, 1)

    def regrouped(halves):
        kept = jnp.where(first, halves[0], halves[1])
        sent = jnp.where(first, halves[1], halves[0])
        received = swap(sent.astype(BF16)).astype(F32)
        return by_layer(kept, received)

    start = mine_of(inputs)[0]
    result_one, kept_one = forward(0, start.astype(F32))
    result_two, kept_two = forward(1, result_one.astype(F32))
    last = mine_of(cotangent)[0]
    last_rows = jnp.concatenate(slots_of(last, "expert"), axis=0)
    grad_mid, experts_two, output_two, qkv_two = backward(1, kept_two, last_rows)
    mid_rows = jnp.concatenate(slots_of(grad_mid, "expert"), axis=0)
    grad_start, experts_one, output_one, qkv_one = backward(0, kept_one, mid_rows)

    def placed(by_layers):
        own = jnp.where(first, by_layers[0], by_layers[1])
        sent = jnp.where(first, by_layers[1], by_layers[0])
        return jnp.stack(by_layer(own, swap(sent)))

    layer_local = placed([result_one, result_two])
    input_local = placed([grad_start, grad_mid])
    scattered_two = expert_scatter(experts_two)
    scattered_one = expert_scatter(experts_one)
    expert_low, expert_high = regrouped([scattered_one, scattered_two])
    output_halves = regrouped([dense_scatter(output_one), dense_scatter(output_two)])
    grad_output = jnp.concatenate(output_halves, axis=1)
    grad_qkv = jnp.concatenate(
        regrouped([dense_scatter(qkv_one), dense_scatter(qkv_two)]), axis=1
    )
    side = grad_qkv[:, query_width + 2 * kv_width :]

    def third(index):
        start = index * half_hidden
        stop = start + half_hidden
        return jnp.concatenate([expert_low[:, :, start:stop], expert_high[:, :, start:stop]], axis=2)

    out_shape = (1, 2, 1, span_rows, model)
    return (
        layer_local.reshape(out_shape),
        input_local.reshape(out_shape),
        side[:, 0][None],
        grad_qkv[:, :query_width][None],
        grad_qkv[:, query_width : query_width + kv_width][None],
        grad_qkv[:, query_width + kv_width : query_width + 2 * kv_width][None],
        grad_output[None],
        side[:, 1][None],
        side[:, 2 : 2 + all_experts][None],
        third(0)[None],
        third(1)[None],
        jnp.swapaxes(third(2), 1, 2)[None],
    )


def solution(mesh):
    placed = (
        P(None, "expert", "shard", None),
        P(None, "expert", "shard", None),
        P(None, "expert", "shard"),
        P("section", None, "expert", "shard", None),
        P("section", ("expert", "shard")),
        P("section", ("expert", "shard"), None),
        P("section", ("expert", "shard"), None),
        P("section", ("expert", "shard"), None),
        P("section", ("expert", "shard"), None),
        P("section", ("expert", "shard")),
        P("section", ("expert", "shard"), None),
        P("section", "expert", "shard", None),
        P("section", "expert", "shard", None),
        P("section", "expert", None, "shard"),
    )
    return jax.shard_map(
        on_device,
        mesh=mesh,
        in_specs=placed,
        out_specs=(
            P("section", None, "expert", "shard", None),
            P("section", None, "expert", "shard", None),
            P("section", ("expert", "shard")),
            P("section", ("expert", "shard"), None),
            P("section", ("expert", "shard"), None),
            P("section", ("expert", "shard"), None),
            P("section", ("expert", "shard"), None),
            P("section", ("expert", "shard")),
            P("section", ("expert", "shard"), None),
            P("section", "expert", "shard", None),
            P("section", "expert", "shard", None),
            P("section", "expert", None, "shard"),
        ),
        check_vma=False,
    )
```

```python
import functools
import math

import jax
import jax.numpy as jnp
from jax import lax
from jax.experimental import pallas as pl
from jax.experimental.pallas import tpu as pltpu
from jax.sharding import PartitionSpec as P

HEADS = 24
KV_HEADS = 8
HEAD = 64

EPSILON = 1e-06
ROPE_BASE = 10000.0
NEGATIVE = -1e30
LANES = 128
TILE = 256
VMEM_LIMIT = 60 * 1024 * 1024

F32 = jnp.float32
BF16 = jnp.bfloat16


def lasting(micros):
    return pl.CostEstimate(
        flops=int(micros * 1.1e9), bytes_accessed=1000000, transcendentals=0
    )


def swap(array):
    return lax.ppermute(array, "section", [(0, 1), (1, 0)])


def shifted(array, axis, by):
    length = lax.axis_size(axis)
    return lax.ppermute(array, axis, [(i, (i + by) % length) for i in range(length)])


def flipped(array, mask):
    return lax.ppermute(array, "shard", [(i, i ^ mask) for i in range(lax.axis_size("shard"))])


def slots_of(array, axis):
    return [array] + [shifted(array, axis, k) for k in range(1, lax.axis_size(axis))]


def after(array, *others):
    return lax.optimization_barrier((array, *others))[0]


def cut(array, start, stop, axis):
    return lax.slice_in_dim(array, start, stop, axis=axis)


def ring_gather(array, axis, held=()):
    count = lax.axis_size("shard")
    me = lax.axis_index("shard")
    if count != 4:
        pieces = [
            (slot, lax.rem(me - k + count, count), 0)
            for k, slot in enumerate(slots_of(array, "shard"))
        ]
        return pieces, [piece for piece, _, _ in pieces[1:]]
    length = array.shape[axis]
    half = length // 2
    one = flipped(array, 1)
    two = flipped(array, 2)
    if held:
        one, two = lax.optimization_barrier((one, two, *held))[:2]
    far_low = flipped(cut(one, 0, half, axis), 2)
    far_high = flipped(cut(two, half, length, axis), 1)
    return [
        (array, me, 0),
        (one, me ^ 1, 0),
        (two, me ^ 2, 0),
        (far_low, me ^ 3, 0),
        (far_high, me ^ 3, half),
    ], [one, two]


def scatter_first(pieces, axis):
    if lax.axis_size("shard") != 4:
        return [shifted(pieces[k], "shard", -k) for k in range(1, len(pieces))]
    own, one, two, far_low, far_high = pieces
    half = far_low.shape[axis]
    length = own.shape[axis]
    return [
        flipped(far_low, 2),
        flipped(far_high, 1),
        flipped(cut(one, half, length, axis), 1),
        flipped(cut(two, 0, half, axis), 2),
    ]


def scatter_second(pieces, first, axis):
    if lax.axis_size("shard") != 4:
        return []
    own, one, two, far_low, far_high = pieces
    half = far_low.shape[axis]
    length = own.shape[axis]
    low, high = first[:2]
    return [
        flipped((cut(one, 0, half, axis).astype(F32) + low.astype(F32)).astype(BF16), 1),
        flipped((cut(two, half, length, axis).astype(F32) + high.astype(F32)).astype(BF16), 2),
    ]


def scatter_end(pieces, first, second, axis):
    if lax.axis_size("shard") != 4:
        return sum((array.astype(F32) for array in first), pieces[0].astype(F32))
    one_high, two_low = first[2:]
    one_low, two_high = second
    return pieces[0].astype(F32) + jnp.concatenate(
        [
            one_low.astype(F32) + two_low.astype(F32),
            one_high.astype(F32) + two_high.astype(F32),
        ],
        axis=axis,
    )


def rotary_tables(positions):
    frequency = 1.0 / ROPE_BASE ** (jnp.arange(0, HEAD, 2, dtype=F32) / HEAD)
    angles = positions.astype(F32)[:, None] * frequency[None, :]
    cosines, sines = jnp.cos(angles), jnp.sin(angles)
    return (
        jnp.concatenate([cosines] * 4, axis=1),
        jnp.concatenate([-sines, sines] * 2, axis=1),
    )


def norm_back(grad_in, values, scale_rows, scale_gain):
    shaped = grad_in * scale_gain
    grad_values = scale_rows * shaped - values * scale_rows**3 * jnp.mean(
        shaped * values, axis=-1, keepdims=True
    )
    return (grad_values, jnp.sum(grad_in * values * scale_rows, axis=0))


def dot_nt(left, right):
    return lax.dot_general(left, right, (((1,), (1,)), ((), ())), preferred_element_type=F32)


def dot_nn(left, right):
    return jnp.dot(left, right, preferred_element_type=F32)


def dot_tn(left, right):
    return lax.dot_general(left, right, (((0,), (0,)), ((), ())), preferred_element_type=F32)


def fill_weights(ref, gate_up, down):
    parts, _, depth, columns = ref.shape
    width = columns // 3
    for index in range(parts):
        half, place = divmod(index, parts // 2)
        span = slice(place * depth, (place + 1) * depth)
        gate_up[span, 2 * half * width : 2 * (half + 1) * width] = ref[index, 0, :, : 2 * width]
        down[span, half * width : (half + 1) * width] = ref[index, 0, :, 2 * width :]


def column_of(table, index):
    lane = lax.broadcasted_iota(jnp.int32, table.shape, 1)
    return jnp.sum(jnp.where(lane == index, table, 0.0), axis=1, keepdims=True)


def split_gate_up(raw, width):
    gate = jnp.concatenate([raw[:, :width], raw[:, 2 * width : 3 * width]], axis=1)
    up = jnp.concatenate([raw[:, width : 2 * width], raw[:, 3 * width :]], axis=1)
    return gate, up


def join_gate_up(gate, up, width):
    return jnp.concatenate(
        [gate[:, :width], up[:, :width], gate[:, width:], up[:, width:]], axis=1
    )


def moe_forward(rows, gates, weights):
    total, model = rows.shape
    parts, experts, depth, columns = weights.shape
    width = columns // 3
    tile = min(TILE, total)

    def body(rows_ref, gates_ref, weights_ref, out_ref, raw_ref, gate_up, down, sums):
        expert = pl.program_id(0)
        fill_weights(weights_ref, gate_up, down)

        def step(index, carry):
            span = pl.ds(pl.multiple_of(index * tile, tile), tile)
            raw = dot_nn(rows_ref[span, :], gate_up[...])
            raw_ref[0, span, :] = raw.astype(BF16)
            gate, up = split_gate_up(raw, width)
            weight = column_of(gates_ref[span, :], expert)
            act = (gate * jax.nn.sigmoid(gate) * up * weight).astype(BF16)
            part = dot_nt(act, down[...])

            @pl.when(expert == 0)
            def _():
                sums[span, :] = part

            @pl.when(expert > 0)
            def _():
                sums[span, :] += part

            @pl.when(expert == experts - 1)
            def _():
                out_ref[span, :] = sums[span, :].astype(BF16)

            return carry

        lax.fori_loop(0, total // tile, step, 0)

    whole = lambda e: (0, 0)
    per_expert = lambda e: (e, 0, 0)
    once = pl.Buffered(1)
    return pl.pallas_call(
        body,
        grid_spec=pltpu.PrefetchScalarGridSpec(
            num_scalar_prefetch=0,
            grid=(experts,),
            in_specs=[
                pl.BlockSpec((total, model), whole, pipeline_mode=once),
                pl.BlockSpec((total, LANES), whole, pipeline_mode=once),
            ]
            + [pl.BlockSpec((parts, 1, depth, columns), lambda e: (0, e, 0, 0))],
            out_specs=[
                pl.BlockSpec((total, model), whole),
                pl.BlockSpec((1, total, 4 * width), per_expert),
            ],
            scratch_shapes=[
                pltpu.VMEM((model, 4 * width), BF16),
                pltpu.VMEM((model, 2 * width), BF16),
                pltpu.VMEM((total, model), F32),
            ],
        ),
        out_shape=[
            jax.ShapeDtypeStruct((total, model), BF16),
            jax.ShapeDtypeStruct((experts, total, 4 * width), BF16),
        ],
        compiler_params=pltpu.CompilerParams(vmem_limit_bytes=VMEM_LIMIT),
        cost_estimate=lasting(40),
        name="moe_forward",
    )(rows, gates, weights)


def moe_backward_rows(grads, gates, raws, weights):
    total, model = grads.shape
    parts, experts, depth, columns = weights.shape
    width = columns // 3
    tile = min(TILE, total)

    def body(
        grads_ref,
        gates_ref,
        raw_ref,
        weights_ref,
        out_ref,
        scores_ref,
        d_raw_ref,
        act_ref,
        gate_up,
        down,
        sums,
    ):
        expert = pl.program_id(0)
        fill_weights(weights_ref, gate_up, down)

        def step(index, carry):
            span = pl.ds(pl.multiple_of(index * tile, tile), tile)
            weight = column_of(gates_ref[span, :], expert)
            gate, up = split_gate_up(raw_ref[0, span, :].astype(F32), width)
            back = dot_nn(grads_ref[span, :], down[...])
            sigmoid = jax.nn.sigmoid(gate)
            swish = gate * sigmoid
            act = swish * up
            score = jnp.sum(back * act, axis=1, keepdims=True)
            act_ref[0, span, :] = (act * weight).astype(BF16)
            d_act = back * weight
            d_gate = d_act * up * sigmoid * (1.0 + gate * (1.0 - sigmoid))
            d_raw = join_gate_up(d_gate, d_act * swish, width).astype(BF16)
            d_raw_ref[0, span, :] = d_raw
            part = dot_nt(d_raw, gate_up[...])
            lane = lax.broadcasted_iota(jnp.int32, (tile, LANES), 1)

            @pl.when(expert == 0)
            def _():
                sums[span, :] = part
                scores_ref[span, :] = jnp.where(lane == 0, score, 0.0)

            @pl.when(expert > 0)
            def _():
                sums[span, :] += part
                scores_ref[span, :] = jnp.where(lane == expert, score, scores_ref[span, :])

            @pl.when(expert == experts - 1)
            def _():
                out_ref[span, :] = sums[span, :].astype(BF16)

            return carry

        lax.fori_loop(0, total // tile, step, 0)

    whole = lambda e: (0, 0)
    per_expert = lambda e: (e, 0, 0)
    once = pl.Buffered(1)
    return pl.pallas_call(
        body,
        grid_spec=pltpu.PrefetchScalarGridSpec(
            num_scalar_prefetch=0,
            grid=(experts,),
            in_specs=[
                pl.BlockSpec((total, model), whole, pipeline_mode=once),
                pl.BlockSpec((total, LANES), whole, pipeline_mode=once),
                pl.BlockSpec((1, total, 4 * width), per_expert),
            ]
            + [pl.BlockSpec((parts, 1, depth, columns), lambda e: (0, e, 0, 0))],
            out_specs=[
                pl.BlockSpec((total, model), whole),
                pl.BlockSpec((total, LANES), whole),
                pl.BlockSpec((1, total, 4 * width), per_expert),
                pl.BlockSpec((1, total, 2 * width), per_expert),
            ],
            scratch_shapes=[
                pltpu.VMEM((model, 4 * width), BF16),
                pltpu.VMEM((model, 2 * width), BF16),
                pltpu.VMEM((total, model), F32),
            ],
        ),
        out_shape=[
            jax.ShapeDtypeStruct((total, model), BF16),
            jax.ShapeDtypeStruct((total, LANES), F32),
            jax.ShapeDtypeStruct((experts, total, 4 * width), BF16),
            jax.ShapeDtypeStruct((experts, total, 2 * width), BF16),
        ],
        compiler_params=pltpu.CompilerParams(vmem_limit_bytes=VMEM_LIMIT),
        cost_estimate=lasting(48),
        name="moe_backward_rows",
    )(grads, gates, raws, weights)


def moe_backward_weights(rows, grads, d_raws, acts, parts):
    total, model = rows.shape
    experts = d_raws.shape[0]
    width = d_raws.shape[2] // 4
    shards = parts // 2
    depth = model // shards

    def body(rows_ref, grads_ref, d_raw_ref, act_ref, out_ref, rows_t, grads_t):
        @pl.when(pl.program_id(0) == 0)
        def _():
            for start in range(0, model, TILE):
                rows_t[start : start + TILE, :] = rows_ref[:, start : start + TILE].T
                grads_t[start : start + TILE, :] = grads_ref[:, start : start + TILE].T

        for place in range(shards):
            span = slice(place * depth, (place + 1) * depth)
            gate_up = dot_nn(rows_t[span, :], d_raw_ref[0]).astype(BF16)
            down = dot_nn(grads_t[span, :], act_ref[0]).astype(BF16)
            for half in range(2):
                index = half * shards + place
                out_ref[index, 0, :, : 2 * width] = gate_up[
                    :, 2 * half * width : 2 * (half + 1) * width
                ]
                out_ref[index, 0, :, 2 * width :] = down[:, half * width : (half + 1) * width]

    whole = lambda e: (0, 0)
    per_expert = lambda e: (e, 0, 0)
    once = pl.Buffered(1)
    return pl.pallas_call(
        body,
        grid_spec=pltpu.PrefetchScalarGridSpec(
            num_scalar_prefetch=0,
            grid=(experts,),
            in_specs=[
                pl.BlockSpec((total, model), whole, pipeline_mode=once),
                pl.BlockSpec((total, model), whole, pipeline_mode=once),
                pl.BlockSpec((1, total, 4 * width), per_expert),
                pl.BlockSpec((1, total, 2 * width), per_expert),
            ],
            out_specs=pl.BlockSpec((parts, 1, depth, 3 * width), lambda e: (0, e, 0, 0)),
            scratch_shapes=[
                pltpu.VMEM((model, total), BF16),
                pltpu.VMEM((model, total), BF16),
            ],
        ),
        out_shape=jax.ShapeDtypeStruct((parts, experts, depth, 3 * width), BF16),
        compiler_params=pltpu.CompilerParams(vmem_limit_bytes=VMEM_LIMIT),
        cost_estimate=lasting(34),
        name="moe_backward_weights",
    )(rows, grads, d_raws, acts)


def line_up(pieces, owners, planes_of, shards):
    arrays = [piece for piece, _, _ in pieces]
    slots, rows, width = arrays[0].shape
    copies = slots * shards
    if rows % 16:
        result = jnp.zeros((slots, shards, rows, width), BF16)
        for place, (array, _, start) in enumerate(pieces):
            for slot in range(array.shape[0]):
                result = lax.dynamic_update_slice(
                    result,
                    array[slot][None, None],
                    (planes_of[start + slot], owners[place], 0, 0),
                )
        return result.reshape(copies * rows, width)

    def body(owner_ref, plane_ref, *refs):
        out_ref, sems = refs[len(arrays) :]
        started = []
        for place, (array, _, start) in enumerate(pieces):
            for slot in range(array.shape[0]):
                index = plane_ref[start + slot] * shards + owner_ref[place]
                started.append(
                    pltpu.make_async_copy(
                        refs[place].at[slot],
                        out_ref.at[pl.ds(pl.multiple_of(index * rows, 16), rows), :],
                        sems.at[len(started)],
                    )
                )
                started[-1].start()
        for copy in started:
            copy.wait()

    return pl.pallas_call(
        body,
        grid_spec=pltpu.PrefetchScalarGridSpec(
            num_scalar_prefetch=2,
            grid=(1,),
            in_specs=[pl.BlockSpec(memory_space=pl.ANY)] * len(arrays),
            out_specs=pl.BlockSpec((copies * rows, width), lambda i, *_: (0, 0)),
            scratch_shapes=[pltpu.SemaphoreType.DMA((copies * 2,))],
        ),
        out_shape=jax.ShapeDtypeStruct((copies * rows, width), BF16),
        compiler_params=pltpu.CompilerParams(vmem_limit_bytes=VMEM_LIMIT),
        cost_estimate=lasting(4),
        name="line_up",
    )(owners, planes_of, *arrays)


def turned(values, cosines, sines):
    lane = lax.broadcasted_iota(jnp.int32, cosines.shape, 1)
    low = lane % HEAD < HEAD // 2
    parts = []
    for start in range(0, values.shape[1], LANES):
        block = values[:, start : start + LANES]
        partner = jnp.where(
            low,
            pltpu.roll(block, LANES - HEAD // 2, 1),
            pltpu.roll(block, HEAD // 2, 1),
        )
        parts.append(block * cosines + partner * sines)
    return jnp.concatenate(parts, axis=1)


def pair_columns(width):
    return [start for start in range(0, width, 2 * LANES)]


def half_specs(halves, columns):
    return [
        pl.BlockSpec((1, array.shape[1], columns), lambda i, place=place: (place, 0, 0))
        for array, place in halves
    ]


def qkv_forward(stream, gain, halves, cosines, sines, columns):
    rows, model = stream.shape
    queries, kv = columns

    def body(stream_ref, gain_ref, mine_ref, other_ref, cos_ref, sin_ref, q_ref, kv_ref, n_ref):
        values = stream_ref[...]
        scale = lax.rsqrt(jnp.mean(values * values, axis=1, keepdims=True) + EPSILON)
        n_ref[...] = (values * scale * gain_ref[...]).astype(BF16)
        cos, sin = cos_ref[...], sin_ref[...]
        for index, ref in enumerate((mine_ref, other_ref)):
            raw = dot_nn(n_ref[...], ref[0])
            q_ref[:, index * queries : (index + 1) * queries] = turned(
                raw[:, :queries], cos, sin
            ).astype(BF16)
            for start in pair_columns(kv):
                place = index * kv + start
                keys = raw[:, queries + start : queries + start + LANES]
                kv_ref[:, place : place + LANES] = turned(keys, cos, sin).astype(BF16)
                kv_ref[:, place + LANES : place + 2 * LANES] = raw[
                    :, queries + start + LANES : queries + start + 2 * LANES
                ].astype(BF16)

    whole = lambda i: (0, 0)
    return pl.pallas_call(
        body,
        grid=(1,),
        in_specs=[
            pl.BlockSpec((rows, model), whole),
            pl.BlockSpec((1, model), whole),
            *half_specs(halves, queries + kv),
            pl.BlockSpec((rows, LANES), whole),
            pl.BlockSpec((rows, LANES), whole),
        ],
        out_specs=[
            pl.BlockSpec((rows, 2 * queries), whole),
            pl.BlockSpec((rows, 2 * kv), whole),
            pl.BlockSpec((rows, model), whole),
        ],
        out_shape=[
            jax.ShapeDtypeStruct((rows, 2 * queries), BF16),
            jax.ShapeDtypeStruct((rows, 2 * kv), BF16),
            jax.ShapeDtypeStruct((rows, model), BF16),
        ],
        compiler_params=pltpu.CompilerParams(vmem_limit_bytes=VMEM_LIMIT),
        cost_estimate=lasting(7),
        name="qkv_forward",
    )(stream, gain, *[array for array, _ in halves], cosines, sines)


def qkv_backward(
    normed, d_queries, d_kv_slots, halves, cosines, sines, columns, stream, side, owns, extra
):
    rows, model = normed.shape
    queries, kv = columns
    qkv = queries + kv
    count = len(d_kv_slots)
    more = extra[0].shape[1] if extra else 0

    def body(n_ref, dq_ref, *refs):
        slots = refs[:count]
        mine_ref, other_ref, cos_ref, sin_ref, stream_ref, side_ref, owns_ref = refs[
            count : count + 7
        ]
        extra_refs = refs[count + 7 : count + 7 + len(extra)]
        out_ref, grad_ref, n_t = refs[count + 7 + len(extra) :]
        cos, sin = cos_ref[...], -sin_ref[...]
        n_t[...] = n_ref[...].T
        for index, ref in ((0, mine_ref), (1, other_ref)):
            span = slice(index * kv, (index + 1) * kv)
            d_kv = slots[0][:, span].astype(F32)
            for slot in slots[1:]:
                d_kv = d_kv + slot[:, span].astype(F32)
            parts = [dq_ref[:, index * queries : (index + 1) * queries]]
            for start in pair_columns(kv):
                parts.append(turned(d_kv[:, start : start + LANES], cos, sin).astype(BF16))
                parts.append(d_kv[:, start + LANES : start + 2 * LANES].astype(BF16))
            d_raw = jnp.concatenate(parts, axis=1)
            back = dot_nt(d_raw, ref[0])
            if index == 0:
                out_ref[...] = back
            else:
                out_ref[...] += back
            grad_ref[index, :, :qkv] = dot_nn(n_t[...], d_raw).astype(BF16)
        values = stream_ref[...]
        scale = lax.rsqrt(jnp.mean(values * values, axis=1, keepdims=True) + EPSILON)
        gain = jnp.sum(out_ref[...] * values * scale, axis=0, keepdims=True)
        gain = jnp.broadcast_to(gain, (LANES, model)).T
        lane = lax.broadcasted_iota(jnp.int32, (model, LANES), 1)
        whole_side = jnp.where(lane == 0, gain, side_ref[...])
        for index in range(2):
            grad_ref[index, :, qkv : qkv + LANES] = (
                whole_side * owns_ref[index : index + 1, :]
            ).astype(BF16)
            if extra:
                grad_ref[index, :, qkv + LANES :] = extra_refs[index][...]

    whole = lambda i: (0, 0)
    return pl.pallas_call(
        body,
        grid=(1,),
        in_specs=[
            pl.BlockSpec((rows, model), whole),
            pl.BlockSpec((rows, 2 * queries), whole),
        ]
        + [pl.BlockSpec((rows, 2 * kv), whole)] * count
        + half_specs(halves, qkv)
        + [
            pl.BlockSpec((rows, LANES), whole),
            pl.BlockSpec((rows, LANES), whole),
            pl.BlockSpec((rows, model), whole),
            pl.BlockSpec((model, LANES), whole),
            pl.BlockSpec((8, LANES), whole),
        ]
        + [pl.BlockSpec((model, more), whole) for _ in extra],
        out_specs=[
            pl.BlockSpec((rows, model), whole),
            pl.BlockSpec((2, model, qkv + LANES + more), lambda i: (0, 0, 0)),
        ],
        out_shape=[
            jax.ShapeDtypeStruct((rows, model), F32),
            jax.ShapeDtypeStruct((2, model, qkv + LANES + more), BF16),
        ],
        scratch_shapes=[pltpu.VMEM((model, rows), BF16)],
        compiler_params=pltpu.CompilerParams(vmem_limit_bytes=VMEM_LIMIT),
        cost_estimate=lasting(14),
        name="qkv_backward",
    )(
        normed,
        d_queries,
        *d_kv_slots,
        *[array for array, _ in halves],
        cosines,
        sines,
        stream,
        side,
        owns,
        *extra,
    )


def head_sides(block):
    lane = lax.broadcasted_iota(jnp.int32, block.shape, 1)
    low = lane < HEAD
    crossed = jnp.concatenate([block[:, HEAD:], block[:, :HEAD]], axis=1)
    nothing = jnp.zeros_like(block)
    return [
        [jnp.where(low, block, nothing), jnp.where(low, nothing, crossed)],
        [jnp.where(low, crossed, nothing), jnp.where(low, nothing, block)],
    ]


def fill_bias(bias, owner_ref, seg_all_ref, seg_ref, rows, count):
    own = owner_ref[0] * rows + lax.broadcasted_iota(jnp.int32, (rows, rows), 1)
    for slot in range(count):
        span = slice(slot * rows, (slot + 1) * rows)
        place = owner_ref[slot] * rows + lax.broadcasted_iota(jnp.int32, (rows, rows), 0)
        allowed = (place <= own) & (seg_all_ref[span, :1] == seg_ref[:1, :])
        bias[span, :] = jnp.where(allowed, 0.0, NEGATIVE)


def attention_specs(rows, count, group):
    whole = lambda p, *_: (0, 0)
    return (
        [
            pl.BlockSpec((count * rows, LANES), whole),
            pl.BlockSpec((8, rows), whole),
            pl.BlockSpec((rows, 2 * group * HEAD), lambda p, *_: (0, p)),
        ]
        + [pl.BlockSpec((rows, 2 * LANES), lambda p, *_: (0, p))] * count
    )


def attention_forward(queries, kv_slots, owners, seg_all, seg_own):
    rows, width = queries.shape
    count = len(kv_slots)
    group = HEADS // KV_HEADS
    pairs = KV_HEADS // 2
    heads = 2 * group
    total = count * rows
    scale = 1.0 / math.sqrt(HEAD)

    def body(owner_ref, seg_all_ref, seg_ref, q_ref, *refs):
        slots = refs[:count]
        out_ref, stat_ref, bias = refs[count:]

        @pl.when(pl.program_id(0) == 0)
        def _():
            fill_bias(bias, owner_ref, seg_all_ref, seg_ref, rows, count)

        keys = head_sides(jnp.concatenate([ref[:, :LANES] for ref in slots], axis=0))
        values = head_sides(jnp.concatenate([ref[:, LANES:] for ref in slots], axis=0))
        values = [[side.T for side in sides] for sides in values]
        scaled = (q_ref[...].astype(F32) * scale).astype(BF16)
        stats = []
        for block in range(group):
            out = None
            for side in range(2):
                head = 2 * block + side
                kv = head // group
                scores = (
                    dot_nt(keys[kv][side], scaled[:, block * LANES : (block + 1) * LANES])
                    + bias[...]
                )
                top = jnp.max(scores, axis=0, keepdims=True)
                exponent = jnp.exp(scores - top)
                total_of = jnp.sum(exponent, axis=0, keepdims=True)
                probs = (exponent * (1.0 / total_of)).astype(BF16)
                part = dot_nn(values[kv][side], probs)
                out = part if out is None else out + part
                stats.append(top + jnp.log(total_of))
            out_ref[:, block * LANES : (block + 1) * LANES] = out.T.astype(BF16)
        stat_ref[0, :heads, :] = jnp.concatenate(stats, axis=0)

    return pl.pallas_call(
        body,
        grid_spec=pltpu.PrefetchScalarGridSpec(
            num_scalar_prefetch=1,
            grid=(pairs,),
            in_specs=attention_specs(rows, count, group),
            out_specs=[
                pl.BlockSpec((rows, heads * HEAD), lambda p, *_: (0, p)),
                pl.BlockSpec((1, 8, rows), lambda p, *_: (p, 0, 0)),
            ],
            scratch_shapes=[pltpu.VMEM((total, rows), F32)],
        ),
        out_shape=[
            jax.ShapeDtypeStruct((rows, width), BF16),
            jax.ShapeDtypeStruct((pairs, 8, rows), F32),
        ],
        compiler_params=pltpu.CompilerParams(vmem_limit_bytes=VMEM_LIMIT),
        cost_estimate=lasting(17),
        name="attention_forward",
    )(owners, seg_all, seg_own, queries, *kv_slots)


def attention_backward(queries, kv_slots, owners, seg_all, seg_own, d_out, stats, cosines, sines):
    rows, width = queries.shape
    count = len(kv_slots)
    group = HEADS // KV_HEADS
    pairs = KV_HEADS // 2
    heads = 2 * group
    total = count * rows
    scale = 1.0 / math.sqrt(HEAD)

    def body(owner_ref, seg_all_ref, seg_ref, q_ref, *refs):
        slots = refs[:count]
        d_out_ref, stat_ref, cos_ref, sin_ref = refs[count : count + 4]
        d_q_ref = refs[count + 4]
        d_slots = refs[count + 5 : 2 * count + 5]
        bias, d_keys, d_values = refs[2 * count + 5 :]

        @pl.when(pl.program_id(0) == 0)
        def _():
            fill_bias(bias, owner_ref, seg_all_ref, seg_ref, rows, count)

        keys = head_sides(jnp.concatenate([ref[:, :LANES] for ref in slots], axis=0))
        values = head_sides(jnp.concatenate([ref[:, LANES:] for ref in slots], axis=0))
        keys_t = [[side.T for side in sides] for sides in keys]
        cos, sin = cos_ref[...], -sin_ref[...]
        for block in range(group):
            span = slice(block * LANES, (block + 1) * LANES)
            scaled = (q_ref[:, span].astype(F32) * scale).astype(BF16)
            d_block = d_out_ref[:, span]
            q_sides = head_sides(scaled)
            d_sides = head_sides(d_block)
            d_q = None
            for side in range(2):
                head = 2 * block + side
                kv = head // group
                scores = dot_nt(keys[kv][side], scaled) + bias[...]
                probs = jnp.exp(scores - stat_ref[0, head : head + 1, :])
                d_probs = dot_nt(values[kv][side], d_block)
                share = jnp.sum(probs * d_probs, axis=0, keepdims=True)
                d_scores = (probs * (d_probs - share)).astype(BF16)
                part = dot_nn(keys_t[kv][side], d_scores)
                d_q = part if d_q is None else d_q + part
                d_key = dot_nn(d_scores, q_sides[side][kv])
                d_value = dot_nn(probs.astype(BF16), d_sides[side][kv])
                if head == 0:
                    d_keys[...] = d_key
                    d_values[...] = d_value
                else:
                    d_keys[...] += d_key
                    d_values[...] += d_value
            d_q_ref[:, span] = turned(d_q.T * scale, cos, sin).astype(BF16)
        for slot in range(count):
            part = slice(slot * rows, (slot + 1) * rows)
            d_slots[slot][:, :LANES] = d_keys[part, :].astype(BF16)
            d_slots[slot][:, LANES:] = d_values[part, :].astype(BF16)

    whole = lambda p, *_: (0, 0)
    return pl.pallas_call(
        body,
        grid_spec=pltpu.PrefetchScalarGridSpec(
            num_scalar_prefetch=1,
            grid=(pairs,),
            in_specs=attention_specs(rows, count, group)
            + [
                pl.BlockSpec((rows, heads * HEAD), lambda p, *_: (0, p)),
                pl.BlockSpec((1, 8, rows), lambda p, *_: (p, 0, 0)),
                pl.BlockSpec((rows, LANES), whole),
                pl.BlockSpec((rows, LANES), whole),
            ],
            out_specs=[pl.BlockSpec((rows, heads * HEAD), lambda p, *_: (0, p))]
            + [pl.BlockSpec((rows, 2 * LANES), lambda p, *_: (0, p))] * count,
            scratch_shapes=[
                pltpu.VMEM((total, rows), F32),
                pltpu.VMEM((total, LANES), F32),
                pltpu.VMEM((total, LANES), F32),
            ],
        ),
        out_shape=[jax.ShapeDtypeStruct((rows, width), BF16)]
        + [jax.ShapeDtypeStruct((rows, 2 * KV_HEADS * HEAD), BF16)] * count,
        compiler_params=pltpu.CompilerParams(vmem_limit_bytes=VMEM_LIMIT),
        cost_estimate=lasting(27),
        name="attention_backward",
    )(owners, seg_all, seg_own, queries, *kv_slots, d_out, stats, cosines, sines)


def on_device(
    inputs,
    cotangent,
    segments,
    routes,
    attn_gain,
    w_query,
    w_key,
    w_value,
    w_output,
    ffn_gain,
    router,
    w_gate,
    w_up,
    w_down,
):
    core = lax.axis_index("section")
    shard = lax.axis_index("shard")
    plane = lax.axis_index("expert")
    shards = lax.axis_size("shard")
    planes = lax.axis_size("expert")
    span_rows, model = inputs.shape[2:]
    seq_rows = span_rows * shards
    gathered_rows = span_rows * planes
    local_experts = w_gate.shape[1]
    all_experts = local_experts * planes
    hidden = w_gate.shape[3]
    half_hidden = hidden // 2
    part_rows = w_query.shape[1]
    query_width = HEADS * HEAD
    kv_width = KV_HEADS * HEAD
    group_size = HEADS // KV_HEADS
    score_scale = 1.0 / math.sqrt(HEAD)
    first = core == 0

    def mine_of(array):
        return lax.dynamic_index_in_dim(array, core, 0, keepdims=False)

    def by_layer(own, received):
        return [jnp.where(first, own, received), jnp.where(first, received, own)]

    def halved(own_halves):
        kept = jnp.where(first, own_halves[0], own_halves[1])
        sent = jnp.where(first, own_halves[1], own_halves[0])
        return by_layer(kept, swap(sent))

    misc = jnp.concatenate(
        [
            attn_gain[0][:, None],
            ffn_gain[0][:, None],
            router[0],
            jnp.zeros((part_rows, LANES - 2 - all_experts), BF16),
        ],
        axis=1,
    )
    half_query = query_width // 2
    half_kv = kv_width // 2
    half_qkv = half_query + 2 * half_kv

    def head_half(index, side):
        return jnp.concatenate(
            [
                w_query[0][:, index * half_query : (index + 1) * half_query],
            ]
            + [
                array[0][:, start : start + LANES]
                for start in range(index * half_kv, (index + 1) * half_kv, LANES)
                for array in (w_key, w_value)
            ]
            + [side],
            axis=1,
        )

    output_half = model // 2
    qkv_mine = halved([head_half(0, misc), head_half(1, jnp.zeros_like(misc))])
    output_mine = halved([w_output[0][:, :output_half], w_output[0][:, output_half:]])
    down_turned = jnp.swapaxes(w_down[0], 1, 2)

    def expert_half(start):
        stop = start + half_hidden
        return jnp.concatenate(
            [w_gate[0][:, :, start:stop], w_up[0][:, :, start:stop], down_turned[:, :, start:stop]],
            axis=2,
        )

    expert_mine = halved([expert_half(0), expert_half(half_hidden)])

    plane_order = jnp.stack(
        [lax.rem(plane - k + planes, planes) for k in range(planes)]
    ).astype(jnp.int32)

    segment_local = mine_of(segments)[0]
    segment_all = jnp.concatenate(
        [slot[0] for slot in slots_of(segment_local[None], "shard")]
    )
    own_routes = routes[0, :, 0]
    route_rows = by_layer(
        lax.dynamic_index_in_dim(own_routes, core, 0, keepdims=False),
        swap(lax.dynamic_index_in_dim(own_routes, 1 - core, 0, keepdims=False)),
    )
    expert_ids = jnp.arange(all_experts, dtype=jnp.int32)
    chosen = jnp.stack(
        [
            jnp.any(rows[:, :, None] == expert_ids[None, None, :], axis=1).astype(BF16)
            for rows in route_rows
        ]
    )
    chosen_all = jnp.concatenate(slots_of(jnp.swapaxes(chosen, 1, 2), "expert"), axis=2)

    def dense_weights(lined, *held):
        pieces, first_step = ring_gather(lined, 0, held)
        owners = jnp.stack([owner for _, owner, _ in pieces]).astype(jnp.int32)
        mine = line_up(pieces, owners, plane_order, shards)
        return (mine, swap(mine)), [piece for piece, _, _ in pieces[-2:]]

    lined = jnp.stack(slots_of(qkv_mine[0], "expert"))
    lined = after(lined, chosen_all, segment_all)
    lined_output = jnp.stack(slots_of(after(output_mine[0], lined), "expert"))
    first_qkv, ring_end = dense_weights(lined)
    first_experts = lax.all_gather(
        after(expert_mine[0], *ring_end), ("section", "shard"), axis=0
    )
    second_pack = lax.all_gather(
        jnp.concatenate([qkv_mine[1], output_mine[1]], axis=1),
        ("section", "expert", "shard"),
        axis=0,
        tiled=True,
    ).reshape(2, model, half_qkv + LANES + output_half)
    second_experts = lax.all_gather(expert_mine[1], ("section", "shard"), axis=0)

    qkv_columns = half_qkv + LANES

    def natural(halves, relative):
        mine, other = halves
        if not relative:
            return jnp.concatenate([mine, other], axis=1)
        return jnp.concatenate(
            [jnp.where(first, mine, other), jnp.where(first, other, mine)], axis=1
        )

    def parted(array, relative):
        half = array.shape[1] // 2
        low, high = array[:, :half], array[:, half:]
        if not relative:
            return low, high
        return jnp.where(first, low, high), jnp.where(first, high, low)

    positions = shard * span_rows + jnp.arange(span_rows, dtype=jnp.int32)
    cosines, sines = rotary_tables(positions)
    key_owners = jnp.stack(
        [lax.rem(shard - k + shards, shards) for k in range(shards)]
    ).astype(jnp.int32)
    seg_all = jnp.broadcast_to(segment_all[:, None], (seq_rows, LANES))
    seg_own = jnp.broadcast_to(segment_local[None, :], (8, span_rows))
    chosen_all = jnp.swapaxes(chosen_all, 1, 2) > 0.5

    last = mine_of(cotangent)[0]

    def attend(stream, pair, side, relative):
        gain_one = side[:, 0].astype(F32)
        gain_two = side[:, 1].astype(F32)
        query_rot, kv_own, normed = qkv_forward(
            stream, gain_one[None], pair, cosines, sines, (half_query, 2 * half_kv)
        )
        kv_slots = slots_of(kv_own, "shard")
        attended, stats = attention_forward(query_rot, kv_slots, key_owners, seg_all, seg_own)
        kept = dict(
            stream=stream,
            normed=normed,
            query_rot=query_rot,
            kv_slots=kv_slots,
            stats=stats,
            gain_one=gain_one,
            gain_two=gain_two,
            router_full=side[:, 2 : 2 + all_experts],
            qkv=pair,
            relative=relative,
        )
        return attended, kept

    def gathered_rows_of(kept, attended, pair):
        relative = kept["relative"]
        attended = natural(
            (attended[:, : query_width // 2], attended[:, query_width // 2 :]), relative
        )
        middle = kept["stream"] + natural([dot_nn(attended, half) for half in pair], relative)
        scale_two = lax.rsqrt(jnp.mean(middle * middle, axis=-1, keepdims=True) + EPSILON)
        hidden_in = (middle * scale_two * kept["gain_two"]).astype(BF16)
        rows = jnp.concatenate(slots_of(hidden_in, "expert"), axis=0)
        kept.update(
            attended=attended, middle=middle, scale_two=scale_two, hidden_in=hidden_in, output=pair
        )
        return rows

    def mix(layer, kept, rows, experts):
        logits = jnp.where(chosen_all[layer], dot_nn(rows, kept["router_full"]), NEGATIVE)
        gates = jax.nn.softmax(logits, axis=-1)
        gates = jnp.where(chosen_all[layer], gates, 0.0)
        own_gates = lax.dynamic_slice_in_dim(gates, plane * local_experts, local_experts, axis=1)
        own_gates = jnp.pad(own_gates, ((0, 0), (0, LANES - local_experts)))
        partial, raws = moe_forward(rows, own_gates, experts)
        kept.update(
            rows=rows,
            gates=gates[:span_rows],
            own_gates=own_gates,
            raws=raws,
            experts=experts,
            partial=partial,
        )
        return partial

    def combine(kept, partial):
        combined = partial[:span_rows].astype(F32)
        for k in range(1, planes):
            back = shifted(partial[k * span_rows : (k + 1) * span_rows], "expert", -k)
            combined = combined + back.astype(F32)
        return (kept["middle"] + combined).astype(BF16)

    def backward(layer, kept, grad_rows, later):
        grad_low = grad_rows[:span_rows]
        grad_out = grad_low.astype(F32)
        relative = kept["relative"]
        d_rows, scores, d_raws, acts = moe_backward_rows(
            grad_rows, kept["own_gates"], kept["raws"], kept["experts"]
        )
        scores_turned = scores.T[: max(8, local_experts)]
        d_hidden = d_rows[:span_rows].astype(F32)
        d_gates = jnp.zeros((all_experts, span_rows), F32)
        d_gates = lax.dynamic_update_slice(
            d_gates, scores_turned[:local_experts, :span_rows], (plane * local_experts, 0)
        )
        for k in range(1, planes):
            span = slice(k * span_rows, (k + 1) * span_rows)
            d_hidden = d_hidden + shifted(d_rows[span], "expert", -k).astype(F32)
            back = shifted(scores_turned[:, span], "expert", -k)
            place = lax.rem(plane + k, planes) * local_experts
            d_gates = lax.dynamic_update_slice(d_gates, back[:local_experts], (place, 0))
        expert_grads = moe_backward_weights(kept["rows"], grad_rows, d_raws, acts, 2 * shards)
        d_hidden = after(d_hidden, expert_grads)
        scattered = lax.psum_scatter(
            expert_grads, ("section", "shard"), scatter_dimension=0
        )
        gates = kept["gates"]
        d_gates = d_gates.T
        d_logits = gates * (d_gates - jnp.sum(gates * d_gates, axis=-1, keepdims=True))
        d_logits_high = d_logits.astype(BF16)
        d_logits_low = (d_logits - d_logits_high.astype(F32)).astype(BF16)
        d_hidden = (
            d_hidden
            + dot_nt(d_logits_high, kept["router_full"])
            + dot_nt(d_logits_low, kept["router_full"])
        )
        grad_router = dot_tn(kept["hidden_in"], d_logits_high) + dot_tn(
            kept["hidden_in"], d_logits_low
        )
        d_middle, grad_gain_two = norm_back(
            d_hidden, kept["middle"], kept["scale_two"], kept["gain_two"]
        )
        d_middle = grad_out + d_middle
        d_branch = d_middle.astype(BF16)
        branch_parts = parted(d_branch, relative)
        d_attended = (
            dot_nt(branch_parts[0], kept["output"][0])
            + dot_nt(branch_parts[1], kept["output"][1])
        ).astype(BF16)
        d_attended = jnp.concatenate(parted(d_attended, relative), axis=1)
        grad_output = [dot_tn(kept["attended"], part).astype(BF16) for part in branch_parts]
        d_query_raw, *d_slots = attention_backward(
            kept["query_rot"],
            kept["kv_slots"],
            key_owners,
            seg_all,
            seg_own,
            d_attended,
            kept["stats"],
            cosines,
            sines,
        )
        d_kv_slots = [d_slots[0]] + [
            shifted(d_slots[k], "shard", -k) for k in range(1, shards)
        ]
        if layer == 1:
            result = combine(kept, after(kept["partial"], d_hidden))
            d_query_raw = after(d_query_raw, result)
        else:
            result = None
            d_query_raw = after(d_query_raw, later)
        lane = jnp.arange(LANES)[None, :]
        grad_side = jnp.where(
            lane == 1,
            grad_gain_two[:, None],
            jnp.pad(grad_router, ((0, 0), (2, LANES - 2 - all_experts))),
        )
        owner = core if relative else 0
        owns = jnp.broadcast_to(
            (jnp.arange(8, dtype=jnp.int32) == owner).astype(F32)[:, None], (8, LANES)
        )
        stream = kept["stream"]
        d_normed, packed = qkv_backward(
            kept["normed"],
            d_query_raw,
            d_kv_slots,
            kept["qkv"],
            cosines,
            sines,
            (half_query, 2 * half_kv),
            stream,
            grad_side,
            owns,
            grad_output if layer == 1 else [],
        )
        scale_one = lax.rsqrt(jnp.mean(stream * stream, axis=-1, keepdims=True) + EPSILON)
        d_stream, _ = norm_back(d_normed, stream, scale_one, kept["gain_one"])
        d_stream = (d_middle + d_stream).astype(BF16)
        return d_stream, scattered, packed, grad_output, result

    def dense_scatter(halves, swapped, *held):
        width = halves[0].shape[1]
        size = (planes, shards, part_rows, width)
        kept = halves[0].reshape(size)
        received = swapped.reshape(size)
        if held:
            received = after(received, *held)

        def chunk(owner, start, stop):
            place = (start, owner, 0, 0)
            part = (stop - start, 1, part_rows, width)
            summed = lax.dynamic_slice(kept, place, part).astype(F32) + lax.dynamic_slice(
                received, place, part
            ).astype(F32)
            return summed[:, 0].astype(BF16)

        if shards == 4:
            middle = planes // 2
            chunks = [
                chunk(shard, 0, planes),
                chunk(shard ^ 1, 0, planes),
                chunk(shard ^ 2, 0, planes),
                chunk(shard ^ 3, 0, middle),
                chunk(shard ^ 3, middle, planes),
            ]
        else:
            chunks = [
                chunk(lax.rem(shard - k + shards, shards), 0, planes) for k in range(shards)
            ]
        first_step = scatter_first(chunks, 0)
        second_step = scatter_second(chunks, first_step, 0)
        lined = scatter_end(chunks, first_step, second_step, 0)
        return {"first": first_step, "second": second_step, "lined": lined}

    def plane_scatter(lined):
        total = lax.dynamic_index_in_dim(lined, plane, 0, keepdims=False)
        for k in range(1, planes):
            sent = lax.dynamic_index_in_dim(
                lined, lax.rem(plane - k + planes, planes), 0, keepdims=False
            )
            total = total + shifted(sent.astype(BF16), "expert", -k).astype(F32)
        return total

    def regrouped(halves):
        kept = jnp.where(first, halves[0], halves[1])
        sent = jnp.where(first, halves[1], halves[0])
        received = swap(sent.astype(BF16)).astype(F32)
        return by_layer(kept, received)

    start = mine_of(inputs)[0]
    side = jnp.where(
        first, first_qkv[0][:, half_qkv:qkv_columns], first_qkv[1][:, half_qkv:qkv_columns]
    )
    attended, kept_one = attend(
        start.astype(F32), [(half[None], 0) for half in first_qkv], side, True
    )
    first_output, _ = dense_weights(after(lined_output, *ring_end), kept_one["query_rot"])
    rows = gathered_rows_of(kept_one, attended, first_output)
    result_one = combine(kept_one, mix(0, kept_one, rows, first_experts))

    last_rows = jnp.concatenate(slots_of(after(last, result_one), "expert"), axis=0)
    attended, kept_two = attend(
        result_one.astype(F32),
        [(second_pack, 0), (second_pack, 1)],
        second_pack[0, :, half_qkv:qkv_columns],
        False,
    )
    attended = after(attended, last_rows)
    rows = gathered_rows_of(kept_two, attended, [half[:, qkv_columns:] for half in second_pack])
    mix(1, kept_two, rows, second_experts)

    grad_mid, scattered_two, packed_two, _, result_two = backward(1, kept_two, last_rows, None)
    pack_two = lax.psum_scatter(
        packed_two.reshape(2 * model, packed_two.shape[2]),
        ("section", "expert", "shard"),
        scatter_dimension=0,
        tiled=True,
    )
    mid_rows = jnp.concatenate(slots_of(grad_mid, "expert"), axis=0)
    mid_rows = after(mid_rows, scattered_two)
    grad_start, scattered_one, packed_one, output_one, _ = backward(
        0, kept_one, mid_rows, pack_two
    )
    qkv_one = [packed_one[0], packed_one[1]]

    def placed(by_layers):
        own = jnp.where(first, by_layers[0], by_layers[1])
        sent = jnp.where(first, by_layers[1], by_layers[0])
        return jnp.stack(by_layer(own, swap(sent)))

    layer_local = placed([result_one, result_two])
    input_local = placed([grad_start, grad_mid])
    expert_low, expert_high = regrouped([scattered_one, scattered_two])
    output_scatter = dense_scatter(output_one, swap(output_one[1]))
    qkv_scatter = dense_scatter(qkv_one, swap(qkv_one[1]))
    dense_one = jnp.concatenate(
        [plane_scatter(qkv_scatter["lined"]), plane_scatter(output_scatter["lined"])], axis=1
    )
    dense_low, dense_high = regrouped([dense_one, pack_two.astype(F32)])

    def both(start, stop):
        return jnp.concatenate([dense_low[:, start:stop], dense_high[:, start:stop]], axis=1)

    def every_other(start):
        return jnp.concatenate(
            [
                half[:, place : place + LANES]
                for half in (dense_low, dense_high)
                for place in range(start, half_qkv, 2 * LANES)
            ],
            axis=1,
        )

    side = dense_low[:, half_qkv:qkv_columns]

    def third(index):
        start = index * half_hidden
        stop = start + half_hidden
        return jnp.concatenate([expert_low[:, :, start:stop], expert_high[:, :, start:stop]], axis=2)

    out_shape = (1, 2, 1, span_rows, model)
    return (
        layer_local.reshape(out_shape),
        input_local.reshape(out_shape),
        side[:, 0][None],
        both(0, half_query)[None],
        every_other(half_query)[None],
        every_other(half_query + LANES)[None],
        both(qkv_columns, qkv_columns + output_half)[None],
        side[:, 1][None],
        side[:, 2 : 2 + all_experts][None],
        third(0)[None],
        third(1)[None],
        jnp.swapaxes(third(2), 1, 2)[None],
    )


def solution(mesh):
    placed = (
        P(None, "expert", "shard", None),
        P(None, "expert", "shard", None),
        P(None, "expert", "shard"),
        P("section", None, "expert", "shard", None),
        P("section", ("expert", "shard")),
        P("section", ("expert", "shard"), None),
        P("section", ("expert", "shard"), None),
        P("section", ("expert", "shard"), None),
        P("section", ("expert", "shard"), None),
        P("section", ("expert", "shard")),
        P("section", ("expert", "shard"), None),
        P("section", "expert", "shard", None),
        P("section", "expert", "shard", None),
        P("section", "expert", None, "shard"),
    )
    return jax.shard_map(
        on_device,
        mesh=mesh,
        in_specs=placed,
        out_specs=(
            P("section", None, "expert", "shard", None),
            P("section", None, "expert", "shard", None),
            P("section", ("expert", "shard")),
            P("section", ("expert", "shard"), None),
            P("section", ("expert", "shard"), None),
            P("section", ("expert", "shard"), None),
            P("section", ("expert", "shard"), None),
            P("section", ("expert", "shard")),
            P("section", ("expert", "shard"), None),
            P("section", "expert", "shard", None),
            P("section", "expert", "shard", None),
            P("section", "expert", None, "shard"),
        ),
        check_vma=False,
    )
```

```python
import functools
import math

import jax
import jax.numpy as jnp
from jax import lax
from jax.experimental import pallas as pl
from jax.experimental.pallas import tpu as pltpu
from jax.sharding import PartitionSpec as P

HEADS = 24
KV_HEADS = 8
HEAD = 64

EPSILON = 1e-06
ROPE_BASE = 10000.0
NEGATIVE = -1e30
LANES = 128
TILE = 256
ROWS = 1024
VMEM_LIMIT = 60 * 1024 * 1024

F32 = jnp.float32
BF16 = jnp.bfloat16


def lasting(micros):
    return pl.CostEstimate(
        flops=int(micros * 1.1e9), bytes_accessed=1000000, transcendentals=0
    )


def swap(array):
    return lax.ppermute(array, "section", [(0, 1), (1, 0)])


def shifted(array, axis, by):
    length = lax.axis_size(axis)
    return lax.ppermute(array, axis, [(i, (i + by) % length) for i in range(length)])


def flipped(array, mask):
    return lax.ppermute(array, "shard", [(i, i ^ mask) for i in range(lax.axis_size("shard"))])


def crossed(array, axis, by):
    length = lax.axis_size(axis)
    if length & (length - 1):
        return shifted(array, axis, by)
    return lax.ppermute(array, axis, [(i, i ^ by) for i in range(length)])


def crossed_back(array, axis, by):
    length = lax.axis_size(axis)
    return shifted(array, axis, -by) if length & (length - 1) else crossed(array, axis, by)


def partner(axis, by, back=False):
    length, me = lax.axis_size(axis), lax.axis_index(axis)
    if length & (length - 1):
        return lax.rem(me + (by if back else length - by), length)
    return me ^ by


def slots_of(array, axis):
    return [array] + [crossed(array, axis, k) for k in range(1, lax.axis_size(axis))]


def after(array, *others):
    return lax.optimization_barrier((array, *others))[0]


def cut(array, start, stop, axis):
    return lax.slice_in_dim(array, start, stop, axis=axis)


def ring_gather(array, axis, held=()):
    count = lax.axis_size("shard")
    me = lax.axis_index("shard")
    if count != 4:
        pieces = [
            (slot, partner("shard", k) if k else me, 0)
            for k, slot in enumerate(slots_of(array, "shard"))
        ]
        return pieces, [piece for piece, _, _ in pieces[1:]]
    length = array.shape[axis]
    half = length // 2
    one = flipped(array, 1)
    two = flipped(array, 2)
    if held:
        one, two = lax.optimization_barrier((one, two, *held))[:2]
    far_low = flipped(cut(one, 0, half, axis), 2)
    far_high = flipped(cut(two, half, length, axis), 1)
    return [
        (array, me, 0),
        (one, me ^ 1, 0),
        (two, me ^ 2, 0),
        (far_low, me ^ 3, 0),
        (far_high, me ^ 3, half),
    ], [one, two]


def rotary_tables(positions):
    frequency = 1.0 / ROPE_BASE ** (jnp.arange(0, HEAD, 2, dtype=F32) / HEAD)
    angles = positions.astype(F32)[:, None] * frequency[None, :]
    cosines, sines = jnp.cos(angles), jnp.sin(angles)
    return (
        jnp.concatenate([cosines] * 4, axis=1),
        jnp.concatenate([-sines, sines] * 2, axis=1),
    )


def norm_back(grad_in, values, scale_rows, scale_gain):
    shaped = grad_in * scale_gain
    grad_values = scale_rows * shaped - values * scale_rows**3 * jnp.mean(
        shaped * values, axis=-1, keepdims=True
    )
    return (grad_values, jnp.sum(grad_in * values * scale_rows, axis=0))


def dot_nt(left, right):
    return lax.dot_general(left, right, (((1,), (1,)), ((), ())), preferred_element_type=F32)


def dot_nn(left, right):
    return jnp.dot(left, right, preferred_element_type=F32)


def dot_tn(left, right):
    return lax.dot_general(left, right, (((0,), (0,)), ((), ())), preferred_element_type=F32)


def fill_weights(ref, gate_up, down):
    parts, _, depth, columns = ref.shape
    width = columns // 3
    for index in range(parts):
        half, place = divmod(index, parts // 2)
        span = slice(place * depth, (place + 1) * depth)
        gate_up[span, 2 * half * width : 2 * (half + 1) * width] = ref[index, 0, :, : 2 * width]
        down[span, half * width : (half + 1) * width] = ref[index, 0, :, 2 * width :]


def column_of(table, index):
    lane = lax.broadcasted_iota(jnp.int32, table.shape, 1)
    return jnp.sum(jnp.where(lane == index, table, 0.0), axis=1, keepdims=True)


def split_gate_up(raw, width):
    gate = jnp.concatenate([raw[:, :width], raw[:, 2 * width : 3 * width]], axis=1)
    up = jnp.concatenate([raw[:, width : 2 * width], raw[:, 3 * width :]], axis=1)
    return gate, up


def join_gate_up(gate, up, width):
    return jnp.concatenate(
        [gate[:, :width], up[:, :width], gate[:, width:], up[:, width:]], axis=1
    )


def moe_forward(rows, gates, weights):
    total, model = rows.shape
    parts, experts, depth, columns = weights.shape
    width = columns // 3
    tile = math.gcd(ROWS, total)

    def body(rows_ref, gates_ref, weights_ref, out_ref, raw_ref, gate_up, down, sums):
        expert = pl.program_id(0)
        fill_weights(weights_ref, gate_up, down)

        def step(index, carry):
            span = pl.ds(pl.multiple_of(index * tile, tile), tile)
            raw = dot_nn(rows_ref[span, :], gate_up[...])
            raw_ref[0, span, :] = raw.astype(BF16)
            gate, up = split_gate_up(raw, width)
            weight = column_of(gates_ref[span, :], expert)
            act = (gate * jax.nn.sigmoid(gate) * up * weight).astype(BF16)
            part = dot_nt(act, down[...])

            @pl.when(expert == 0)
            def _():
                sums[span, :] = part

            @pl.when(expert > 0)
            def _():
                sums[span, :] += part

            @pl.when(expert == experts - 1)
            def _():
                out_ref[span, :] = sums[span, :].astype(BF16)

            return carry

        lax.fori_loop(0, total // tile, step, 0)

    whole = lambda e: (0, 0)
    per_expert = lambda e: (e, 0, 0)
    once = pl.Buffered(1)
    return pl.pallas_call(
        body,
        grid_spec=pltpu.PrefetchScalarGridSpec(
            num_scalar_prefetch=0,
            grid=(experts,),
            in_specs=[
                pl.BlockSpec((total, model), whole, pipeline_mode=once),
                pl.BlockSpec((total, LANES), whole, pipeline_mode=once),
            ]
            + [pl.BlockSpec((parts, 1, depth, columns), lambda e: (0, e, 0, 0))],
            out_specs=[
                pl.BlockSpec((total, model), whole),
                pl.BlockSpec((1, total, 4 * width), per_expert),
            ],
            scratch_shapes=[
                pltpu.VMEM((model, 4 * width), BF16),
                pltpu.VMEM((model, 2 * width), BF16),
                pltpu.VMEM((total, model), F32),
            ],
        ),
        out_shape=[
            jax.ShapeDtypeStruct((total, model), BF16),
            jax.ShapeDtypeStruct((experts, total, 4 * width), BF16),
        ],
        compiler_params=pltpu.CompilerParams(vmem_limit_bytes=VMEM_LIMIT),
        cost_estimate=lasting(40),
        name="moe_forward",
    )(rows, gates, weights)


def moe_backward_rows(grads, gates, raws, weights):
    total, model = grads.shape
    parts, experts, depth, columns = weights.shape
    width = columns // 3
    tile = math.gcd(ROWS, total)

    def body(
        grads_ref,
        gates_ref,
        raw_ref,
        weights_ref,
        out_ref,
        d_raw_ref,
        act_ref,
        gate_up,
        down,
        sums,
        scores,
    ):
        expert = pl.program_id(0)
        fill_weights(weights_ref, gate_up, down)

        def step(index, carry):
            span = pl.ds(pl.multiple_of(index * tile, tile), tile)
            weight = column_of(gates_ref[span, :], expert)
            gate, up = split_gate_up(raw_ref[0, span, :].astype(F32), width)
            back = dot_nn(grads_ref[span, :], down[...])
            sigmoid = jax.nn.sigmoid(gate)
            swish = gate * sigmoid
            act = swish * up
            score = jnp.sum(back * act, axis=1, keepdims=True)
            act_ref[0, span, :] = (act * weight).astype(BF16)
            d_act = back * weight
            d_gate = d_act * up * sigmoid * (1.0 + gate * (1.0 - sigmoid))
            d_raw = join_gate_up(d_gate, d_act * swish, width).astype(BF16)
            d_raw_ref[0, span, :] = d_raw
            part = dot_nt(d_raw, gate_up[...])
            lane = lax.broadcasted_iota(jnp.int32, (tile, LANES), 1)

            @pl.when(expert == 0)
            def _():
                sums[span, :] = part
                scores[span, :] = jnp.where(lane == 0, score, 0.0)

            @pl.when(expert > 0)
            def _():
                sums[span, :] += part
                scores[span, :] = jnp.where(lane == expert, score, scores[span, :])

            @pl.when(expert == experts - 1)
            def _():
                out_ref[span, :model] = sums[span, :].astype(BF16)
                whole_scores = scores[span, :]
                high = whole_scores.astype(BF16).astype(F32)
                out_ref[span, model:] = jnp.where(
                    lane < HEAD, high, pltpu.roll(whole_scores - high, HEAD, 1)
                ).astype(BF16)

            return carry

        lax.fori_loop(0, total // tile, step, 0)

    whole = lambda e: (0, 0)
    per_expert = lambda e: (e, 0, 0)
    once = pl.Buffered(1)
    return pl.pallas_call(
        body,
        grid_spec=pltpu.PrefetchScalarGridSpec(
            num_scalar_prefetch=0,
            grid=(experts,),
            in_specs=[
                pl.BlockSpec((total, model), whole, pipeline_mode=once),
                pl.BlockSpec((total, LANES), whole, pipeline_mode=once),
                pl.BlockSpec((1, total, 4 * width), per_expert),
            ]
            + [pl.BlockSpec((parts, 1, depth, columns), lambda e: (0, e, 0, 0))],
            out_specs=[
                pl.BlockSpec((total, model + LANES), whole),
                pl.BlockSpec((1, total, 4 * width), per_expert),
                pl.BlockSpec((1, total, 2 * width), per_expert),
            ],
            scratch_shapes=[
                pltpu.VMEM((model, 4 * width), BF16),
                pltpu.VMEM((model, 2 * width), BF16),
                pltpu.VMEM((total, model), F32),
                pltpu.VMEM((total, LANES), F32),
            ],
        ),
        out_shape=[
            jax.ShapeDtypeStruct((total, model + LANES), BF16),
            jax.ShapeDtypeStruct((experts, total, 4 * width), BF16),
            jax.ShapeDtypeStruct((experts, total, 2 * width), BF16),
        ],
        compiler_params=pltpu.CompilerParams(vmem_limit_bytes=VMEM_LIMIT),
        cost_estimate=lasting(48),
        name="moe_backward_rows",
    )(grads, gates, raws, weights)


def moe_backward_weights(rows, grads, d_raws, acts, parts):
    total, model = rows.shape
    experts = d_raws.shape[0]
    width = d_raws.shape[2] // 4
    shards = parts // 2
    depth = model // shards

    def body(rows_ref, grads_ref, d_raw_ref, act_ref, out_ref, rows_t, grads_t):
        @pl.when(pl.program_id(0) == 0)
        def _():
            for start in range(0, model, TILE):
                rows_t[start : start + TILE, :] = rows_ref[:, start : start + TILE].T
                grads_t[start : start + TILE, :] = grads_ref[:, start : start + TILE].T

        for place in range(shards):
            span = slice(place * depth, (place + 1) * depth)
            gate_up = dot_nn(rows_t[span, :], d_raw_ref[0]).astype(BF16)
            down = dot_nn(grads_t[span, :], act_ref[0]).astype(BF16)
            for half in range(2):
                index = half * shards + place
                out_ref[index, 0, :, : 2 * width] = gate_up[
                    :, 2 * half * width : 2 * (half + 1) * width
                ]
                out_ref[index, 0, :, 2 * width :] = down[:, half * width : (half + 1) * width]

    whole = lambda e: (0, 0)
    per_expert = lambda e: (e, 0, 0)
    once = pl.Buffered(1)
    return pl.pallas_call(
        body,
        grid_spec=pltpu.PrefetchScalarGridSpec(
            num_scalar_prefetch=0,
            grid=(experts,),
            in_specs=[
                pl.BlockSpec((total, model), whole, pipeline_mode=once),
                pl.BlockSpec((total, model), whole, pipeline_mode=once),
                pl.BlockSpec((1, total, 4 * width), per_expert),
                pl.BlockSpec((1, total, 2 * width), per_expert),
            ],
            out_specs=pl.BlockSpec((parts, 1, depth, 3 * width), lambda e: (0, e, 0, 0)),
            scratch_shapes=[
                pltpu.VMEM((model, total), BF16),
                pltpu.VMEM((model, total), BF16),
            ],
        ),
        out_shape=jax.ShapeDtypeStruct((parts, experts, depth, 3 * width), BF16),
        compiler_params=pltpu.CompilerParams(vmem_limit_bytes=VMEM_LIMIT),
        cost_estimate=lasting(34),
        name="moe_backward_weights",
    )(rows, grads, d_raws, acts)


def expert_outputs(mine, other, core):
    experts, depth, columns = mine.shape
    width = columns // 3

    def body(core_ref, mine_ref, other_ref, gate_ref, up_ref, down_ref):
        is_first = core_ref[0] == 0
        own, received = mine_ref[0].astype(F32), other_ref[0].astype(F32)
        low = jnp.where(is_first, own, received)
        high = jnp.where(is_first, received, own)
        for index, half in enumerate((low, high)):
            span = slice(index * width, (index + 1) * width)
            gate_ref[0, :, span] = half[:, :width]
            up_ref[0, :, span] = half[:, width : 2 * width]
            down_ref[0, span, :] = half[:, 2 * width :].T

    block = lambda e, *_: (e, 0, 0)
    return pl.pallas_call(
        body,
        grid_spec=pltpu.PrefetchScalarGridSpec(
            num_scalar_prefetch=1,
            grid=(experts,),
            in_specs=[pl.BlockSpec((1, depth, columns), block)] * 2,
            out_specs=[
                pl.BlockSpec((1, depth, 2 * width), block),
                pl.BlockSpec((1, depth, 2 * width), block),
                pl.BlockSpec((1, 2 * width, depth), block),
            ],
        ),
        out_shape=[
            jax.ShapeDtypeStruct((experts, depth, 2 * width), F32),
            jax.ShapeDtypeStruct((experts, depth, 2 * width), F32),
            jax.ShapeDtypeStruct((experts, 2 * width, depth), F32),
        ],
        compiler_params=pltpu.CompilerParams(vmem_limit_bytes=VMEM_LIMIT),
        cost_estimate=lasting(6),
        name="expert_outputs",
    )(jnp.reshape(core, (1,)).astype(jnp.int32), mine, other)


def line_up(pieces, owners, planes_of, shards):
    arrays = [piece for piece, _, _ in pieces]
    slots, rows, width = arrays[0].shape
    copies = slots * shards
    if rows % 16:
        result = jnp.zeros((slots, shards, rows, width), BF16)
        for place, (array, _, start) in enumerate(pieces):
            for slot in range(array.shape[0]):
                result = lax.dynamic_update_slice(
                    result,
                    array[slot][None, None],
                    (planes_of[start + slot], owners[place], 0, 0),
                )
        return result.reshape(copies * rows, width)

    def body(owner_ref, plane_ref, *refs):
        out_ref, sems = refs[len(arrays) :]
        started = []
        for place, (array, _, start) in enumerate(pieces):
            for slot in range(array.shape[0]):
                index = plane_ref[start + slot] * shards + owner_ref[place]
                started.append(
                    pltpu.make_async_copy(
                        refs[place].at[slot],
                        out_ref.at[pl.ds(pl.multiple_of(index * rows, 16), rows), :],
                        sems.at[len(started)],
                    )
                )
                started[-1].start()
        for copy in started:
            copy.wait()

    return pl.pallas_call(
        body,
        grid_spec=pltpu.PrefetchScalarGridSpec(
            num_scalar_prefetch=2,
            grid=(1,),
            in_specs=[pl.BlockSpec(memory_space=pl.ANY)] * len(arrays),
            out_specs=pl.BlockSpec((copies * rows, width), lambda i, *_: (0, 0)),
            scratch_shapes=[pltpu.SemaphoreType.DMA((copies * 2,))],
        ),
        out_shape=jax.ShapeDtypeStruct((copies * rows, width), BF16),
        compiler_params=pltpu.CompilerParams(vmem_limit_bytes=VMEM_LIMIT),
        cost_estimate=lasting(4),
        name="line_up",
    )(owners, planes_of, *arrays)


def turned(values, cosines, sines):
    lane = lax.broadcasted_iota(jnp.int32, cosines.shape, 1)
    low = lane % HEAD < HEAD // 2
    parts = []
    for start in range(0, values.shape[1], LANES):
        block = values[:, start : start + LANES]
        partner = jnp.where(
            low,
            pltpu.roll(block, LANES - HEAD // 2, 1),
            pltpu.roll(block, HEAD // 2, 1),
        )
        parts.append(block * cosines + partner * sines)
    return jnp.concatenate(parts, axis=1)


def pair_columns(width):
    return [start for start in range(0, width, 2 * LANES)]


def half_specs(halves, columns):
    return [
        pl.BlockSpec((1, array.shape[1], columns), lambda i, *_, place=place: (place, 0, 0))
        for array, place in halves
    ]


def qkv_forward(stream, gain, halves, cosines, sines, columns):
    rows, model = stream.shape
    queries, kv = columns

    def body(stream_ref, gain_ref, mine_ref, other_ref, cos_ref, sin_ref, q_ref, kv_ref, n_ref):
        values = stream_ref[...]
        scale = lax.rsqrt(jnp.mean(values * values, axis=1, keepdims=True) + EPSILON)
        n_ref[...] = (values * scale * gain_ref[...]).astype(BF16)
        cos, sin = cos_ref[...], sin_ref[...]
        for index, ref in enumerate((mine_ref, other_ref)):
            raw = dot_nn(n_ref[...], ref[0])
            q_ref[:, index * queries : (index + 1) * queries] = turned(
                raw[:, :queries], cos, sin
            ).astype(BF16)
            for start in pair_columns(kv):
                place = index * kv + start
                keys = raw[:, queries + start : queries + start + LANES]
                kv_ref[:, place : place + LANES] = turned(keys, cos, sin).astype(BF16)
                kv_ref[:, place + LANES : place + 2 * LANES] = raw[
                    :, queries + start + LANES : queries + start + 2 * LANES
                ].astype(BF16)

    whole = lambda i: (0, 0)
    return pl.pallas_call(
        body,
        grid=(1,),
        in_specs=[
            pl.BlockSpec((rows, model), whole),
            pl.BlockSpec((1, model), whole),
            *half_specs(halves, queries + kv),
            pl.BlockSpec((rows, LANES), whole),
            pl.BlockSpec((rows, LANES), whole),
        ],
        out_specs=[
            pl.BlockSpec((rows, 2 * queries), whole),
            pl.BlockSpec((rows, 2 * kv), whole),
            pl.BlockSpec((rows, model), whole),
        ],
        out_shape=[
            jax.ShapeDtypeStruct((rows, 2 * queries), BF16),
            jax.ShapeDtypeStruct((rows, 2 * kv), BF16),
            jax.ShapeDtypeStruct((rows, model), BF16),
        ],
        compiler_params=pltpu.CompilerParams(vmem_limit_bytes=VMEM_LIMIT),
        cost_estimate=lasting(7),
        name="qkv_forward",
    )(stream, gain, *[array for array, _ in halves], cosines, sines)


def branch_backward(backs, places, experts, gates, side, middle, gain, grad_out, halves, flip):
    rows, model = middle.shape
    count = len(backs)
    half_width = halves[0].shape[1]

    def body(places_ref, flip_ref, *refs):
        slots = refs[:count]
        gates_ref, side_ref, middle_ref, gain_ref, out_grad_ref, one_ref, two_ref = refs[
            count : count + 7
        ]
        d_middle_ref, branch_ref, attended_ref, high_ref, low_ref, d_gain_ref = refs[count + 7 :]
        lane = lax.broadcasted_iota(jnp.int32, (LANES, LANES), 0) % HEAD
        column = lax.broadcasted_iota(jnp.int32, (LANES, LANES), 1)
        d_hidden = None
        d_gates = None
        for index, slot in enumerate(slots):
            placing = (lane < experts) & (column == lane + 2 + places_ref[index] * experts)
            part = dot_nn(slot[:, model:], placing.astype(F32).astype(BF16))
            values = slot[:, :model].astype(F32)
            d_hidden = values if d_hidden is None else d_hidden + values
            d_gates = part if d_gates is None else d_gates + part
        gate_table = gates_ref[...]
        share = jnp.sum(gate_table * d_gates, axis=1, keepdims=True)
        d_logits = gate_table * (d_gates - share)
        high = d_logits.astype(BF16)
        low = (d_logits - high.astype(F32)).astype(BF16)
        high_ref[...] = high
        low_ref[...] = low
        d_hidden = d_hidden + dot_nt(high, side_ref[...]) + dot_nt(low, side_ref[...])
        values = middle_ref[...]
        scale = lax.rsqrt(jnp.mean(values * values, axis=1, keepdims=True) + EPSILON)
        d_gain = jnp.sum(d_hidden * values * scale, axis=0, keepdims=True)
        d_gain_ref[...] = jnp.broadcast_to(d_gain, (8, model))
        shaped = d_hidden * gain_ref[...]
        mean = jnp.mean(shaped * values, axis=1, keepdims=True)
        d_middle = (
            out_grad_ref[...].astype(F32) + scale * shaped - values * (scale * scale * scale * mean)
        )
        d_middle_ref[...] = d_middle
        branch = d_middle.astype(BF16)
        branch_ref[...] = branch
        flipped_order = flip_ref[0] == 1
        first_half, second_half = branch[:, :half_width], branch[:, half_width:]
        attended = dot_nt(
            jnp.where(flipped_order, second_half, first_half), one_ref[...]
        ) + dot_nt(jnp.where(flipped_order, first_half, second_half), two_ref[...])
        width = attended.shape[1] // 2
        left, right = attended[:, :width], attended[:, width:]
        attended_ref[:, :width] = jnp.where(flipped_order, right, left).astype(BF16)
        attended_ref[:, width:] = jnp.where(flipped_order, left, right).astype(BF16)

    arrays = [*backs, gates, side, middle, gain, grad_out, *halves]
    whole = lambda i, *_: (0, 0)
    outs = [
        ((rows, model), F32),
        ((rows, model), BF16),
        ((rows, halves[0].shape[0]), BF16),
        ((rows, LANES), BF16),
        ((rows, LANES), BF16),
        ((8, model), F32),
    ]
    return pl.pallas_call(
        body,
        grid_spec=pltpu.PrefetchScalarGridSpec(
            num_scalar_prefetch=2,
            grid=(1,),
            in_specs=[pl.BlockSpec(array.shape, whole) for array in arrays],
            out_specs=[pl.BlockSpec(shape, whole) for shape, _ in outs],
        ),
        out_shape=[jax.ShapeDtypeStruct(shape, dtype) for shape, dtype in outs],
        compiler_params=pltpu.CompilerParams(vmem_limit_bytes=VMEM_LIMIT),
        cost_estimate=lasting(12),
        name="branch_backward",
    )(places, flip, *arrays)


def qkv_backward(
    normed, d_queries, d_kv_slots, halves, cosines, sines, columns, stream, side, flip, extra, grid
):
    rows, model = normed.shape
    queries, kv = columns
    qkv = queries + kv
    count = len(d_kv_slots)
    shards, planes = grid
    depth = model // (shards * planes)
    more = extra[1].shape[1] if extra else 0

    def body(flip_ref, n_ref, dq_ref, *refs):
        slots = refs[:count]
        mine_ref, other_ref, cos_ref, sin_ref, stream_ref = refs[count : count + 5]
        hidden_ref, high_ref, low_ref, gain_two_ref = refs[count + 5 : count + 9]
        extra_refs = refs[count + 9 : count + 9 + len(extra)]
        out_ref, grad_ref, n_t, grads = refs[count + 9 + len(extra) :]
        flipped_order = flip_ref[0]
        cos, sin = cos_ref[...], -sin_ref[...]

        def write(index, first_column, values):
            last_column = first_column + values.shape[1]
            grads[:, : values.shape[1]] = values
            for plane in range(planes):
                for shard in range(shards):
                    start = (plane * shards + shard) * depth
                    grad_ref[index * shards + shard, plane, :, first_column:last_column] = grads[
                        start : start + depth, : values.shape[1]
                    ].astype(BF16)

        n_t[...] = n_ref[...].T
        for index, ref in ((0, mine_ref), (1, other_ref)):
            span = slice(index * kv, (index + 1) * kv)
            d_kv = slots[0][:, span].astype(F32)
            for slot in slots[1:]:
                d_kv = d_kv + slot[:, span].astype(F32)
            parts = [dq_ref[:, index * queries : (index + 1) * queries]]
            for start in pair_columns(kv):
                parts.append(turned(d_kv[:, start : start + LANES], cos, sin).astype(BF16))
                parts.append(d_kv[:, start + LANES : start + 2 * LANES].astype(BF16))
            d_raw = jnp.concatenate(parts, axis=1)
            back = dot_nt(d_raw, ref[0])
            if index == 0:
                out_ref[...] = back
            else:
                out_ref[...] += back
            place = flipped_order if index == 0 else 1 - flipped_order
            write(place, 0, dot_nn(n_t[...], d_raw))
        values = stream_ref[...]
        scale = lax.rsqrt(jnp.mean(values * values, axis=1, keepdims=True) + EPSILON)
        gain = jnp.sum(out_ref[...] * values * scale, axis=0, keepdims=True)
        gain = jnp.broadcast_to(gain, (LANES, model)).T
        gain_two = jnp.broadcast_to(gain_two_ref[:1, :], (LANES, model)).T
        n_t[...] = hidden_ref[...].T
        routing = dot_nn(n_t[...], high_ref[...]) + dot_nn(n_t[...], low_ref[...])
        lane = lax.broadcasted_iota(jnp.int32, (model, LANES), 1)
        whole_side = jnp.where(lane == 0, gain, jnp.where(lane == 1, gain_two, routing))
        write(0, qkv, whole_side)
        write(1, qkv, jnp.zeros_like(whole_side))
        if extra:
            n_t[...] = extra_refs[0][...].T
            for index in range(2):
                write(index, qkv + LANES, dot_nn(n_t[...], extra_refs[index + 1][...]))

    whole = lambda i, *_: (0, 0)
    return pl.pallas_call(
        body,
        grid_spec=pltpu.PrefetchScalarGridSpec(
            num_scalar_prefetch=1,
            grid=(1,),
        in_specs=[
            pl.BlockSpec((rows, model), whole),
            pl.BlockSpec((rows, 2 * queries), whole),
        ]
        + [pl.BlockSpec((rows, 2 * kv), whole)] * count
        + half_specs(halves, qkv)
        + [
            pl.BlockSpec((rows, LANES), whole),
            pl.BlockSpec((rows, LANES), whole),
            pl.BlockSpec((rows, model), whole),
        ]
        + [pl.BlockSpec(array.shape, whole) for array in (*side, *extra)],
        out_specs=[
            pl.BlockSpec((rows, model), whole),
            pl.BlockSpec(
                (2 * shards, planes, depth, qkv + LANES + more), lambda i, *_: (0, 0, 0, 0)
            ),
        ],
        scratch_shapes=[pltpu.VMEM((model, rows), BF16), pltpu.VMEM((model, qkv), F32)],
        ),
        out_shape=[
            jax.ShapeDtypeStruct((rows, model), F32),
            jax.ShapeDtypeStruct((2 * shards, planes, depth, qkv + LANES + more), BF16),
        ],
        compiler_params=pltpu.CompilerParams(vmem_limit_bytes=VMEM_LIMIT),
        cost_estimate=lasting(14),
        name="qkv_backward",
    )(
        flip,
        normed,
        d_queries,
        *d_kv_slots,
        *[array for array, _ in halves],
        cosines,
        sines,
        stream,
        *side,
        *extra,
    )


def head_sides(block):
    lane = lax.broadcasted_iota(jnp.int32, block.shape, 1)
    low = lane < HEAD
    crossed = jnp.concatenate([block[:, HEAD:], block[:, :HEAD]], axis=1)
    nothing = jnp.zeros_like(block)
    return [
        [jnp.where(low, block, nothing), jnp.where(low, nothing, crossed)],
        [jnp.where(low, crossed, nothing), jnp.where(low, nothing, block)],
    ]


def fill_bias(bias, owner_ref, seg_all_ref, seg_ref, rows, count):
    own = owner_ref[0] * rows + lax.broadcasted_iota(jnp.int32, (rows, rows), 1)
    for slot in range(count):
        span = slice(slot * rows, (slot + 1) * rows)
        place = owner_ref[slot] * rows + lax.broadcasted_iota(jnp.int32, (rows, rows), 0)
        allowed = (place <= own) & (seg_all_ref[span, :1] == seg_ref[:1, :])
        bias[span, :] = jnp.where(allowed, 0.0, NEGATIVE)


def attention_specs(rows, count, group):
    whole = lambda p, *_: (0, 0)
    return (
        [
            pl.BlockSpec((count * rows, LANES), whole),
            pl.BlockSpec((8, rows), whole),
            pl.BlockSpec((rows, 2 * group * HEAD), lambda p, *_: (0, p)),
        ]
        + [pl.BlockSpec((rows, 2 * LANES), lambda p, *_: (0, p))] * count
    )


def attention_forward(queries, kv_slots, owners, seg_all, seg_own):
    rows, width = queries.shape
    count = len(kv_slots)
    group = HEADS // KV_HEADS
    pairs = KV_HEADS // 2
    heads = 2 * group
    total = count * rows
    scale = 1.0 / math.sqrt(HEAD)

    def body(owner_ref, seg_all_ref, seg_ref, q_ref, *refs):
        slots = refs[:count]
        out_ref, stat_ref, bias = refs[count:]

        @pl.when(pl.program_id(0) == 0)
        def _():
            fill_bias(bias, owner_ref, seg_all_ref, seg_ref, rows, count)

        keys = head_sides(jnp.concatenate([ref[:, :LANES] for ref in slots], axis=0))
        values = head_sides(jnp.concatenate([ref[:, LANES:] for ref in slots], axis=0))
        values = [[side.T for side in sides] for sides in values]
        scaled = (q_ref[...].astype(F32) * scale).astype(BF16)
        stats = []
        for block in range(group):
            out = None
            for side in range(2):
                head = 2 * block + side
                kv = head // group
                scores = (
                    dot_nt(keys[kv][side], scaled[:, block * LANES : (block + 1) * LANES])
                    + bias[...]
                )
                top = jnp.max(scores, axis=0, keepdims=True)
                exponent = jnp.exp(scores - top)
                total_of = jnp.sum(exponent, axis=0, keepdims=True)
                probs = (exponent * (1.0 / total_of)).astype(BF16)
                part = dot_nn(values[kv][side], probs)
                out = part if out is None else out + part
                stats.append(top + jnp.log(total_of))
            out_ref[:, block * LANES : (block + 1) * LANES] = out.T.astype(BF16)
        stat_ref[0, :heads, :] = jnp.concatenate(stats, axis=0)

    return pl.pallas_call(
        body,
        grid_spec=pltpu.PrefetchScalarGridSpec(
            num_scalar_prefetch=1,
            grid=(pairs,),
            in_specs=attention_specs(rows, count, group),
            out_specs=[
                pl.BlockSpec((rows, heads * HEAD), lambda p, *_: (0, p)),
                pl.BlockSpec((1, 8, rows), lambda p, *_: (p, 0, 0)),
            ],
            scratch_shapes=[pltpu.VMEM((total, rows), F32)],
        ),
        out_shape=[
            jax.ShapeDtypeStruct((rows, width), BF16),
            jax.ShapeDtypeStruct((pairs, 8, rows), F32),
        ],
        compiler_params=pltpu.CompilerParams(vmem_limit_bytes=VMEM_LIMIT),
        cost_estimate=lasting(17),
        name="attention_forward",
    )(owners, seg_all, seg_own, queries, *kv_slots)


def attention_backward(queries, kv_slots, owners, seg_all, seg_own, d_out, stats, cosines, sines):
    rows, width = queries.shape
    count = len(kv_slots)
    group = HEADS // KV_HEADS
    pairs = KV_HEADS // 2
    heads = 2 * group
    total = count * rows
    scale = 1.0 / math.sqrt(HEAD)

    def body(owner_ref, seg_all_ref, seg_ref, q_ref, *refs):
        slots = refs[:count]
        d_out_ref, stat_ref, cos_ref, sin_ref = refs[count : count + 4]
        d_q_ref = refs[count + 4]
        d_slots = refs[count + 5 : 2 * count + 5]
        bias, d_keys, d_values = refs[2 * count + 5 :]

        @pl.when(pl.program_id(0) == 0)
        def _():
            fill_bias(bias, owner_ref, seg_all_ref, seg_ref, rows, count)

        keys = head_sides(jnp.concatenate([ref[:, :LANES] for ref in slots], axis=0))
        values = head_sides(jnp.concatenate([ref[:, LANES:] for ref in slots], axis=0))
        keys_t = [[side.T for side in sides] for sides in keys]
        cos, sin = cos_ref[...], -sin_ref[...]
        for block in range(group):
            span = slice(block * LANES, (block + 1) * LANES)
            scaled = (q_ref[:, span].astype(F32) * scale).astype(BF16)
            d_block = d_out_ref[:, span]
            q_sides = head_sides(scaled)
            d_sides = head_sides(d_block)
            d_q = None
            for side in range(2):
                head = 2 * block + side
                kv = head // group
                scores = dot_nt(keys[kv][side], scaled) + bias[...]
                probs = jnp.exp(scores - stat_ref[0, head : head + 1, :])
                d_probs = dot_nt(values[kv][side], d_block)
                share = jnp.sum(probs * d_probs, axis=0, keepdims=True)
                d_scores = (probs * (d_probs - share)).astype(BF16)
                part = dot_nn(keys_t[kv][side], d_scores)
                d_q = part if d_q is None else d_q + part
                d_key = dot_nn(d_scores, q_sides[side][kv])
                d_value = dot_nn(probs.astype(BF16), d_sides[side][kv])
                if head == 0:
                    d_keys[...] = d_key
                    d_values[...] = d_value
                else:
                    d_keys[...] += d_key
                    d_values[...] += d_value
            d_q_ref[:, span] = turned(d_q.T * scale, cos, sin).astype(BF16)
        for slot in range(count):
            part = slice(slot * rows, (slot + 1) * rows)
            d_slots[slot][:, :LANES] = d_keys[part, :].astype(BF16)
            d_slots[slot][:, LANES:] = d_values[part, :].astype(BF16)

    whole = lambda p, *_: (0, 0)
    return pl.pallas_call(
        body,
        grid_spec=pltpu.PrefetchScalarGridSpec(
            num_scalar_prefetch=1,
            grid=(pairs,),
            in_specs=attention_specs(rows, count, group)
            + [
                pl.BlockSpec((rows, heads * HEAD), lambda p, *_: (0, p)),
                pl.BlockSpec((1, 8, rows), lambda p, *_: (p, 0, 0)),
                pl.BlockSpec((rows, LANES), whole),
                pl.BlockSpec((rows, LANES), whole),
            ],
            out_specs=[pl.BlockSpec((rows, heads * HEAD), lambda p, *_: (0, p))]
            + [pl.BlockSpec((rows, 2 * LANES), lambda p, *_: (0, p))] * count,
            scratch_shapes=[
                pltpu.VMEM((total, rows), F32),
                pltpu.VMEM((total, LANES), F32),
                pltpu.VMEM((total, LANES), F32),
            ],
        ),
        out_shape=[jax.ShapeDtypeStruct((rows, width), BF16)]
        + [jax.ShapeDtypeStruct((rows, 2 * KV_HEADS * HEAD), BF16)] * count,
        compiler_params=pltpu.CompilerParams(vmem_limit_bytes=VMEM_LIMIT),
        cost_estimate=lasting(27),
        name="attention_backward",
    )(owners, seg_all, seg_own, queries, *kv_slots, d_out, stats, cosines, sines)


def on_device(
    inputs,
    cotangent,
    segments,
    routes,
    attn_gain,
    w_query,
    w_key,
    w_value,
    w_output,
    ffn_gain,
    router,
    w_gate,
    w_up,
    w_down,
):
    core = lax.axis_index("section")
    shard = lax.axis_index("shard")
    plane = lax.axis_index("expert")
    shards = lax.axis_size("shard")
    planes = lax.axis_size("expert")
    span_rows, model = inputs.shape[2:]
    seq_rows = span_rows * shards
    gathered_rows = span_rows * planes
    local_experts = w_gate.shape[1]
    all_experts = local_experts * planes
    hidden = w_gate.shape[3]
    half_hidden = hidden // 2
    part_rows = w_query.shape[1]
    query_width = HEADS * HEAD
    kv_width = KV_HEADS * HEAD
    group_size = HEADS // KV_HEADS
    score_scale = 1.0 / math.sqrt(HEAD)
    first = core == 0

    def mine_of(array):
        return lax.dynamic_index_in_dim(array, core, 0, keepdims=False)

    def by_layer(own, received):
        return [jnp.where(first, own, received), jnp.where(first, received, own)]

    def halved(own_halves):
        kept = jnp.where(first, own_halves[0], own_halves[1])
        sent = jnp.where(first, own_halves[1], own_halves[0])
        return by_layer(kept, swap(sent))

    misc = jnp.concatenate(
        [
            attn_gain[0][:, None],
            ffn_gain[0][:, None],
            router[0],
            jnp.zeros((part_rows, LANES - 2 - all_experts), BF16),
        ],
        axis=1,
    )
    half_query = query_width // 2
    half_kv = kv_width // 2
    half_qkv = half_query + 2 * half_kv

    def head_half(index, side):
        return jnp.concatenate(
            [
                w_query[0][:, index * half_query : (index + 1) * half_query],
            ]
            + [
                array[0][:, start : start + LANES]
                for start in range(index * half_kv, (index + 1) * half_kv, LANES)
                for array in (w_key, w_value)
            ]
            + [side],
            axis=1,
        )

    output_half = model // 2
    qkv_mine = halved([head_half(0, misc), head_half(1, jnp.zeros_like(misc))])
    output_mine = halved([w_output[0][:, :output_half], w_output[0][:, output_half:]])

    plane_order = jnp.stack(
        [plane] + [partner("expert", k) for k in range(1, planes)]
    ).astype(jnp.int32)

    segment_local = mine_of(segments)[0]
    segment_all = jnp.concatenate(
        [slot[0] for slot in slots_of(segment_local[None], "shard")]
    )
    own_routes = routes[0, :, 0]
    route_rows = by_layer(
        lax.dynamic_index_in_dim(own_routes, core, 0, keepdims=False),
        swap(lax.dynamic_index_in_dim(own_routes, 1 - core, 0, keepdims=False)),
    )
    expert_ids = jnp.arange(all_experts, dtype=jnp.int32)
    chosen = jnp.stack(
        [
            jnp.any(rows[:, :, None] == expert_ids[None, None, :], axis=1).astype(BF16)
            for rows in route_rows
        ]
    )
    chosen_all = jnp.concatenate(slots_of(jnp.swapaxes(chosen, 1, 2), "expert"), axis=2)

    def dense_weights(lined, held=(), before=()):
        pieces, first_step = ring_gather(lined, 0, held)
        if before:
            last = lax.optimization_barrier((pieces[-1][0], *before))[0]
            pieces[-1] = (last, *pieces[-1][1:])
        owners = jnp.stack([owner for _, owner, _ in pieces]).astype(jnp.int32)
        mine = line_up(pieces, owners, plane_order, shards)
        return (mine, swap(mine)), first_step, [piece for piece, _, _ in pieces[-2:]]

    lined = jnp.stack(slots_of(qkv_mine[0], "expert"))
    first_qkv, ring_start, ring_end = dense_weights(lined, before=(chosen_all, segment_all))
    lined_output = jnp.stack(slots_of(after(output_mine[0], *ring_start), "expert"))
    own_gate, own_up, own_down, *_ = lax.optimization_barrier(
        (w_gate[0], w_up[0], w_down[0], *ring_start)
    )
    down_turned = jnp.swapaxes(own_down, 1, 2)

    def expert_half(start):
        stop = start + half_hidden
        return jnp.concatenate(
            [own_gate[:, :, start:stop], own_up[:, :, start:stop], down_turned[:, :, start:stop]],
            axis=2,
        )

    expert_mine = halved([expert_half(0), expert_half(half_hidden)])
    first_experts = lax.all_gather(
        after(expert_mine[0], *ring_end), ("section", "shard"), axis=0
    )
    second_pack = lax.all_gather(
        jnp.concatenate([qkv_mine[1], output_mine[1]], axis=1), "expert", axis=0
    )
    second_pack = lax.all_gather(second_pack, ("section", "shard"), axis=0)
    second_pack = (
        second_pack.reshape(2, shards, planes, part_rows, -1)
        .swapaxes(1, 2)
        .reshape(2, model, half_qkv + LANES + output_half)
    )
    second_experts = lax.all_gather(expert_mine[1], ("section", "shard"), axis=0)

    qkv_columns = half_qkv + LANES

    def natural(halves, relative):
        mine, other = halves
        if not relative:
            return jnp.concatenate([mine, other], axis=1)
        return jnp.concatenate(
            [jnp.where(first, mine, other), jnp.where(first, other, mine)], axis=1
        )

    def parted(array, relative):
        half = array.shape[1] // 2
        low, high = array[:, :half], array[:, half:]
        if not relative:
            return low, high
        return jnp.where(first, low, high), jnp.where(first, high, low)

    positions = shard * span_rows + jnp.arange(span_rows, dtype=jnp.int32)
    cosines, sines = rotary_tables(positions)
    key_owners = jnp.stack(
        [shard] + [partner("shard", k) for k in range(1, shards)]
    ).astype(jnp.int32)
    seg_all = jnp.broadcast_to(segment_all[:, None], (seq_rows, LANES))
    seg_own = jnp.broadcast_to(segment_local[None, :], (8, span_rows))
    chosen_all = jnp.swapaxes(chosen_all, 1, 2) > 0.5

    last = mine_of(cotangent)[0]

    def attend(stream, pair, side, relative):
        gain_one = side[:, 0].astype(F32)
        gain_two = side[:, 1].astype(F32)
        query_rot, kv_own, normed = qkv_forward(
            stream, gain_one[None], pair, cosines, sines, (half_query, 2 * half_kv)
        )
        kv_slots = slots_of(kv_own, "shard")
        attended, stats = attention_forward(query_rot, kv_slots, key_owners, seg_all, seg_own)
        kept = dict(
            stream=stream,
            normed=normed,
            query_rot=query_rot,
            kv_slots=kv_slots,
            stats=stats,
            gain_one=gain_one,
            gain_two=gain_two,
            router_full=side[:, 2 : 2 + all_experts],
            side=side,
            qkv=pair,
            relative=relative,
        )
        return attended, kept

    def gathered_rows_of(kept, attended, pair):
        relative = kept["relative"]
        attended = natural(
            (attended[:, : query_width // 2], attended[:, query_width // 2 :]), relative
        )
        middle = kept["stream"] + natural([dot_nn(attended, half) for half in pair], relative)
        scale_two = lax.rsqrt(jnp.mean(middle * middle, axis=-1, keepdims=True) + EPSILON)
        hidden_in = (middle * scale_two * kept["gain_two"]).astype(BF16)
        rows = jnp.concatenate(slots_of(hidden_in, "expert"), axis=0)
        kept.update(
            attended=attended, middle=middle, scale_two=scale_two, hidden_in=hidden_in, output=pair
        )
        return rows

    def mix(layer, kept, rows, experts):
        logits = jnp.where(chosen_all[layer], dot_nn(rows, kept["router_full"]), NEGATIVE)
        gates = jax.nn.softmax(logits, axis=-1)
        gates = jnp.where(chosen_all[layer], gates, 0.0)
        own_gates = lax.dynamic_slice_in_dim(gates, plane * local_experts, local_experts, axis=1)
        own_gates = jnp.pad(own_gates, ((0, 0), (0, LANES - local_experts)))
        partial, raws = moe_forward(rows, own_gates, experts)
        kept.update(
            rows=rows,
            gates=gates[:span_rows],
            own_gates=own_gates,
            raws=raws,
            experts=experts,
            partial=partial,
        )
        return partial

    def combine(kept, partial, *held):
        combined = after(partial[:span_rows], *held).astype(F32)
        for k in range(1, planes):
            back = crossed_back(partial[k * span_rows : (k + 1) * span_rows], "expert", k)
            combined = combined + back.astype(F32)
        return (kept["middle"] + combined).astype(BF16)

    def backward(layer, kept, grad_rows, earlier):
        grad_low = grad_rows[:span_rows]
        relative = kept["relative"]
        d_rows, d_raws, acts = moe_backward_rows(
            grad_rows, kept["own_gates"], kept["raws"], kept["experts"]
        )
        expert_grads = moe_backward_weights(kept["rows"], grad_rows, d_raws, acts, 2 * shards)
        backs = [after(d_rows[:span_rows], expert_grads)]
        for k in range(1, planes):
            backs.append(crossed_back(d_rows[k * span_rows : (k + 1) * span_rows], "expert", k))
        flip = jnp.reshape(core if relative else 0, (1,)).astype(jnp.int32)
        places = jnp.stack(
            [plane] + [partner("expert", k, True) for k in range(1, planes)]
        ).astype(jnp.int32)
        d_middle, d_branch, d_attended, logits_high, logits_low, d_gain_two = branch_backward(
            backs,
            places,
            local_experts,
            jnp.pad(kept["gates"], ((0, 0), (2, LANES - 2 - all_experts))),
            kept["side"],
            kept["middle"],
            kept["gain_two"][None],
            grad_low,
            kept["output"],
            flip,
        )
        sent_grads = after(expert_grads, d_branch)
        if earlier is not None:
            sent_grads, earlier = lax.optimization_barrier((sent_grads, earlier))
        scattered = lax.psum_scatter(sent_grads, ("section", "shard"), scatter_dimension=0)
        branch_halves = [d_branch[:, :output_half], d_branch[:, output_half:]]
        grad_output = None
        if layer == 0:
            grad_output = jnp.stack(
                [dot_tn(kept["attended"], part).astype(BF16) for part in branch_halves]
            )
            grad_output = (
                grad_output.reshape(2, planes, shards, part_rows, output_half)
                .swapaxes(1, 2)
                .reshape(2 * shards, planes, part_rows, output_half)
            )
        d_query_raw, *d_slots = attention_backward(
            kept["query_rot"],
            kept["kv_slots"],
            key_owners,
            seg_all,
            seg_own,
            d_attended,
            kept["stats"],
            cosines,
            sines,
        )
        result = None
        if layer == 1:
            partial = after(kept["partial"], d_branch)
            result = combine(kept, partial, d_slots[0])
            d_query_raw, result = lax.optimization_barrier((d_query_raw, result))
        else:
            grad_output = sum_over("expert", grad_output)
        d_kv_slots = [d_slots[0]] + [
            crossed_back(d_slots[k], "shard", k) for k in range(1, shards)
        ]
        stream = kept["stream"]
        d_normed, packed = qkv_backward(
            kept["normed"],
            d_query_raw,
            d_kv_slots,
            kept["qkv"],
            cosines,
            sines,
            (half_query, 2 * half_kv),
            stream,
            (kept["hidden_in"], logits_high, logits_low, d_gain_two),
            flip,
            [kept["attended"], *branch_halves] if layer == 1 else [],
            (shards, planes),
        )
        scale_one = lax.rsqrt(jnp.mean(stream * stream, axis=-1, keepdims=True) + EPSILON)
        d_stream, _ = norm_back(d_normed, stream, scale_one, kept["gain_one"])
        d_stream = (d_middle + d_stream).astype(BF16)
        return d_stream, scattered, packed, grad_output, earlier, result

    homes = {"shard": (shard, shards, 0), "expert": (plane, planes, 1)}

    def place_of(axis, k):
        return partner(axis, k, True) if k else homes[axis][0]

    def sum_over(axis, array):
        size = (shards, *array.shape[1:])
        kept = lax.dynamic_slice(array, (core * shards, 0, 0, 0), size)
        received = swap(lax.dynamic_slice(array, ((1 - core) * shards, 0, 0, 0), size))
        _, count, dim = homes[axis]

        def chunk(k):
            place = place_of(axis, k)
            return lax.dynamic_index_in_dim(kept, place, dim, keepdims=False).astype(
                F32
            ) + lax.dynamic_index_in_dim(received, place, dim, keepdims=False).astype(F32)

        total = chunk(0)
        for k in range(1, count):
            total = total + crossed_back(chunk(k).astype(BF16), axis, k).astype(F32)
        return total

    def sum_rest(axis, total, *held):
        result = lax.dynamic_index_in_dim(total, place_of(axis, 0), 0, keepdims=False)
        if held:
            result = after(result, *held)
        for k in range(1, homes[axis][1]):
            part = lax.dynamic_index_in_dim(total, place_of(axis, k), 0, keepdims=False)
            result = result + crossed_back(part.astype(BF16), axis, k).astype(F32)
        return result.astype(BF16)

    def exchanged(halves):
        kept = jnp.where(first, halves[0], halves[1])
        sent = jnp.where(first, halves[1], halves[0])
        return kept, swap(sent)

    start = mine_of(inputs)[0]
    side = jnp.where(
        first, first_qkv[0][:, half_qkv:qkv_columns], first_qkv[1][:, half_qkv:qkv_columns]
    )
    attended, kept_one = attend(
        start.astype(F32), [(half[None], 0) for half in first_qkv], side, True
    )
    first_output, _, _ = dense_weights(
        after(lined_output, *ring_end), held=(kept_one["query_rot"],)
    )
    rows = gathered_rows_of(kept_one, attended, first_output)
    result_one = combine(kept_one, mix(0, kept_one, rows, first_experts))

    last_rows = jnp.concatenate(slots_of(after(last, result_one), "expert"), axis=0)
    attended, kept_two = attend(
        result_one.astype(F32),
        [(second_pack, 0), (second_pack, 1)],
        second_pack[0, :, half_qkv:qkv_columns],
        False,
    )
    attended = after(attended, last_rows)
    rows = gathered_rows_of(
        kept_two, attended, [second_pack[half, :, qkv_columns:] for half in range(2)]
    )
    partial = mix(1, kept_two, rows, second_experts)
    grad_mid, scattered_two, packed_two, _, _, result_two = backward(
        1, kept_two, last_rows, None
    )
    mid_rows = jnp.concatenate(slots_of(grad_mid, "expert"), axis=0)
    packed_two, scattered_two, _ = lax.optimization_barrier((packed_two, scattered_two, mid_rows))
    pack_two = lax.psum_scatter(packed_two, ("section", "shard"), scatter_dimension=0)
    grad_start, scattered_one, packed_one, output_one, pack_two, _ = backward(
        0, kept_one, mid_rows, pack_two
    )
    qkv_one = sum_over("shard", packed_one)
    qkv_one, output_one = lax.optimization_barrier((qkv_one, output_one))
    pack_two, scattered_one, _ = lax.optimization_barrier((pack_two, scattered_one, qkv_one))
    pack_two = lax.psum_scatter(pack_two, "expert", scatter_dimension=0)
    expert_mine_half, expert_other_half = exchanged([scattered_one, scattered_two])
    grad_gate, grad_up, grad_down = expert_outputs(expert_mine_half, expert_other_half, core)
    qkv_one = sum_rest("expert", qkv_one, grad_gate)
    output_one = sum_rest("shard", output_one)

    def placed(by_layers):
        own = jnp.where(first, by_layers[0], by_layers[1])
        sent = jnp.where(first, by_layers[1], by_layers[0])
        return jnp.stack(by_layer(own, swap(sent)))

    layer_local = placed([result_one, result_two])
    input_local = placed([grad_start, grad_mid])
    dense_one = jnp.concatenate([qkv_one, output_one], axis=1)
    dense_low, dense_high = by_layer(*exchanged([dense_one, pack_two]))
    dense_low, dense_high = dense_low.astype(F32), dense_high.astype(F32)

    def both(start, stop):
        return jnp.concatenate([dense_low[:, start:stop], dense_high[:, start:stop]], axis=1)

    def every_other(start):
        return jnp.concatenate(
            [
                half[:, place : place + LANES]
                for half in (dense_low, dense_high)
                for place in range(start, half_qkv, 2 * LANES)
            ],
            axis=1,
        )

    side = dense_low[:, half_qkv:qkv_columns]

    out_shape = (1, 2, 1, span_rows, model)
    return (
        layer_local.reshape(out_shape),
        input_local.reshape(out_shape),
        side[:, 0][None],
        both(0, half_query)[None],
        every_other(half_query)[None],
        every_other(half_query + LANES)[None],
        both(qkv_columns, qkv_columns + output_half)[None],
        side[:, 1][None],
        side[:, 2 : 2 + all_experts][None],
        grad_gate[None],
        grad_up[None],
        grad_down[None],
    )


def solution(mesh):
    placed = (
        P(None, "expert", "shard", None),
        P(None, "expert", "shard", None),
        P(None, "expert", "shard"),
        P("section", None, "expert", "shard", None),
        P("section", ("expert", "shard")),
        P("section", ("expert", "shard"), None),
        P("section", ("expert", "shard"), None),
        P("section", ("expert", "shard"), None),
        P("section", ("expert", "shard"), None),
        P("section", ("expert", "shard")),
        P("section", ("expert", "shard"), None),
        P("section", "expert", "shard", None),
        P("section", "expert", "shard", None),
        P("section", "expert", None, "shard"),
    )
    return jax.shard_map(
        on_device,
        mesh=mesh,
        in_specs=placed,
        out_specs=(
            P("section", None, "expert", "shard", None),
            P("section", None, "expert", "shard", None),
            P("section", ("expert", "shard")),
            P("section", ("expert", "shard"), None),
            P("section", ("expert", "shard"), None),
            P("section", ("expert", "shard"), None),
            P("section", ("expert", "shard"), None),
            P("section", ("expert", "shard")),
            P("section", ("expert", "shard"), None),
            P("section", "expert", "shard", None),
            P("section", "expert", "shard", None),
            P("section", "expert", None, "shard"),
        ),
        check_vma=False,
    )
```

```python
import functools
import math

import jax
import jax.numpy as jnp
from jax import lax
from jax.experimental import pallas as pl
from jax.experimental.pallas import tpu as pltpu
from jax.sharding import PartitionSpec as P

HEADS = 24
KV_HEADS = 8
HEAD = 64

EPSILON = 1e-06
ROPE_BASE = 10000.0
NEGATIVE = -1e30
LANES = 128
TILE = 256
ROWS = 1024
VMEM_LIMIT = 60 * 1024 * 1024

F32 = jnp.float32
BF16 = jnp.bfloat16


def lasting(micros):
    return pl.CostEstimate(
        flops=int(micros * 1.1e9), bytes_accessed=1000000, transcendentals=0
    )


def swap(array):
    return lax.ppermute(array, "section", [(0, 1), (1, 0)])


def shifted(array, axis, by):
    length = lax.axis_size(axis)
    return lax.ppermute(array, axis, [(i, (i + by) % length) for i in range(length)])


def flipped(array, mask):
    return lax.ppermute(array, "shard", [(i, i ^ mask) for i in range(lax.axis_size("shard"))])


def crossed(array, axis, by):
    length = lax.axis_size(axis)
    if length & (length - 1):
        return shifted(array, axis, by)
    return lax.ppermute(array, axis, [(i, i ^ by) for i in range(length)])


def crossed_back(array, axis, by):
    length = lax.axis_size(axis)
    return shifted(array, axis, -by) if length & (length - 1) else crossed(array, axis, by)


def partner(axis, by, back=False):
    length, me = lax.axis_size(axis), lax.axis_index(axis)
    if length & (length - 1):
        return lax.rem(me + (by if back else length - by), length)
    return me ^ by


def slots_of(array, axis):
    return [array] + [crossed(array, axis, k) for k in range(1, lax.axis_size(axis))]


def after(array, *others):
    return lax.optimization_barrier((array, *others))[0]


def cut(array, start, stop, axis):
    return lax.slice_in_dim(array, start, stop, axis=axis)


def ring_gather(array, axis, held=()):
    count = lax.axis_size("shard")
    me = lax.axis_index("shard")
    if count != 4:
        pieces = [
            (slot, partner("shard", k) if k else me, 0)
            for k, slot in enumerate(slots_of(array, "shard"))
        ]
        return pieces, [piece for piece, _, _ in pieces[1:]]
    length = array.shape[axis]
    half = length // 2
    one = flipped(array, 1)
    two = flipped(array, 2)
    if held:
        one, two = lax.optimization_barrier((one, two, *held))[:2]
    far_low = flipped(cut(one, 0, half, axis), 2)
    far_high = flipped(cut(two, half, length, axis), 1)
    return [
        (array, me, 0),
        (one, me ^ 1, 0),
        (two, me ^ 2, 0),
        (far_low, me ^ 3, 0),
        (far_high, me ^ 3, half),
    ], [one, two]


def rotary_tables(positions):
    frequency = 1.0 / ROPE_BASE ** (jnp.arange(0, HEAD, 2, dtype=F32) / HEAD)
    angles = positions.astype(F32)[:, None] * frequency[None, :]
    cosines, sines = jnp.cos(angles), jnp.sin(angles)
    return (
        jnp.concatenate([cosines] * 4, axis=1),
        jnp.concatenate([-sines, sines] * 2, axis=1),
    )


def norm_back(grad_in, values, scale_rows, scale_gain):
    shaped = grad_in * scale_gain
    grad_values = scale_rows * shaped - values * scale_rows**3 * jnp.mean(
        shaped * values, axis=-1, keepdims=True
    )
    return (grad_values, jnp.sum(grad_in * values * scale_rows, axis=0))


def dot_nt(left, right):
    return lax.dot_general(left, right, (((1,), (1,)), ((), ())), preferred_element_type=F32)


def dot_nn(left, right):
    return jnp.dot(left, right, preferred_element_type=F32)


def dot_tn(left, right):
    return lax.dot_general(left, right, (((0,), (0,)), ((), ())), preferred_element_type=F32)


def fill_weights(ref, gate_up, down):
    parts, _, depth, columns = ref.shape
    width = columns // 3
    for index in range(parts):
        half, place = divmod(index, parts // 2)
        span = slice(place * depth, (place + 1) * depth)
        gate_up[span, 2 * half * width : 2 * (half + 1) * width] = ref[index, 0, :, : 2 * width]
        down[span, half * width : (half + 1) * width] = ref[index, 0, :, 2 * width :]


def column_of(table, index):
    lane = lax.broadcasted_iota(jnp.int32, table.shape, 1)
    return jnp.sum(jnp.where(lane == index, table, 0.0), axis=1, keepdims=True)


def split_gate_up(raw, width):
    gate = jnp.concatenate([raw[:, :width], raw[:, 2 * width : 3 * width]], axis=1)
    up = jnp.concatenate([raw[:, width : 2 * width], raw[:, 3 * width :]], axis=1)
    return gate, up


def join_gate_up(gate, up, width):
    return jnp.concatenate(
        [gate[:, :width], up[:, :width], gate[:, width:], up[:, width:]], axis=1
    )


def moe_forward(rows, gates, weights):
    total, model = rows.shape
    parts, experts, depth, columns = weights.shape
    width = columns // 3
    tile = math.gcd(ROWS, total)

    def body(rows_ref, gates_ref, weights_ref, out_ref, raw_ref, gate_up, down, sums):
        expert = pl.program_id(0)
        fill_weights(weights_ref, gate_up, down)

        def step(index, carry):
            span = pl.ds(pl.multiple_of(index * tile, tile), tile)
            raw = dot_nn(rows_ref[span, :], gate_up[...])
            raw_ref[0, span, :] = raw.astype(BF16)
            gate, up = split_gate_up(raw, width)
            weight = column_of(gates_ref[span, :], expert)
            act = (gate * jax.nn.sigmoid(gate) * up * weight).astype(BF16)
            part = dot_nt(act, down[...])

            @pl.when(expert == 0)
            def _():
                sums[span, :] = part

            @pl.when(expert > 0)
            def _():
                sums[span, :] += part

            @pl.when(expert == experts - 1)
            def _():
                out_ref[span, :] = sums[span, :].astype(BF16)

            return carry

        lax.fori_loop(0, total // tile, step, 0)

    whole = lambda e: (0, 0)
    per_expert = lambda e: (e, 0, 0)
    once = pl.Buffered(1)
    return pl.pallas_call(
        body,
        grid_spec=pltpu.PrefetchScalarGridSpec(
            num_scalar_prefetch=0,
            grid=(experts,),
            in_specs=[
                pl.BlockSpec((total, model), whole, pipeline_mode=once),
                pl.BlockSpec((total, LANES), whole, pipeline_mode=once),
            ]
            + [pl.BlockSpec((parts, 1, depth, columns), lambda e: (0, e, 0, 0))],
            out_specs=[
                pl.BlockSpec((total, model), whole),
                pl.BlockSpec((1, total, 4 * width), per_expert),
            ],
            scratch_shapes=[
                pltpu.VMEM((model, 4 * width), BF16),
                pltpu.VMEM((model, 2 * width), BF16),
                pltpu.VMEM((total, model), F32),
            ],
        ),
        out_shape=[
            jax.ShapeDtypeStruct((total, model), BF16),
            jax.ShapeDtypeStruct((experts, total, 4 * width), BF16),
        ],
        compiler_params=pltpu.CompilerParams(vmem_limit_bytes=VMEM_LIMIT),
        cost_estimate=lasting(40),
        name="moe_forward",
    )(rows, gates, weights)


def moe_backward_rows(grads, gates, raws, weights):
    total, model = grads.shape
    parts, experts, depth, columns = weights.shape
    width = columns // 3
    tile = math.gcd(ROWS, total)

    def body(
        grads_ref,
        gates_ref,
        raw_ref,
        weights_ref,
        out_ref,
        d_raw_ref,
        act_ref,
        gate_up,
        down,
        sums,
        scores,
    ):
        expert = pl.program_id(0)
        fill_weights(weights_ref, gate_up, down)

        def step(index, carry):
            span = pl.ds(pl.multiple_of(index * tile, tile), tile)
            weight = column_of(gates_ref[span, :], expert)
            gate, up = split_gate_up(raw_ref[0, span, :].astype(F32), width)
            back = dot_nn(grads_ref[span, :], down[...])
            sigmoid = jax.nn.sigmoid(gate)
            swish = gate * sigmoid
            act = swish * up
            score = jnp.sum(back * act, axis=1, keepdims=True)
            act_ref[0, span, :] = (act * weight).astype(BF16)
            d_act = back * weight
            d_gate = d_act * up * sigmoid * (1.0 + gate * (1.0 - sigmoid))
            d_raw = join_gate_up(d_gate, d_act * swish, width).astype(BF16)
            d_raw_ref[0, span, :] = d_raw
            part = dot_nt(d_raw, gate_up[...])
            lane = lax.broadcasted_iota(jnp.int32, (tile, LANES), 1)

            @pl.when(expert == 0)
            def _():
                sums[span, :] = part
                scores[span, :] = jnp.where(lane == 0, score, 0.0)

            @pl.when(expert > 0)
            def _():
                sums[span, :] += part
                scores[span, :] = jnp.where(lane == expert, score, scores[span, :])

            @pl.when(expert == experts - 1)
            def _():
                out_ref[span, :model] = sums[span, :].astype(BF16)
                whole_scores = scores[span, :]
                high = whole_scores.astype(BF16).astype(F32)
                out_ref[span, model:] = jnp.where(
                    lane < HEAD, high, pltpu.roll(whole_scores - high, HEAD, 1)
                ).astype(BF16)

            return carry

        lax.fori_loop(0, total // tile, step, 0)

    whole = lambda e: (0, 0)
    per_expert = lambda e: (e, 0, 0)
    once = pl.Buffered(1)
    return pl.pallas_call(
        body,
        grid_spec=pltpu.PrefetchScalarGridSpec(
            num_scalar_prefetch=0,
            grid=(experts,),
            in_specs=[
                pl.BlockSpec((total, model), whole, pipeline_mode=once),
                pl.BlockSpec((total, LANES), whole, pipeline_mode=once),
                pl.BlockSpec((1, total, 4 * width), per_expert),
            ]
            + [pl.BlockSpec((parts, 1, depth, columns), lambda e: (0, e, 0, 0))],
            out_specs=[
                pl.BlockSpec((total, model + LANES), whole),
                pl.BlockSpec((1, total, 4 * width), per_expert),
                pl.BlockSpec((1, total, 2 * width), per_expert),
            ],
            scratch_shapes=[
                pltpu.VMEM((model, 4 * width), BF16),
                pltpu.VMEM((model, 2 * width), BF16),
                pltpu.VMEM((total, model), F32),
                pltpu.VMEM((total, LANES), F32),
            ],
        ),
        out_shape=[
            jax.ShapeDtypeStruct((total, model + LANES), BF16),
            jax.ShapeDtypeStruct((experts, total, 4 * width), BF16),
            jax.ShapeDtypeStruct((experts, total, 2 * width), BF16),
        ],
        compiler_params=pltpu.CompilerParams(vmem_limit_bytes=VMEM_LIMIT),
        cost_estimate=lasting(48),
        name="moe_backward_rows",
    )(grads, gates, raws, weights)


def moe_backward_weights(rows, grads, d_raws, acts, parts):
    total, model = rows.shape
    experts = d_raws.shape[0]
    width = d_raws.shape[2] // 4
    shards = parts // 2
    depth = model // shards

    def body(rows_ref, grads_ref, d_raw_ref, act_ref, out_ref, rows_t, grads_t):
        @pl.when(pl.program_id(0) == 0)
        def _():
            for start in range(0, model, TILE):
                rows_t[start : start + TILE, :] = rows_ref[:, start : start + TILE].T
                grads_t[start : start + TILE, :] = grads_ref[:, start : start + TILE].T

        for place in range(shards):
            span = slice(place * depth, (place + 1) * depth)
            gate_up = dot_nn(rows_t[span, :], d_raw_ref[0]).astype(BF16)
            down = dot_nn(grads_t[span, :], act_ref[0]).astype(BF16)
            for half in range(2):
                index = half * shards + place
                out_ref[index, 0, :, : 2 * width] = gate_up[
                    :, 2 * half * width : 2 * (half + 1) * width
                ]
                out_ref[index, 0, :, 2 * width :] = down[:, half * width : (half + 1) * width]

    whole = lambda e: (0, 0)
    per_expert = lambda e: (e, 0, 0)
    once = pl.Buffered(1)
    return pl.pallas_call(
        body,
        grid_spec=pltpu.PrefetchScalarGridSpec(
            num_scalar_prefetch=0,
            grid=(experts,),
            in_specs=[
                pl.BlockSpec((total, model), whole, pipeline_mode=once),
                pl.BlockSpec((total, model), whole, pipeline_mode=once),
                pl.BlockSpec((1, total, 4 * width), per_expert),
                pl.BlockSpec((1, total, 2 * width), per_expert),
            ],
            out_specs=pl.BlockSpec((parts, 1, depth, 3 * width), lambda e: (0, e, 0, 0)),
            scratch_shapes=[
                pltpu.VMEM((model, total), BF16),
                pltpu.VMEM((model, total), BF16),
            ],
        ),
        out_shape=jax.ShapeDtypeStruct((parts, experts, depth, 3 * width), BF16),
        compiler_params=pltpu.CompilerParams(vmem_limit_bytes=VMEM_LIMIT),
        cost_estimate=lasting(34),
        name="moe_backward_weights",
    )(rows, grads, d_raws, acts)


def expert_outputs(mine, other, core):
    experts, depth, columns = mine.shape
    width = columns // 3

    def body(core_ref, mine_ref, other_ref, gate_ref, up_ref, down_ref):
        is_first = core_ref[0] == 0
        own, received = mine_ref[0].astype(F32), other_ref[0].astype(F32)
        low = jnp.where(is_first, own, received)
        high = jnp.where(is_first, received, own)
        for index, half in enumerate((low, high)):
            span = slice(index * width, (index + 1) * width)
            gate_ref[0, :, span] = half[:, :width]
            up_ref[0, :, span] = half[:, width : 2 * width]
            down_ref[0, span, :] = half[:, 2 * width :].T

    block = lambda e, *_: (e, 0, 0)
    return pl.pallas_call(
        body,
        grid_spec=pltpu.PrefetchScalarGridSpec(
            num_scalar_prefetch=1,
            grid=(experts,),
            in_specs=[pl.BlockSpec((1, depth, columns), block)] * 2,
            out_specs=[
                pl.BlockSpec((1, depth, 2 * width), block),
                pl.BlockSpec((1, depth, 2 * width), block),
                pl.BlockSpec((1, 2 * width, depth), block),
            ],
        ),
        out_shape=[
            jax.ShapeDtypeStruct((experts, depth, 2 * width), F32),
            jax.ShapeDtypeStruct((experts, depth, 2 * width), F32),
            jax.ShapeDtypeStruct((experts, 2 * width, depth), F32),
        ],
        compiler_params=pltpu.CompilerParams(vmem_limit_bytes=VMEM_LIMIT),
        cost_estimate=lasting(6),
        name="expert_outputs",
    )(jnp.reshape(core, (1,)).astype(jnp.int32), mine, other)


def line_up(pieces, owners, planes_of, shards):
    arrays = [piece for piece, _, _ in pieces]
    slots, rows, width = arrays[0].shape
    copies = slots * shards
    if rows % 16:
        result = jnp.zeros((slots, shards, rows, width), BF16)
        for place, (array, _, start) in enumerate(pieces):
            for slot in range(array.shape[0]):
                result = lax.dynamic_update_slice(
                    result,
                    array[slot][None, None],
                    (planes_of[start + slot], owners[place], 0, 0),
                )
        return result.reshape(copies * rows, width)

    def body(owner_ref, plane_ref, *refs):
        out_ref, sems = refs[len(arrays) :]
        started = []
        for place, (array, _, start) in enumerate(pieces):
            for slot in range(array.shape[0]):
                index = plane_ref[start + slot] * shards + owner_ref[place]
                started.append(
                    pltpu.make_async_copy(
                        refs[place].at[slot],
                        out_ref.at[pl.ds(pl.multiple_of(index * rows, 16), rows), :],
                        sems.at[len(started)],
                    )
                )
                started[-1].start()
        for copy in started:
            copy.wait()

    return pl.pallas_call(
        body,
        grid_spec=pltpu.PrefetchScalarGridSpec(
            num_scalar_prefetch=2,
            grid=(1,),
            in_specs=[pl.BlockSpec(memory_space=pl.ANY)] * len(arrays),
            out_specs=pl.BlockSpec((copies * rows, width), lambda i, *_: (0, 0)),
            scratch_shapes=[pltpu.SemaphoreType.DMA((copies * 2,))],
        ),
        out_shape=jax.ShapeDtypeStruct((copies * rows, width), BF16),
        compiler_params=pltpu.CompilerParams(vmem_limit_bytes=VMEM_LIMIT),
        cost_estimate=lasting(4),
        name="line_up",
    )(owners, planes_of, *arrays)


def turned(values, cosines, sines):
    lane = lax.broadcasted_iota(jnp.int32, cosines.shape, 1)
    low = lane % HEAD < HEAD // 2
    parts = []
    for start in range(0, values.shape[1], LANES):
        block = values[:, start : start + LANES]
        partner = jnp.where(
            low,
            pltpu.roll(block, LANES - HEAD // 2, 1),
            pltpu.roll(block, HEAD // 2, 1),
        )
        parts.append(block * cosines + partner * sines)
    return jnp.concatenate(parts, axis=1)


def pair_columns(width):
    return [start for start in range(0, width, 2 * LANES)]


def half_specs(halves, columns):
    return [
        pl.BlockSpec((1, array.shape[1], columns), lambda i, *_, place=place: (place, 0, 0))
        for array, place in halves
    ]


def qkv_forward(stream, gain, halves, cosines, sines, columns):
    rows, model = stream.shape
    queries, kv = columns

    def body(stream_ref, gain_ref, mine_ref, other_ref, cos_ref, sin_ref, q_ref, kv_ref, n_ref):
        values = stream_ref[...]
        scale = lax.rsqrt(jnp.mean(values * values, axis=1, keepdims=True) + EPSILON)
        n_ref[...] = (values * scale * gain_ref[...]).astype(BF16)
        cos, sin = cos_ref[...], sin_ref[...]
        for index, ref in enumerate((mine_ref, other_ref)):
            raw = dot_nn(n_ref[...], ref[0])
            q_ref[:, index * queries : (index + 1) * queries] = turned(
                raw[:, :queries], cos, sin
            ).astype(BF16)
            for start in pair_columns(kv):
                place = index * kv + start
                keys = raw[:, queries + start : queries + start + LANES]
                kv_ref[:, place : place + LANES] = turned(keys, cos, sin).astype(BF16)
                kv_ref[:, place + LANES : place + 2 * LANES] = raw[
                    :, queries + start + LANES : queries + start + 2 * LANES
                ].astype(BF16)

    whole = lambda i: (0, 0)
    return pl.pallas_call(
        body,
        grid=(1,),
        in_specs=[
            pl.BlockSpec((rows, model), whole),
            pl.BlockSpec((1, model), whole),
            *half_specs(halves, queries + kv),
            pl.BlockSpec((rows, LANES), whole),
            pl.BlockSpec((rows, LANES), whole),
        ],
        out_specs=[
            pl.BlockSpec((rows, 2 * queries), whole),
            pl.BlockSpec((rows, 2 * kv), whole),
            pl.BlockSpec((rows, model), whole),
        ],
        out_shape=[
            jax.ShapeDtypeStruct((rows, 2 * queries), BF16),
            jax.ShapeDtypeStruct((rows, 2 * kv), BF16),
            jax.ShapeDtypeStruct((rows, model), BF16),
        ],
        compiler_params=pltpu.CompilerParams(vmem_limit_bytes=VMEM_LIMIT),
        cost_estimate=lasting(7),
        name="qkv_forward",
    )(stream, gain, *[array for array, _ in halves], cosines, sines)


def branch_backward(backs, places, experts, gates, side, middle, gain, grad_out, halves, flip):
    rows, model = middle.shape
    count = len(backs)
    half_width = halves[0].shape[1]

    def body(places_ref, flip_ref, *refs):
        slots = refs[:count]
        gates_ref, side_ref, middle_ref, gain_ref, out_grad_ref, one_ref, two_ref = refs[
            count : count + 7
        ]
        d_middle_ref, branch_ref, attended_ref, high_ref, low_ref, d_gain_ref = refs[count + 7 :]
        lane = lax.broadcasted_iota(jnp.int32, (LANES, LANES), 0) % HEAD
        column = lax.broadcasted_iota(jnp.int32, (LANES, LANES), 1)
        d_hidden = None
        d_gates = None
        for index, slot in enumerate(slots):
            placing = (lane < experts) & (column == lane + 2 + places_ref[index] * experts)
            part = dot_nn(slot[:, model:], placing.astype(F32).astype(BF16))
            values = slot[:, :model].astype(F32)
            d_hidden = values if d_hidden is None else d_hidden + values
            d_gates = part if d_gates is None else d_gates + part
        gate_table = gates_ref[...]
        share = jnp.sum(gate_table * d_gates, axis=1, keepdims=True)
        d_logits = gate_table * (d_gates - share)
        high = d_logits.astype(BF16)
        low = (d_logits - high.astype(F32)).astype(BF16)
        high_ref[...] = high
        low_ref[...] = low
        d_hidden = d_hidden + dot_nt(high, side_ref[...]) + dot_nt(low, side_ref[...])
        values = middle_ref[...]
        scale = lax.rsqrt(jnp.mean(values * values, axis=1, keepdims=True) + EPSILON)
        d_gain = jnp.sum(d_hidden * values * scale, axis=0, keepdims=True)
        d_gain_ref[...] = jnp.broadcast_to(d_gain, (8, model))
        shaped = d_hidden * gain_ref[...]
        mean = jnp.mean(shaped * values, axis=1, keepdims=True)
        d_middle = (
            out_grad_ref[...].astype(F32) + scale * shaped - values * (scale * scale * scale * mean)
        )
        d_middle_ref[...] = d_middle
        branch = d_middle.astype(BF16)
        branch_ref[...] = branch
        flipped_order = flip_ref[0] == 1
        first_half, second_half = branch[:, :half_width], branch[:, half_width:]
        attended = dot_nt(
            jnp.where(flipped_order, second_half, first_half), one_ref[...]
        ) + dot_nt(jnp.where(flipped_order, first_half, second_half), two_ref[...])
        width = attended.shape[1] // 2
        left, right = attended[:, :width], attended[:, width:]
        attended_ref[:, :width] = jnp.where(flipped_order, right, left).astype(BF16)
        attended_ref[:, width:] = jnp.where(flipped_order, left, right).astype(BF16)

    arrays = [*backs, gates, side, middle, gain, grad_out, *halves]
    whole = lambda i, *_: (0, 0)
    outs = [
        ((rows, model), F32),
        ((rows, model), BF16),
        ((rows, halves[0].shape[0]), BF16),
        ((rows, LANES), BF16),
        ((rows, LANES), BF16),
        ((8, model), F32),
    ]
    return pl.pallas_call(
        body,
        grid_spec=pltpu.PrefetchScalarGridSpec(
            num_scalar_prefetch=2,
            grid=(1,),
            in_specs=[pl.BlockSpec(array.shape, whole) for array in arrays],
            out_specs=[pl.BlockSpec(shape, whole) for shape, _ in outs],
        ),
        out_shape=[jax.ShapeDtypeStruct(shape, dtype) for shape, dtype in outs],
        compiler_params=pltpu.CompilerParams(vmem_limit_bytes=VMEM_LIMIT),
        cost_estimate=lasting(12),
        name="branch_backward",
    )(places, flip, *arrays)


def qkv_backward(
    normed, d_queries, d_kv_slots, halves, cosines, sines, columns, stream, side, flip, extra, grid
):
    rows, model = normed.shape
    queries, kv = columns
    qkv = queries + kv
    count = len(d_kv_slots)
    shards, planes = grid
    depth = model // (shards * planes)
    more = extra[1].shape[1] if extra else 0

    def body(flip_ref, n_ref, dq_ref, *refs):
        slots = refs[:count]
        mine_ref, other_ref, cos_ref, sin_ref, stream_ref = refs[count : count + 5]
        hidden_ref, high_ref, low_ref, gain_two_ref = refs[count + 5 : count + 9]
        extra_refs = refs[count + 9 : count + 9 + len(extra)]
        out_ref, grad_ref, n_t, grads = refs[count + 9 + len(extra) :]
        flipped_order = flip_ref[0]
        cos, sin = cos_ref[...], -sin_ref[...]

        def write(index, first_column, values):
            last_column = first_column + values.shape[1]
            grads[:, : values.shape[1]] = values
            for plane in range(planes):
                for shard in range(shards):
                    start = (plane * shards + shard) * depth
                    grad_ref[index * shards + shard, plane, :, first_column:last_column] = grads[
                        start : start + depth, : values.shape[1]
                    ].astype(BF16)

        n_t[...] = n_ref[...].T
        for index, ref in ((0, mine_ref), (1, other_ref)):
            span = slice(index * kv, (index + 1) * kv)
            d_kv = slots[0][:, span].astype(F32)
            for slot in slots[1:]:
                d_kv = d_kv + slot[:, span].astype(F32)
            parts = [dq_ref[:, index * queries : (index + 1) * queries]]
            for start in pair_columns(kv):
                parts.append(turned(d_kv[:, start : start + LANES], cos, sin).astype(BF16))
                parts.append(d_kv[:, start + LANES : start + 2 * LANES].astype(BF16))
            d_raw = jnp.concatenate(parts, axis=1)
            back = dot_nt(d_raw, ref[0])
            if index == 0:
                out_ref[...] = back
            else:
                out_ref[...] += back
            place = flipped_order if index == 0 else 1 - flipped_order
            write(place, 0, dot_nn(n_t[...], d_raw))
        values = stream_ref[...]
        scale = lax.rsqrt(jnp.mean(values * values, axis=1, keepdims=True) + EPSILON)
        gain = jnp.sum(out_ref[...] * values * scale, axis=0, keepdims=True)
        gain = jnp.broadcast_to(gain, (LANES, model)).T
        gain_two = jnp.broadcast_to(gain_two_ref[:1, :], (LANES, model)).T
        n_t[...] = hidden_ref[...].T
        routing = dot_nn(n_t[...], high_ref[...]) + dot_nn(n_t[...], low_ref[...])
        lane = lax.broadcasted_iota(jnp.int32, (model, LANES), 1)
        whole_side = jnp.where(lane == 0, gain, jnp.where(lane == 1, gain_two, routing))
        write(0, qkv, whole_side)
        write(1, qkv, jnp.zeros_like(whole_side))
        if extra:
            n_t[...] = extra_refs[0][...].T
            for index in range(2):
                write(index, qkv + LANES, dot_nn(n_t[...], extra_refs[index + 1][...]))

    whole = lambda i, *_: (0, 0)
    return pl.pallas_call(
        body,
        grid_spec=pltpu.PrefetchScalarGridSpec(
            num_scalar_prefetch=1,
            grid=(1,),
        in_specs=[
            pl.BlockSpec((rows, model), whole),
            pl.BlockSpec((rows, 2 * queries), whole),
        ]
        + [pl.BlockSpec((rows, 2 * kv), whole)] * count
        + half_specs(halves, qkv)
        + [
            pl.BlockSpec((rows, LANES), whole),
            pl.BlockSpec((rows, LANES), whole),
            pl.BlockSpec((rows, model), whole),
        ]
        + [pl.BlockSpec(array.shape, whole) for array in (*side, *extra)],
        out_specs=[
            pl.BlockSpec((rows, model), whole),
            pl.BlockSpec(
                (2 * shards, planes, depth, qkv + LANES + more), lambda i, *_: (0, 0, 0, 0)
            ),
        ],
        scratch_shapes=[pltpu.VMEM((model, rows), BF16), pltpu.VMEM((model, qkv), F32)],
        ),
        out_shape=[
            jax.ShapeDtypeStruct((rows, model), F32),
            jax.ShapeDtypeStruct((2 * shards, planes, depth, qkv + LANES + more), BF16),
        ],
        compiler_params=pltpu.CompilerParams(vmem_limit_bytes=VMEM_LIMIT),
        cost_estimate=lasting(14),
        name="qkv_backward",
    )(
        flip,
        normed,
        d_queries,
        *d_kv_slots,
        *[array for array, _ in halves],
        cosines,
        sines,
        stream,
        *side,
        *extra,
    )


def head_sides(block):
    lane = lax.broadcasted_iota(jnp.int32, block.shape, 1)
    low = lane < HEAD
    crossed = jnp.concatenate([block[:, HEAD:], block[:, :HEAD]], axis=1)
    nothing = jnp.zeros_like(block)
    return [
        [jnp.where(low, block, nothing), jnp.where(low, nothing, crossed)],
        [jnp.where(low, crossed, nothing), jnp.where(low, nothing, block)],
    ]


def fill_bias(bias, owner_ref, seg_all_ref, seg_ref, rows, count):
    own = owner_ref[0] * rows + lax.broadcasted_iota(jnp.int32, (rows, rows), 1)
    for slot in range(count):
        span = slice(slot * rows, (slot + 1) * rows)
        place = owner_ref[slot] * rows + lax.broadcasted_iota(jnp.int32, (rows, rows), 0)
        allowed = (place <= own) & (seg_all_ref[span, :1] == seg_ref[:1, :])
        bias[span, :] = jnp.where(allowed, 0.0, NEGATIVE)


def attention_specs(rows, count, group):
    whole = lambda p, *_: (0, 0)
    return (
        [
            pl.BlockSpec((count * rows, LANES), whole),
            pl.BlockSpec((8, rows), whole),
            pl.BlockSpec((rows, 2 * group * HEAD), lambda p, *_: (0, p)),
        ]
        + [pl.BlockSpec((rows, 2 * LANES), lambda p, *_: (0, p))] * count
    )


def attention_forward(queries, kv_slots, owners, seg_all, seg_own):
    rows, width = queries.shape
    count = len(kv_slots)
    group = HEADS // KV_HEADS
    pairs = KV_HEADS // 2
    heads = 2 * group
    total = count * rows
    scale = 1.0 / math.sqrt(HEAD)

    def body(owner_ref, seg_all_ref, seg_ref, q_ref, *refs):
        slots = refs[:count]
        out_ref, stat_ref, bias = refs[count:]

        @pl.when(pl.program_id(0) == 0)
        def _():
            fill_bias(bias, owner_ref, seg_all_ref, seg_ref, rows, count)

        keys = head_sides(jnp.concatenate([ref[:, :LANES] for ref in slots], axis=0))
        values = head_sides(jnp.concatenate([ref[:, LANES:] for ref in slots], axis=0))
        values = [[side.T for side in sides] for sides in values]
        scaled = (q_ref[...].astype(F32) * scale).astype(BF16)
        stats = []
        for block in range(group):
            out = None
            for side in range(2):
                head = 2 * block + side
                kv = head // group
                scores = (
                    dot_nt(keys[kv][side], scaled[:, block * LANES : (block + 1) * LANES])
                    + bias[...]
                )
                top = jnp.max(scores, axis=0, keepdims=True)
                exponent = jnp.exp(scores - top)
                total_of = jnp.sum(exponent, axis=0, keepdims=True)
                probs = (exponent * (1.0 / total_of)).astype(BF16)
                part = dot_nn(values[kv][side], probs)
                out = part if out is None else out + part
                stats.append(top + jnp.log(total_of))
            out_ref[:, block * LANES : (block + 1) * LANES] = out.T.astype(BF16)
        stat_ref[0, :heads, :] = jnp.concatenate(stats, axis=0)

    return pl.pallas_call(
        body,
        grid_spec=pltpu.PrefetchScalarGridSpec(
            num_scalar_prefetch=1,
            grid=(pairs,),
            in_specs=attention_specs(rows, count, group),
            out_specs=[
                pl.BlockSpec((rows, heads * HEAD), lambda p, *_: (0, p)),
                pl.BlockSpec((1, 8, rows), lambda p, *_: (p, 0, 0)),
            ],
            scratch_shapes=[pltpu.VMEM((total, rows), F32)],
        ),
        out_shape=[
            jax.ShapeDtypeStruct((rows, width), BF16),
            jax.ShapeDtypeStruct((pairs, 8, rows), F32),
        ],
        compiler_params=pltpu.CompilerParams(vmem_limit_bytes=VMEM_LIMIT),
        cost_estimate=lasting(17),
        name="attention_forward",
    )(owners, seg_all, seg_own, queries, *kv_slots)


def attention_backward(queries, kv_slots, owners, seg_all, seg_own, d_out, stats, cosines, sines):
    rows, width = queries.shape
    count = len(kv_slots)
    group = HEADS // KV_HEADS
    pairs = KV_HEADS // 2
    heads = 2 * group
    total = count * rows
    scale = 1.0 / math.sqrt(HEAD)

    def body(owner_ref, seg_all_ref, seg_ref, q_ref, *refs):
        slots = refs[:count]
        d_out_ref, stat_ref, cos_ref, sin_ref = refs[count : count + 4]
        d_q_ref = refs[count + 4]
        d_slots = refs[count + 5 : 2 * count + 5]
        bias, d_keys, d_values = refs[2 * count + 5 :]

        @pl.when(pl.program_id(0) == 0)
        def _():
            fill_bias(bias, owner_ref, seg_all_ref, seg_ref, rows, count)

        keys = head_sides(jnp.concatenate([ref[:, :LANES] for ref in slots], axis=0))
        values = head_sides(jnp.concatenate([ref[:, LANES:] for ref in slots], axis=0))
        keys_t = [[side.T for side in sides] for sides in keys]
        cos, sin = cos_ref[...], -sin_ref[...]
        for block in range(group):
            span = slice(block * LANES, (block + 1) * LANES)
            scaled = (q_ref[:, span].astype(F32) * scale).astype(BF16)
            d_block = d_out_ref[:, span]
            q_sides = head_sides(scaled)
            d_sides = head_sides(d_block)
            d_q = None
            for side in range(2):
                head = 2 * block + side
                kv = head // group
                scores = dot_nt(keys[kv][side], scaled) + bias[...]
                probs = jnp.exp(scores - stat_ref[0, head : head + 1, :])
                d_probs = dot_nt(values[kv][side], d_block)
                share = jnp.sum(probs * d_probs, axis=0, keepdims=True)
                d_scores = (probs * (d_probs - share)).astype(BF16)
                part = dot_nn(keys_t[kv][side], d_scores)
                d_q = part if d_q is None else d_q + part
                d_key = dot_nn(d_scores, q_sides[side][kv])
                d_value = dot_nn(probs.astype(BF16), d_sides[side][kv])
                if head == 0:
                    d_keys[...] = d_key
                    d_values[...] = d_value
                else:
                    d_keys[...] += d_key
                    d_values[...] += d_value
            d_q_ref[:, span] = turned(d_q.T * scale, cos, sin).astype(BF16)
        for slot in range(count):
            part = slice(slot * rows, (slot + 1) * rows)
            d_slots[slot][:, :LANES] = d_keys[part, :].astype(BF16)
            d_slots[slot][:, LANES:] = d_values[part, :].astype(BF16)

    whole = lambda p, *_: (0, 0)
    return pl.pallas_call(
        body,
        grid_spec=pltpu.PrefetchScalarGridSpec(
            num_scalar_prefetch=1,
            grid=(pairs,),
            in_specs=attention_specs(rows, count, group)
            + [
                pl.BlockSpec((rows, heads * HEAD), lambda p, *_: (0, p)),
                pl.BlockSpec((1, 8, rows), lambda p, *_: (p, 0, 0)),
                pl.BlockSpec((rows, LANES), whole),
                pl.BlockSpec((rows, LANES), whole),
            ],
            out_specs=[pl.BlockSpec((rows, heads * HEAD), lambda p, *_: (0, p))]
            + [pl.BlockSpec((rows, 2 * LANES), lambda p, *_: (0, p))] * count,
            scratch_shapes=[
                pltpu.VMEM((total, rows), F32),
                pltpu.VMEM((total, LANES), F32),
                pltpu.VMEM((total, LANES), F32),
            ],
        ),
        out_shape=[jax.ShapeDtypeStruct((rows, width), BF16)]
        + [jax.ShapeDtypeStruct((rows, 2 * KV_HEADS * HEAD), BF16)] * count,
        compiler_params=pltpu.CompilerParams(vmem_limit_bytes=VMEM_LIMIT),
        cost_estimate=lasting(27),
        name="attention_backward",
    )(owners, seg_all, seg_own, queries, *kv_slots, d_out, stats, cosines, sines)


def on_device(
    inputs,
    cotangent,
    segments,
    routes,
    attn_gain,
    w_query,
    w_key,
    w_value,
    w_output,
    ffn_gain,
    router,
    w_gate,
    w_up,
    w_down,
):
    core = lax.axis_index("section")
    shard = lax.axis_index("shard")
    plane = lax.axis_index("expert")
    shards = lax.axis_size("shard")
    planes = lax.axis_size("expert")
    span_rows, model = inputs.shape[2:]
    seq_rows = span_rows * shards
    gathered_rows = span_rows * planes
    local_experts = w_gate.shape[1]
    all_experts = local_experts * planes
    hidden = w_gate.shape[3]
    half_hidden = hidden // 2
    part_rows = w_query.shape[1]
    query_width = HEADS * HEAD
    kv_width = KV_HEADS * HEAD
    group_size = HEADS // KV_HEADS
    score_scale = 1.0 / math.sqrt(HEAD)
    first = core == 0

    def mine_of(array):
        return lax.dynamic_index_in_dim(array, core, 0, keepdims=False)

    def by_layer(own, received):
        return [jnp.where(first, own, received), jnp.where(first, received, own)]

    def halved(own_halves):
        kept = jnp.where(first, own_halves[0], own_halves[1])
        sent = jnp.where(first, own_halves[1], own_halves[0])
        return by_layer(kept, swap(sent))

    misc = jnp.concatenate(
        [
            attn_gain[0][:, None],
            ffn_gain[0][:, None],
            router[0],
            jnp.zeros((part_rows, LANES - 2 - all_experts), BF16),
        ],
        axis=1,
    )
    half_query = query_width // 2
    half_kv = kv_width // 2
    half_qkv = half_query + 2 * half_kv

    def head_half(index, side):
        return jnp.concatenate(
            [
                w_query[0][:, index * half_query : (index + 1) * half_query],
            ]
            + [
                array[0][:, start : start + LANES]
                for start in range(index * half_kv, (index + 1) * half_kv, LANES)
                for array in (w_key, w_value)
            ]
            + [side],
            axis=1,
        )

    output_half = model // 2
    qkv_mine = halved([head_half(0, misc), head_half(1, jnp.zeros_like(misc))])
    output_mine = halved([w_output[0][:, :output_half], w_output[0][:, output_half:]])

    plane_order = jnp.stack(
        [plane] + [partner("expert", k) for k in range(1, planes)]
    ).astype(jnp.int32)

    segment_local = mine_of(segments)[0]
    segment_all = jnp.concatenate(
        [slot[0] for slot in slots_of(segment_local[None], "shard")]
    )
    own_routes = routes[0, :, 0]
    route_rows = by_layer(
        lax.dynamic_index_in_dim(own_routes, core, 0, keepdims=False),
        swap(lax.dynamic_index_in_dim(own_routes, 1 - core, 0, keepdims=False)),
    )
    expert_ids = jnp.arange(all_experts, dtype=jnp.int32)
    chosen = jnp.stack(
        [
            jnp.any(rows[:, :, None] == expert_ids[None, None, :], axis=1).astype(BF16)
            for rows in route_rows
        ]
    )
    chosen_all = jnp.concatenate(slots_of(jnp.swapaxes(chosen, 1, 2), "expert"), axis=2)

    def dense_weights(lined, held=(), before=()):
        pieces, first_step = ring_gather(lined, 0, held)
        if before:
            last = lax.optimization_barrier((pieces[-1][0], *before))[0]
            pieces[-1] = (last, *pieces[-1][1:])
        owners = jnp.stack([owner for _, owner, _ in pieces]).astype(jnp.int32)
        mine = line_up(pieces, owners, plane_order, shards)
        return (mine, swap(mine)), first_step, [piece for piece, _, _ in pieces[-2:]]

    lined = jnp.stack(slots_of(qkv_mine[0], "expert"))
    first_qkv, ring_start, ring_end = dense_weights(lined, before=(chosen_all, segment_all))
    lined_output = jnp.stack(slots_of(after(output_mine[0], *ring_start), "expert"))
    own_gate, own_up, own_down, *_ = lax.optimization_barrier(
        (w_gate[0], w_up[0], w_down[0], *ring_start)
    )
    down_turned = jnp.swapaxes(own_down, 1, 2)

    def expert_half(start):
        stop = start + half_hidden
        return jnp.concatenate(
            [own_gate[:, :, start:stop], own_up[:, :, start:stop], down_turned[:, :, start:stop]],
            axis=2,
        )

    expert_mine = halved([expert_half(0), expert_half(half_hidden)])
    first_experts = lax.all_gather(
        after(expert_mine[0], *ring_end), ("section", "shard"), axis=0
    )
    second_pack = lax.all_gather(
        jnp.concatenate([qkv_mine[1], output_mine[1]], axis=1), "expert", axis=0
    )
    second_pack = lax.all_gather(second_pack, ("section", "shard"), axis=0)
    second_pack = (
        second_pack.reshape(2, shards, planes, part_rows, -1)
        .swapaxes(1, 2)
        .reshape(2, model, half_qkv + LANES + output_half)
    )
    second_experts = lax.all_gather(expert_mine[1], ("section", "shard"), axis=0)

    qkv_columns = half_qkv + LANES

    def natural(halves, relative):
        mine, other = halves
        if not relative:
            return jnp.concatenate([mine, other], axis=1)
        return jnp.concatenate(
            [jnp.where(first, mine, other), jnp.where(first, other, mine)], axis=1
        )

    def parted(array, relative):
        half = array.shape[1] // 2
        low, high = array[:, :half], array[:, half:]
        if not relative:
            return low, high
        return jnp.where(first, low, high), jnp.where(first, high, low)

    positions = shard * span_rows + jnp.arange(span_rows, dtype=jnp.int32)
    cosines, sines = rotary_tables(positions)
    key_owners = jnp.stack(
        [shard] + [partner("shard", k) for k in range(1, shards)]
    ).astype(jnp.int32)
    seg_all = jnp.broadcast_to(segment_all[:, None], (seq_rows, LANES))
    seg_own = jnp.broadcast_to(segment_local[None, :], (8, span_rows))
    chosen_all = jnp.swapaxes(chosen_all, 1, 2) > 0.5

    last = mine_of(cotangent)[0]

    def attend(stream, pair, side, relative):
        gain_one = side[:, 0].astype(F32)
        gain_two = side[:, 1].astype(F32)
        query_rot, kv_own, normed = qkv_forward(
            stream, gain_one[None], pair, cosines, sines, (half_query, 2 * half_kv)
        )
        kv_slots = slots_of(kv_own, "shard")
        attended, stats = attention_forward(query_rot, kv_slots, key_owners, seg_all, seg_own)
        kept = dict(
            stream=stream,
            normed=normed,
            query_rot=query_rot,
            kv_slots=kv_slots,
            stats=stats,
            gain_one=gain_one,
            gain_two=gain_two,
            router_full=side[:, 2 : 2 + all_experts],
            side=side,
            qkv=pair,
            relative=relative,
        )
        return attended, kept

    def gathered_rows_of(kept, attended, pair):
        relative = kept["relative"]
        attended = natural(
            (attended[:, : query_width // 2], attended[:, query_width // 2 :]), relative
        )
        middle = kept["stream"] + natural([dot_nn(attended, half) for half in pair], relative)
        scale_two = lax.rsqrt(jnp.mean(middle * middle, axis=-1, keepdims=True) + EPSILON)
        hidden_in = (middle * scale_two * kept["gain_two"]).astype(BF16)
        rows = jnp.concatenate(slots_of(hidden_in, "expert"), axis=0)
        kept.update(
            attended=attended, middle=middle, scale_two=scale_two, hidden_in=hidden_in, output=pair
        )
        return rows

    def mix(layer, kept, rows, experts):
        logits = jnp.where(chosen_all[layer], dot_nn(rows, kept["router_full"]), NEGATIVE)
        gates = jax.nn.softmax(logits, axis=-1)
        gates = jnp.where(chosen_all[layer], gates, 0.0)
        own_gates = lax.dynamic_slice_in_dim(gates, plane * local_experts, local_experts, axis=1)
        own_gates = jnp.pad(own_gates, ((0, 0), (0, LANES - local_experts)))
        partial, raws = moe_forward(rows, own_gates, experts)
        kept.update(
            rows=rows,
            gates=gates[:span_rows],
            own_gates=own_gates,
            raws=raws,
            experts=experts,
            partial=partial,
        )
        return partial

    def combine(kept, partial, *held):
        combined = after(partial[:span_rows], *held).astype(F32)
        for k in range(1, planes):
            back = crossed_back(partial[k * span_rows : (k + 1) * span_rows], "expert", k)
            combined = combined + back.astype(F32)
        return (kept["middle"] + combined).astype(BF16)

    def backward(layer, kept, grad_rows, earlier):
        grad_low = grad_rows[:span_rows]
        relative = kept["relative"]
        d_rows, d_raws, acts = moe_backward_rows(
            grad_rows, kept["own_gates"], kept["raws"], kept["experts"]
        )
        expert_grads = moe_backward_weights(kept["rows"], grad_rows, d_raws, acts, 2 * shards)
        backs = [after(d_rows[:span_rows], expert_grads)]
        for k in range(1, planes):
            backs.append(crossed_back(d_rows[k * span_rows : (k + 1) * span_rows], "expert", k))
        flip = jnp.reshape(core if relative else 0, (1,)).astype(jnp.int32)
        places = jnp.stack(
            [plane] + [partner("expert", k, True) for k in range(1, planes)]
        ).astype(jnp.int32)
        d_middle, d_branch, d_attended, logits_high, logits_low, d_gain_two = branch_backward(
            backs,
            places,
            local_experts,
            jnp.pad(kept["gates"], ((0, 0), (2, LANES - 2 - all_experts))),
            kept["side"],
            kept["middle"],
            kept["gain_two"][None],
            grad_low,
            kept["output"],
            flip,
        )
        sent_grads = after(expert_grads, d_branch)
        if earlier is not None:
            sent_grads, earlier = lax.optimization_barrier((sent_grads, earlier))
        scattered = lax.psum_scatter(sent_grads, ("section", "shard"), scatter_dimension=0)
        branch_halves = [d_branch[:, :output_half], d_branch[:, output_half:]]
        grad_output = None
        if layer == 0:
            grad_output = jnp.stack(
                [dot_tn(kept["attended"], part).astype(BF16) for part in branch_halves]
            )
            grad_output = (
                grad_output.reshape(2, planes, shards, part_rows, output_half)
                .swapaxes(1, 2)
                .reshape(2 * shards, planes, part_rows, output_half)
            )
        d_query_raw, *d_slots = attention_backward(
            kept["query_rot"],
            kept["kv_slots"],
            key_owners,
            seg_all,
            seg_own,
            d_attended,
            kept["stats"],
            cosines,
            sines,
        )
        result = None
        if layer == 1:
            partial = after(kept["partial"], d_branch)
            result = combine(kept, partial, d_slots[0])
            d_query_raw, result = lax.optimization_barrier((d_query_raw, result))
        else:
            earlier = sum_rest("expert", after(earlier, d_branch), d_slots[0])
            d_query_raw, earlier = lax.optimization_barrier((d_query_raw, earlier))
        d_kv_slots = [d_slots[0]] + [
            crossed_back(d_slots[k], "shard", k) for k in range(1, shards)
        ]
        stream = kept["stream"]
        d_normed, packed = qkv_backward(
            kept["normed"],
            d_query_raw,
            d_kv_slots,
            kept["qkv"],
            cosines,
            sines,
            (half_query, 2 * half_kv),
            stream,
            (kept["hidden_in"], logits_high, logits_low, d_gain_two),
            flip,
            [kept["attended"], *branch_halves] if layer == 1 else [],
            (shards, planes),
        )
        scale_one = lax.rsqrt(jnp.mean(stream * stream, axis=-1, keepdims=True) + EPSILON)
        d_stream, _ = norm_back(d_normed, stream, scale_one, kept["gain_one"])
        d_stream = (d_middle + d_stream).astype(BF16)
        return d_stream, scattered, packed, grad_output, earlier, result

    homes = {"shard": (shard, shards, 0), "expert": (plane, planes, 1)}

    def place_of(axis, k):
        return partner(axis, k, True) if k else homes[axis][0]

    def sum_over(axis, array, *held):
        size = (shards, *array.shape[1:])
        kept = lax.dynamic_slice(array, (core * shards, 0, 0, 0), size)
        received = swap(lax.dynamic_slice(array, ((1 - core) * shards, 0, 0, 0), size))
        _, count, dim = homes[axis]

        def chunk(k):
            place = place_of(axis, k)
            return lax.dynamic_index_in_dim(kept, place, dim, keepdims=False).astype(
                F32
            ) + lax.dynamic_index_in_dim(received, place, dim, keepdims=False).astype(F32)

        total = chunk(0)
        chunks = [chunk(k).astype(BF16) for k in range(1, count)]
        if held:
            *chunks, later = lax.optimization_barrier((*chunks, *held))
        for k in range(1, count):
            total = total + crossed_back(chunks[k - 1], axis, k).astype(F32)
        return (total, later) if held else total

    def sum_rest(axis, total, *held, meanwhile=None):
        result = lax.dynamic_index_in_dim(total, place_of(axis, 0), 0, keepdims=False)
        backs = []
        for k in range(1, homes[axis][1]):
            part = lax.dynamic_index_in_dim(total, place_of(axis, k), 0, keepdims=False)
            backs.append(crossed_back(part.astype(BF16), axis, k))
        if meanwhile is not None:
            held = (meanwhile(backs[0]),)
        result = after(result, *held) if held else result
        return sum((back.astype(F32) for back in backs), result.astype(F32)).astype(BF16)

    def exchanged(halves):
        kept = jnp.where(first, halves[0], halves[1])
        sent = jnp.where(first, halves[1], halves[0])
        return kept, swap(sent)

    start = mine_of(inputs)[0]
    side = jnp.where(
        first, first_qkv[0][:, half_qkv:qkv_columns], first_qkv[1][:, half_qkv:qkv_columns]
    )
    attended, kept_one = attend(
        start.astype(F32), [(half[None], 0) for half in first_qkv], side, True
    )
    first_output, _, _ = dense_weights(
        after(lined_output, *ring_end), held=(kept_one["query_rot"],)
    )
    rows = gathered_rows_of(kept_one, attended, first_output)
    result_one = combine(kept_one, mix(0, kept_one, rows, first_experts))

    last_rows = jnp.concatenate(slots_of(after(last, result_one), "expert"), axis=0)
    attended, kept_two = attend(
        result_one.astype(F32),
        [(second_pack, 0), (second_pack, 1)],
        second_pack[0, :, half_qkv:qkv_columns],
        False,
    )
    attended = after(attended, last_rows)
    rows = gathered_rows_of(
        kept_two, attended, [second_pack[half, :, qkv_columns:] for half in range(2)]
    )
    partial = mix(1, kept_two, rows, second_experts)
    grad_mid, scattered_two, packed_two, _, _, result_two = backward(
        1, kept_two, last_rows, None
    )
    mid_rows = jnp.concatenate(slots_of(grad_mid, "expert"), axis=0)
    packed_two, scattered_two, _ = lax.optimization_barrier((packed_two, scattered_two, mid_rows))
    pack_two = lax.psum_scatter(packed_two, ("section", "shard"), scatter_dimension=0)
    grad_start, scattered_one, packed_one, output_one, pack_two, _ = backward(
        0, kept_one, mid_rows, pack_two
    )
    qkv_one, output_one = sum_over("shard", packed_one, output_one)
    output_one = sum_over("expert", output_one)
    qkv_one, output_one = lax.optimization_barrier((qkv_one, output_one))
    expert_grads = []

    def unpack(returned):
        halves = exchanged([after(scattered_one, qkv_one, returned), scattered_two])
        expert_grads.extend(expert_outputs(*halves, core))
        return expert_grads[0]

    qkv_one = sum_rest("expert", qkv_one, meanwhile=unpack)
    grad_gate, grad_up, grad_down = expert_grads
    output_one = sum_rest("shard", output_one)

    def placed(by_layers):
        own = jnp.where(first, by_layers[0], by_layers[1])
        sent = jnp.where(first, by_layers[1], by_layers[0])
        return jnp.stack(by_layer(own, swap(sent)))

    layer_local = placed([result_one, result_two])
    input_local = placed([grad_start, grad_mid])
    dense_one = jnp.concatenate([qkv_one, output_one], axis=1)
    dense_low, dense_high = by_layer(*exchanged([dense_one, pack_two]))
    dense_low, dense_high = dense_low.astype(F32), dense_high.astype(F32)

    def both(start, stop):
        return jnp.concatenate([dense_low[:, start:stop], dense_high[:, start:stop]], axis=1)

    def every_other(start):
        return jnp.concatenate(
            [
                half[:, place : place + LANES]
                for half in (dense_low, dense_high)
                for place in range(start, half_qkv, 2 * LANES)
            ],
            axis=1,
        )

    side = dense_low[:, half_qkv:qkv_columns]

    out_shape = (1, 2, 1, span_rows, model)
    return (
        layer_local.reshape(out_shape),
        input_local.reshape(out_shape),
        side[:, 0][None],
        both(0, half_query)[None],
        every_other(half_query)[None],
        every_other(half_query + LANES)[None],
        both(qkv_columns, qkv_columns + output_half)[None],
        side[:, 1][None],
        side[:, 2 : 2 + all_experts][None],
        grad_gate[None],
        grad_up[None],
        grad_down[None],
    )


def solution(mesh):
    placed = (
        P(None, "expert", "shard", None),
        P(None, "expert", "shard", None),
        P(None, "expert", "shard"),
        P("section", None, "expert", "shard", None),
        P("section", ("expert", "shard")),
        P("section", ("expert", "shard"), None),
        P("section", ("expert", "shard"), None),
        P("section", ("expert", "shard"), None),
        P("section", ("expert", "shard"), None),
        P("section", ("expert", "shard")),
        P("section", ("expert", "shard"), None),
        P("section", "expert", "shard", None),
        P("section", "expert", "shard", None),
        P("section", "expert", None, "shard"),
    )
    return jax.shard_map(
        on_device,
        mesh=mesh,
        in_specs=placed,
        out_specs=(
            P("section", None, "expert", "shard", None),
            P("section", None, "expert", "shard", None),
            P("section", ("expert", "shard")),
            P("section", ("expert", "shard"), None),
            P("section", ("expert", "shard"), None),
            P("section", ("expert", "shard"), None),
            P("section", ("expert", "shard"), None),
            P("section", ("expert", "shard")),
            P("section", ("expert", "shard"), None),
            P("section", "expert", "shard", None),
            P("section", "expert", "shard", None),
            P("section", "expert", None, "shard"),
        ),
        check_vma=False,
    )
```
